32 devices in a mesh: fsdp: 16 (over z, y, core), rep: 2 (over x).
Axes of the slice: x: 2, y: 2, z: 4, core: 2. Of those that a mesh axis runs over, the one named last changes fastest.
Arguments:
- block_input: bfloat16 [64, 128, 768], P(('fsdp', 'rep')), may hold values from -6 to 6
- span_lengths: int32 [64], P(('fsdp', 'rep')), may hold values from 32 to 128, as said below
- mlm_positions: int32 [64, 32], P(('fsdp', 'rep')), may hold values from 0 to 127, as said below
- mlm_labels: int32 [64, 32], P(('fsdp', 'rep')), may hold values from 0 to 30521
- span_pairs: int32 [64], P(('fsdp', 'rep')), may hold values from 0 to 63, as said below
- layer_mats: float32 [7077888], P(('fsdp', 'rep'))
- vectors: float32 [9216], P(('fsdp', 'rep'))
- embedding: float32 [23440896], P(('fsdp', 'rep'))
- mom1_mats: float32 [7077888], P(('fsdp', 'rep')), may hold values from -6 to 6
- mom2_mats: float32 [7077888], P(('fsdp', 'rep')), may hold values from 0.01 to 10
- mom1_vecs: float32 [9216], P(('fsdp', 'rep')), may hold values from -6 to 6
- mom2_vecs: float32 [9216], P(('fsdp', 'rep')), may hold values from 0.01 to 10
- mom1_embed: float32 [23440896], P(('fsdp', 'rep')), may hold values from -6 to 6
- mom2_embed: float32 [23440896], P(('fsdp', 'rep')), may hold values from 0.01 to 10
Outputs:
- grad_input: float32 [64, 128, 768], P(('fsdp', 'rep'))
- grad_mats: float32 [7077888], P(('fsdp', 'rep'))
- grad_vecs: float32 [9216], P(('fsdp', 'rep'))
- grad_embed: float32 [23440896], P(('fsdp', 'rep'))
- step_mats: float32 [7077888], P(('fsdp', 'rep'))
- step_vecs: float32 [9216], P(('fsdp', 'rep'))
- step_embed: float32 [23440896], P(('fsdp', 'rep'))
The draws below stay inside these ranges and needn't reach their ends.
Inputs may be any that keep to these rules, and one draw needn't show every extreme that they name: `span_lengths`: A sequence's real tokens come first, padding after; some sequence has exactly 128 and some exactly 32 real tokens. `mlm_positions`: every slot's position lies below its sequence's span length; positions may repeat within a sequence; slot j of sequence s is used when j < span_lengths[s] // 4. span_pairs[span_pairs[s]] = s and span_pairs[s] != s for every s.
All inputs are finite; a program needn't handle non-finite values.
Results may differ from the reference program's by a relative error of at most 0.012.
The reference program's roundings to bfloat16 on the way count: a program that leaves them out, or rounds other values in their place, can miss the bound.
Values may be sent and summed in bfloat16 or wider, within the bound.
No kernel may reach another device: no remote copies, remote signals or barrier semaphores. Data moves between devices by JAX's collectives and lax.ppermute only.
A program may use at most 512 MiB of HBM per device.

```python
import math
import jax
import jax.numpy as jnp
from jax import lax

D = 768
FF = 3072
HEAD_DIM = 64
VOCAB = 30522
LENGTH = 128
ADAM_STEP = 10
MLM_SEQ = 32
SEQS = 64
MATS = 7077888
VECS = 9216


def draw_spans(key):
    lengths = jax.random.randint(key, (SEQS,), LENGTH // 4, LENGTH + 1)
    longest = jax.random.randint(jax.random.fold_in(key, 1), (), 0, SEQS)
    shortest = (longest + SEQS // 2) % SEQS
    lengths = lengths.at[longest].set(LENGTH).at[shortest].set(LENGTH // 4)
    return (lengths.astype(jnp.int32), longest)


def vector_signs(key):
    sign_key = jax.random.fold_in(key, 29)
    return (jax.random.randint(sign_key, (VECS,), 0, 2) * 2 - 1).astype(jnp.float32)


def draw_span_lengths(key, part):
    lengths, longest = draw_spans(key)
    return lengths


def draw_mlm_positions(key, part):
    lengths, longest = draw_spans(key)
    key = jax.random.fold_in(key, 5)
    places = jax.random.randint(key, (SEQS, MLM_SEQ), 0, lengths[:, None])
    places = places.at[longest, 0].set(LENGTH - 1).at[longest, 1].set(0)
    return places.astype(jnp.int32)


def draw_span_pairs(key, part):
    key = jax.random.fold_in(key, 7)
    order = jax.random.permutation(key, SEQS).astype(jnp.int32)
    place = jnp.argsort(order).astype(jnp.int32)
    return order[jnp.bitwise_xor(place, 1)].astype(jnp.int32)


def draw_layer_mats(key, part):
    key = jax.random.fold_in(key, 11)
    index = jnp.arange(MATS)
    first = 3 * D * D
    second = first + D * D
    third = second + D * FF
    column = index % (3 * D)
    scale = jnp.where(index < first, jnp.where(column < 2 * D, 1.3, 1.0) / math.sqrt(D), jnp.where(index < second, 5.0 / math.sqrt(D), jnp.where(index < third, 1.0 / math.sqrt(D), 1.0 / math.sqrt(FF))))
    base = jax.random.normal(key, (MATS,), jnp.float32)
    return (base * scale).astype(jnp.float32)


def draw_vectors(key, part):
    signs = vector_signs(key)
    key = jax.random.fold_in(key, 13)
    index = jnp.arange(VECS)
    is_gain = (index >= 3 * D) & (index < 4 * D) | (index >= 6 * D + FF) & (index < 7 * D + FF)
    magnitude = jnp.abs(jax.random.normal(key, (VECS,), jnp.float32))
    base = signs * magnitude
    return jnp.where(is_gain, 1.0 + 0.15 * base, 0.2 * base).astype(jnp.float32)


def draw_embedding(key, part):
    signs = vector_signs(key)
    shift_sign = signs[7 * D + FF:8 * D + FF]
    key = jax.random.fold_in(key, 19)
    often = (jax.random.randint(jax.random.fold_in(key, 1), (VOCAB,), 0, 128) == 0).astype(jnp.float32)
    noise = jnp.clip(jax.random.normal(key, (VOCAB, D), jnp.float32), -6.0, 6.0)
    table = (noise + 1.1 * often[:, None] * shift_sign[None, :]) / math.sqrt(D)
    return table.reshape(-1).astype(jnp.float32)


def set_ends(array, stream_key, smallest, top_value):
    spot = [jax.random.randint(jax.random.fold_in(stream_key, axis), (), 0, length) for axis, length in enumerate(array.shape)]
    widest = array.shape.index(max(array.shape))
    beside = spot[:widest] + [(spot[widest] + 1) % array.shape[widest]] + spot[widest + 1:]
    return array.at[tuple(spot)].set(smallest).at[tuple(beside)].set(top_value)


def block_scale(stream_key, extent, cuts, low, high):
    level = 1.0
    for position, parts in cuts:
        heights = jax.random.uniform(jax.random.fold_in(jax.random.fold_in(stream_key, 6), position), (parts,), jnp.float32, low / len(cuts), high / len(cuts))
        level = level * jnp.repeat(jnp.exp(heights), extent[position] // parts).reshape((-1,) + (1,) * (len(extent) - 1 - position))
    return level


def scatter_about(stream_key, shape, deviation, bound, cuts=(), kind=jnp.bfloat16):
    values = deviation * jax.random.normal(stream_key, shape, jnp.float32)
    if cuts:
        values = values * block_scale(stream_key, shape, cuts, -0.22, 0.18)
    return jnp.clip(values, -bound, bound).astype(kind)


def setup_inputs(seed: int = 0) -> dict:
    streams_of = jax.random.split(jax.random.key(seed), 15)
    return {
        "block_input": scatter_about(streams_of[0], (SEQS, LENGTH, D), 1.0, 6.0, ((0, 32),)),
        "span_lengths": draw_span_lengths(jax.random.fold_in(streams_of[14], 71), 0),
        "mlm_positions": draw_mlm_positions(jax.random.fold_in(streams_of[14], 71), 0),
        "mlm_labels": set_ends(jax.random.randint(streams_of[3], (SEQS, MLM_SEQ), 0, VOCAB), jax.random.fold_in(streams_of[3], 1), 0, VOCAB - 1).astype(jnp.int32),
        "span_pairs": draw_span_pairs(jax.random.fold_in(streams_of[14], 71), 0),
        "layer_mats": draw_layer_mats(jax.random.fold_in(streams_of[14], 71), 0),
        "vectors": draw_vectors(jax.random.fold_in(streams_of[14], 71), 0),
        "embedding": draw_embedding(jax.random.fold_in(streams_of[14], 71), 0),
        "mom1_mats": scatter_about(streams_of[8], (MATS,), 1.0, 6.0, ((0, 32),), jnp.float32),
        "mom2_mats": jnp.clip(jnp.exp(math.log(10.0) - 6.9077553 * jax.random.uniform(streams_of[9], (MATS,), jnp.float32) ** block_scale(streams_of[9], (MATS,), ((0, 32),), -0.2, 0.2)), 0.01, 10.0),
        "mom1_vecs": scatter_about(streams_of[10], (VECS,), 1.0, 6.0, ((0, 32),), jnp.float32),
        "mom2_vecs": jnp.clip(jnp.exp(math.log(10.0) - 6.9077553 * jax.random.uniform(streams_of[11], (VECS,), jnp.float32) ** block_scale(streams_of[11], (VECS,), ((0, 32),), -0.2, 0.2)), 0.01, 10.0),
        "mom1_embed": scatter_about(streams_of[12], (VOCAB * D,), 1.0, 6.0, ((0, 32),), jnp.float32),
        "mom2_embed": jnp.clip(jnp.exp(math.log(10.0) - 6.9077553 * jax.random.uniform(streams_of[13], (VOCAB * D,), jnp.float32) ** block_scale(streams_of[13], (VOCAB * D,), ((0, 32),), -0.2, 0.2)), 0.01, 10.0),
    }


@jax.custom_vjp
def low(v):
    return lax.optimization_barrier(v.astype(jnp.bfloat16)).astype(jnp.float32)

@jax.custom_vjp
def low_back(v):
    return v

def low_keep(v):
    return (low(v), None)

def low_pass(kept, grad):
    return (grad,)

def back_keep(v):
    return (v, None)

def back_low(kept, grad):
    return (low(grad),)
low.defvjp(low_keep, low_pass)
low_back.defvjp(back_keep, back_low)
highest_prec = lax.Precision.HIGHEST
norm_eps = 1e-12
beta_one = 0.9
beta_two = 0.999
adam_eps = 1e-06
decay_rate = 0.01
seqs_per_group = 32

def round_both(value):
    return low(low_back(value))

def split_mats(flat):
    first = 3 * D * D
    second = first + D * D
    third = second + D * FF
    return (flat[:first].reshape(D, 3 * D), flat[first:second].reshape(D, D), flat[second:third].reshape(D, FF), flat[third:].reshape(FF, D))

def split_vecs(flat):
    widths_list = [D, D, D, D, D, FF, D, D, D]
    pieces = []
    offset = 0
    for piece_width in widths_list:
        pieces.append(flat[offset:offset + piece_width])
        offset = offset + piece_width
    return pieces

def norm_rows(resid, gain_row, shift_row):
    center = resid - lax.optimization_barrier(jnp.mean(resid, axis=-1, keepdims=True))
    spread = lax.optimization_barrier(jnp.mean(center * center, axis=-1, keepdims=True))
    return center * lax.rsqrt(spread + norm_eps) * gain_row + shift_row

def layer_group(inputs, weights):
    group_input, group_lengths, group_places, group_labels = inputs
    w_qkv, w_out, w_up, w_down, bias_q, bias_v, bias_out, gain_one, shift_one, bias_up, bias_down, gain_two, shift_two, table = weights
    seq_count = group_input.shape[0]
    heads_count = D // HEAD_DIM
    valid = (jnp.arange(LENGTH)[None, :] < group_lengths[:, None]).astype(jnp.float32)
    tok_rows = (group_input * valid[:, :, None]).reshape(seq_count * LENGTH, D)
    qkv_bias = jnp.concatenate([bias_q, jnp.zeros((D,), jnp.float32), bias_v])
    projected = round_both(jnp.dot(tok_rows, w_qkv, precision=highest_prec) + qkv_bias)
    shaped = projected.reshape(seq_count, LENGTH, 3, heads_count, HEAD_DIM)
    queries = shaped[:, :, 0]
    key_rows = shaped[:, :, 1]
    value_rows = shaped[:, :, 2]
    scores = low_back(jnp.einsum('sqhd,skhd->shqk', queries, key_rows, precision=highest_prec) * HEAD_DIM ** (-0.5))
    scores = jnp.where(valid[:, None, None, :] > 0, scores, -1e+30)
    attn_probs = low(jax.nn.softmax(scores, axis=-1))
    attended = round_both(jnp.einsum('shqk,skhd->sqhd', attn_probs, value_rows, precision=highest_prec).reshape(seq_count * LENGTH, D))
    branch = low_back(jnp.dot(attended, w_out, precision=highest_prec) + bias_out)
    hidden_one = norm_rows(tok_rows + branch, gain_one, shift_one)
    pre_act = low_back(jnp.dot(low(hidden_one), w_up, precision=highest_prec) + bias_up)
    act_low = low(jax.nn.gelu(pre_act, approximate=False))
    ffn_out = low_back(jnp.dot(act_low, w_down, precision=highest_prec) + bias_down)
    output = norm_rows(hidden_one + ffn_out, gain_two, shift_two).reshape(seq_count, LENGTH, D) * valid[:, :, None]
    picked = low(jnp.take_along_axis(output, group_places[:, :, None], axis=1).reshape(-1, D))
    logits = low_back(jnp.dot(picked, table.T, precision=highest_prec))
    label_logit = jnp.take_along_axis(logits, group_labels.reshape(-1, 1), axis=1)[:, 0]
    used = (jnp.arange(MLM_SEQ)[None, :] < (group_lengths // 4)[:, None]).astype(jnp.float32).reshape(-1)
    mlm_part = jnp.sum((jax.nn.logsumexp(logits, axis=-1) - label_logit) * used)
    return (mlm_part, output[:, 0, :])

def total_loss(block_input, layer_mats, vectors, embedding, span_lengths, mlm_positions, mlm_labels, span_pairs):
    mats_four = split_mats(low(layer_mats))
    vec_nine = split_vecs(low(vectors))
    table = low(embedding).reshape(VOCAB, D)
    weights = tuple(mats_four) + tuple(vec_nine) + (table,)
    groups = SEQS // seqs_per_group
    checked = jax.checkpoint(layer_group)

    def group_step(carry, inputs):
        mlm_part, cls_rows = checked(inputs, weights)
        return (carry + mlm_part, cls_rows)
    stacked = (block_input.reshape(groups, seqs_per_group, LENGTH, D), span_lengths.reshape(groups, seqs_per_group), mlm_positions.reshape(groups, seqs_per_group, MLM_SEQ), mlm_labels.reshape(groups, seqs_per_group, MLM_SEQ))
    mlm_loss, cls_all = lax.scan(group_step, jnp.zeros((), jnp.float32), stacked)
    cls_all = low(cls_all.reshape(SEQS, D))
    sims = low_back(jnp.dot(cls_all, cls_all.T, precision=highest_prec) * (2.0 / math.sqrt(D)))
    diagonal = jnp.arange(SEQS)[:, None] == jnp.arange(SEQS)[None, :]
    sims = jnp.where(diagonal, -1e+30, sims)
    partner = jnp.take_along_axis(sims, span_pairs[:, None], axis=1)[:, 0]
    return mlm_loss + jnp.sum(jax.nn.logsumexp(sims, axis=-1) - partner)

def adam_step(weight, grad, first, second, step_float, decay):
    first_new = beta_one * first + (1.0 - beta_one) * grad
    second_new = beta_two * second + (1.0 - beta_two) * grad * grad
    first_hat = first_new / (1.0 - beta_one ** step_float)
    second_hat = second_new / (1.0 - beta_two ** step_float)
    return first_hat / (jnp.sqrt(second_hat) + adam_eps) + decay * weight

def reference(block_input, span_lengths, mlm_positions, mlm_labels, span_pairs, layer_mats, vectors, embedding, mom1_mats, mom2_mats, mom1_vecs, mom2_vecs, mom1_embed, mom2_embed):
    input_float = block_input.astype(jnp.float32)

    def loss_of(inp, mats, vecs, embed):
        return total_loss(inp, mats, vecs, embed, span_lengths, mlm_positions, mlm_labels, span_pairs)
    loss_value, pull_back = jax.vjp(loss_of, input_float, layer_mats, vectors, embedding)
    grad_input, grad_mats, grad_vecs, grad_embed = pull_back(jnp.ones((), jnp.float32))
    step_float = float(ADAM_STEP)
    step_mats = adam_step(layer_mats, grad_mats, mom1_mats, mom2_mats, step_float, decay_rate)
    step_vecs = adam_step(vectors, grad_vecs, mom1_vecs, mom2_vecs, step_float, 0.0)
    step_embed = adam_step(embedding, grad_embed, mom1_embed, mom2_embed, step_float, decay_rate)
    return (grad_input, grad_mats, grad_vecs, grad_embed, step_mats, step_vecs, step_embed)
```

```python
import functools
import math

import jax
import jax.numpy as jnp
from jax import lax
from jax.sharding import Mesh, PartitionSpec as P

D = 768
FF = 3072
HEAD_DIM = 64
VOCAB = 30522
ADAM_STEP = 10


norm_eps = 1e-12
beta_one = 0.9
beta_two = 0.999
adam_eps = 1e-06
decay_rate = 0.01


def split_mats(flat):
    first = 3 * D * D
    second = first + D * D
    third = second + D * FF
    return (
        flat[:first].reshape(D, 3 * D),
        flat[first:second].reshape(D, D),
        flat[second:third].reshape(D, FF),
        flat[third:].reshape(FF, D),
    )


def split_vecs(flat):
    widths_list = [D, D, D, D, D, FF, D, D, D]
    pieces = []
    offset = 0
    for piece_width in widths_list:
        pieces.append(flat[offset : offset + piece_width].astype(jnp.float32))
        offset = offset + piece_width
    return pieces


def center_scale(resid):
    center = resid - jnp.mean(resid, axis=-1, keepdims=True)
    inverse = lax.rsqrt(jnp.mean(center * center, axis=-1, keepdims=True) + norm_eps)
    return (center * inverse, inverse)


def norm_back(d_normed, normed, inverse):
    return inverse * (
        d_normed
        - jnp.mean(d_normed, axis=-1, keepdims=True)
        - normed * jnp.mean(d_normed * normed, axis=-1, keepdims=True)
    )


def gelu_slope(value):
    return (
        0.5 * (1.0 + lax.erf(value * 0.7071067811865476))
        + value * jnp.exp(-0.5 * value * value) * 0.3989422804014327
    )


def contract_rows(left, right):
    return lax.dot_general(
        left, right, (((0,), (0,)), ((), ())), preferred_element_type=jnp.float32
    )


def contract_cols(left, right):
    return lax.dot_general(
        left, right, (((1,), (1,)), ((), ())), preferred_element_type=jnp.float32
    )


def adam_step(weight, grad, first, second, step_float, decay):
    first_new = beta_one * first + (1.0 - beta_one) * grad
    second_new = beta_two * second + (1.0 - beta_two) * grad * grad
    first_hat = first_new / (1.0 - beta_one**step_float)
    second_hat = second_new / (1.0 - beta_two**step_float)
    return first_hat / (jnp.sqrt(second_hat) + adam_eps) + decay * weight


def flip(value, name):
    return lax.ppermute(value, name, [(0, 1), (1, 0)])


def gather_bits(shard, order, names):
    grown = shard
    for name in order:
        other = flip(grown, name)
        first = lax.axis_index(name) == 0
        grown = jnp.stack([jnp.where(first, grown, other), jnp.where(first, other, grown)])
    axes = list(reversed(order))
    rank = len(axes)
    turn = [axes.index(name) for name in names] + list(range(rank, grown.ndim))
    return grown.transpose(turn).reshape((2**rank,) + shard.shape)


def reduce_bits(blocks, order, names):
    left = list(names)
    held = blocks.reshape((2,) * len(left) + blocks.shape[1:])
    for name in order:
        axis = left.index(name)
        here = lax.axis_index(name)
        send = lax.dynamic_index_in_dim(held, 1 - here, axis, keepdims=False)
        keep = lax.dynamic_index_in_dim(held, here, axis, keepdims=False)
        other = flip(send, name)
        held = (keep.astype(jnp.float32) + other.astype(jnp.float32)).astype(blocks.dtype)
        left.remove(name)
    return held


def bit_orders(names, core):
    outer = [name for name in names if name != core]
    count = len(outer)
    if count == 4:
        picks = ((0, 1, 3, 2), (3, 2, 0, 1), (0, 1, 2, 3))
        return [[outer[k] for k in pick] + [core] for pick in picks]
    step = max(1, count // 3)
    return [outer[step * k :] + outer[: step * k] + [core] for k in range(3)]


def on_device(
    names,
    core,
    block_input,
    span_lengths,
    mlm_positions,
    mlm_labels,
    span_pairs,
    layer_mats,
    vectors,
    embedding,
    mom1_mats,
    mom2_mats,
    mom1_vecs,
    mom2_vecs,
    mom1_embed,
    mom2_embed,
):
    seq_here, length, width = block_input.shape
    rows_here = seq_here * length
    heads_count = width // HEAD_DIM
    head_scale = HEAD_DIM ** (-0.5)
    devices = 2 ** len(names)
    me = lax.axis_index(names)
    orders = bit_orders(names, core)
    slots = mlm_positions.shape[1]
    picks_here = seq_here * slots
    low = jnp.bfloat16

    mat_rows = layer_mats.shape[0] // width
    third = mat_rows // 3
    vec_here = vectors.shape[0]
    mats_low = layer_mats.astype(low).reshape(3, third, width)

    def pad_row(row):
        return jnp.pad(row, (0, width - row.shape[0])).astype(low)[None]

    labels_flat = mlm_labels.reshape(-1)
    small = jnp.concatenate(
        [
            pad_row(vectors.astype(low)),
            pad_row(labels_flat // 256),
            pad_row(labels_flat % 256),
            pad_row(jnp.concatenate([span_pairs // 256, span_pairs % 256, span_lengths // 4])),
            jnp.zeros((4, width), low),
        ]
    )
    gathered = [
        gather_bits(mats_low[0], orders[0], names),
        gather_bits(mats_low[1], orders[1], names),
        gather_bits(jnp.concatenate([mats_low[2], small]), orders[2], names),
    ]
    small_all = gathered[2][:, third:, :]
    mats_all = jnp.stack([gathered[0], gathered[1], gathered[2][:, :third, :]], axis=1).reshape(-1)
    vecs_all = small_all[:, 0, :vec_here].reshape(-1)
    labels_all = (
        small_all[:, 1, :picks_here].astype(jnp.int32) * 256
        + small_all[:, 2, :picks_here].astype(jnp.int32)
    ).reshape(-1)
    ints_all = small_all[:, 3, : 3 * seq_here].astype(jnp.int32)
    pairs_all = (ints_all[:, :seq_here] * 256 + ints_all[:, seq_here : 2 * seq_here]).reshape(-1)
    quarter_all = ints_all[:, 2 * seq_here :].reshape(-1)

    embed_here = embedding.shape[0]
    shifted_rows = -(-embed_here // width)
    shift = (me * (embed_here % width)) % width
    first_row = me * (embed_here // width) + (me * (embed_here % width)) // width
    embed_low = embedding.astype(low)
    ring = range(devices)
    from_left = lax.ppermute(embed_low[-width:], names, [(k, (k + 1) % devices) for k in ring])
    from_right = lax.ppermute(embed_low[:width], names, [((k + 1) % devices, k) for k in ring])
    shifted = jnp.concatenate(
        [
            from_left,
            embed_low,
            from_right,
            jnp.zeros((shifted_rows * width - embed_here,), low),
        ]
    ).reshape(shifted_rows + 2, width)
    lanes = jnp.arange(width)
    same_row = (lanes < width - shift)[None, :]
    rolled = jnp.where(same_row, shifted[1:], shifted[:-1])
    turn = ((lanes[:, None] + shift) % width == lanes[None, :]).astype(low)
    table = jnp.dot(rolled, turn, preferred_element_type=jnp.float32).astype(low)
    row_start = jnp.arange(shifted_rows + 1) * width - shift
    owned = (row_start >= 0) & (row_start < embed_here)
    touched = (row_start + width > 0) & (row_start < embed_here)
    table_owned = jnp.where(owned[:, None], table, 0)

    w_qkv, w_out, w_up, w_down = split_mats(mats_all)
    bias_q, bias_v, bias_out, gain_one, shift_one, bias_up, bias_down, gain_two, shift_two = (
        split_vecs(vecs_all)
    )
    valid = jnp.arange(length)[None, :] < span_lengths[:, None]
    valid_col = valid.reshape(rows_here, 1).astype(jnp.float32)
    tok_rows = (block_input * valid[:, :, None].astype(low)).reshape(rows_here, width)
    qkv_bias = jnp.concatenate([bias_q, jnp.zeros((width,), jnp.float32), bias_v])
    projected = (jnp.dot(tok_rows, w_qkv, preferred_element_type=jnp.float32) + qkv_bias).astype(
        low
    )
    shaped = projected.reshape(seq_here, length, 3, heads_count, HEAD_DIM)
    queries = shaped[:, :, 0]
    key_rows = shaped[:, :, 1]
    value_rows = shaped[:, :, 2]
    key_valid = valid[:, None, None, :]

    def make_scores():
        raw = (
            jnp.einsum("sqhd,skhd->shqk", queries, key_rows, preferred_element_type=jnp.float32)
            * head_scale
        )
        return jnp.where(key_valid, raw, -1e30)

    scores = make_scores()
    row_max = jnp.max(scores, axis=-1, keepdims=True)
    expo_vals = jnp.exp(scores - row_max)
    row_sum = jnp.sum(expo_vals, axis=-1, keepdims=True)
    row_lse = row_max + jnp.log(row_sum)
    attn_probs = (expo_vals / row_sum).astype(low)
    attended = (
        jnp.einsum("shqk,skhd->sqhd", attn_probs, value_rows, preferred_element_type=jnp.float32)
        .reshape(rows_here, width)
        .astype(low)
    )
    branch = jnp.dot(attended, w_out, preferred_element_type=jnp.float32) + bias_out
    normed_one, inverse_one = center_scale(tok_rows.astype(jnp.float32) + branch)
    hidden_one = normed_one * gain_one + shift_one
    hidden_low = hidden_one.astype(low)
    pre_act = jnp.dot(hidden_low, w_up, preferred_element_type=jnp.float32) + bias_up
    act_low = jax.nn.gelu(pre_act, approximate=False).astype(low)
    ffn_out = jnp.dot(act_low, w_down, preferred_element_type=jnp.float32) + bias_down
    normed_two, inverse_two = center_scale(hidden_one + ffn_out)
    output = (normed_two * gain_two + shift_two) * valid_col
    output_seq = output.reshape(seq_here, length, width)

    picked_here = jnp.take_along_axis(output_seq, mlm_positions[:, :, None], axis=1).reshape(
        -1, width
    )
    cls_pad = -seq_here % 8
    heads_rows = jnp.concatenate(
        [picked_here, output_seq[:, 0, :], jnp.zeros((cls_pad, width), jnp.float32)]
    ).astype(low)
    cut = width // 3
    heads_all = jnp.concatenate(
        [
            gather_bits(heads_rows[:, k * cut : (k + 1) * cut], orders[k], names)
            for k in range(3)
        ],
        axis=2,
    )
    picked = heads_all[:, :picks_here, :].reshape(-1, width)
    cls_all = heads_all[:, picks_here : picks_here + seq_here, :].reshape(-1, width)

    logits = contract_cols(picked, table)
    masked = jnp.where(owned[None, :], logits, -jnp.inf)
    part_max = jnp.max(masked, axis=-1)
    part_sum = jnp.sum(jnp.exp(masked - part_max[:, None]), axis=-1)
    stats = jnp.stack([part_max, part_sum]).reshape(1, -1, 128)
    stats_all = lax.all_to_all(
        jnp.broadcast_to(stats, (devices,) + stats.shape[1:]), names, 0, 0, tiled=True
    ).reshape(devices, 2, -1)
    full_max = jnp.max(stats_all[:, 0], axis=0)
    full_sum = jnp.sum(stats_all[:, 1] * jnp.exp(stats_all[:, 0] - full_max), axis=0)
    row_of = labels_all - first_row
    hot = row_of[:, None] == jnp.arange(shifted_rows + 1)[None, :]
    used = (jnp.arange(slots)[None, :] < quarter_all[:, None]).reshape(-1, 1)
    probs = jnp.exp(logits - full_max[:, None]) / full_sum[:, None]
    d_logits = jnp.where(
        used & touched[None, :], probs - hot.astype(jnp.float32), 0.0
    ).astype(low)
    d_picked_part = jnp.dot(d_logits, table_owned, preferred_element_type=jnp.float32).astype(low)
    blocks = d_picked_part.reshape(devices, picks_here, width)
    d_picked = jnp.concatenate(
        [
            reduce_bits(blocks[:, :, k * cut : (k + 1) * cut], orders[k][::-1], names)
            for k in range(3)
        ],
        axis=1,
    ).astype(jnp.float32)

    select = (mlm_positions[:, :, None] == jnp.arange(length)[None, None, :]).astype(jnp.float32)
    d_output_seq = jnp.einsum(
        "gor,gon->grn",
        select,
        d_picked.reshape(seq_here, slots, width),
        precision=lax.Precision.HIGHEST,
    )
    span_scale = 2.0 / math.sqrt(width)
    columns = jnp.arange(cls_all.shape[0])
    sims = contract_cols(cls_all, cls_all) * span_scale
    sims = jnp.where(columns[None, :] == columns[:, None], -1e30, sims)
    partner_hot = (columns[None, :] == pairs_all[:, None]).astype(jnp.float32)
    d_sims = (jax.nn.softmax(sims, axis=-1) - partner_hot).astype(low)
    mine = me * seq_here
    d_sims_rows = lax.dynamic_slice_in_dim(d_sims, mine, seq_here, 0)
    d_sims_cols = lax.dynamic_slice_in_dim(d_sims, mine, seq_here, 1)
    d_cls = (
        jnp.dot(d_sims_rows, cls_all, preferred_element_type=jnp.float32)
        + contract_rows(d_sims_cols, cls_all)
    ) * span_scale
    d_output_seq = d_output_seq.at[:, 0, :].add(d_cls)
    d_output = d_output_seq.reshape(rows_here, width) * valid_col
    d_gain_two = jnp.sum(d_output * normed_two, axis=0)
    d_shift_two = jnp.sum(d_output, axis=0)
    d_resid_two = norm_back(d_output * gain_two, normed_two, inverse_two)
    d_ffn = d_resid_two.astype(low)
    d_bias_down = jnp.sum(d_ffn.astype(jnp.float32), axis=0)
    d_w_down = contract_rows(act_low, d_ffn)
    d_act = contract_cols(d_ffn, w_down)
    d_pre = (d_act * gelu_slope(pre_act)).astype(low)
    d_bias_up = jnp.sum(d_pre.astype(jnp.float32), axis=0)
    d_w_up = contract_rows(hidden_low, d_pre)
    d_hidden = contract_cols(d_pre, w_up) + d_resid_two
    d_gain_one = jnp.sum(d_hidden * normed_one, axis=0)
    d_shift_one = jnp.sum(d_hidden, axis=0)
    d_resid_one = norm_back(d_hidden * gain_one, normed_one, inverse_one)
    d_branch = d_resid_one.astype(low)
    d_bias_out = jnp.sum(d_branch.astype(jnp.float32), axis=0)
    d_w_out = contract_rows(attended, d_branch)
    d_attended = (
        contract_cols(d_branch, w_out).astype(low).reshape(seq_here, length, heads_count, HEAD_DIM)
    )
    probs_again = jnp.exp(make_scores() - row_lse)
    probs_low = probs_again.astype(low)
    d_probs = jnp.einsum(
        "sqhd,skhd->shqk", d_attended, value_rows, preferred_element_type=jnp.float32
    )
    d_values = jnp.einsum(
        "shqk,sqhd->skhd", probs_low, d_attended, preferred_element_type=jnp.float32
    )
    row_delta = jnp.sum(d_probs * probs_again, axis=-1, keepdims=True)
    d_scores = (probs_again * (d_probs - row_delta)).astype(low)
    d_queries = (
        jnp.einsum("shqk,skhd->sqhd", d_scores, key_rows, preferred_element_type=jnp.float32)
        * head_scale
    )
    d_keys = (
        jnp.einsum("shqk,sqhd->skhd", d_scores, queries, preferred_element_type=jnp.float32)
        * head_scale
    )
    d_qkv = jnp.concatenate(
        [
            d_queries.reshape(rows_here, width),
            d_keys.reshape(rows_here, width),
            d_values.reshape(rows_here, width),
        ],
        axis=1,
    ).astype(low)
    d_qkv_float = d_qkv.astype(jnp.float32)
    d_bias_q = jnp.sum(d_qkv_float[:, :width], axis=0)
    d_bias_v = jnp.sum(d_qkv_float[:, 2 * width :], axis=0)
    d_w_qkv = contract_rows(tok_rows, d_qkv)
    grad_input = ((contract_cols(d_qkv, w_qkv) + d_resid_one) * valid_col).reshape(
        seq_here, length, width
    )

    d_mats = jnp.concatenate(
        [
            piece.astype(low).reshape(-1, width)
            for piece in (d_w_qkv, d_w_out, d_w_up, d_w_down)
        ]
    ).reshape(devices, 3, third, width)
    d_vecs = jnp.concatenate(
        [
            d_bias_q,
            d_bias_v,
            d_bias_out,
            d_gain_one,
            d_shift_one,
            d_bias_up,
            d_bias_down,
            d_gain_two,
            d_shift_two,
        ]
    ).reshape(devices, 1, vec_here)
    d_small = jnp.pad(d_vecs, ((0, 0), (0, 7), (0, width - vec_here))).astype(low)
    summed = [
        reduce_bits(d_mats[:, 0], orders[0][::-1], names),
        reduce_bits(d_mats[:, 1], orders[1][::-1], names),
        reduce_bits(jnp.concatenate([d_mats[:, 2], d_small], axis=1), orders[2][::-1], names),
    ]
    grad_vecs = summed[2][third, :vec_here].astype(jnp.float32)
    grad_mats = (
        jnp.concatenate([summed[0], summed[1], summed[2][:third]]).astype(jnp.float32).reshape(-1)
    )

    picked_turned = jnp.dot(picked, turn.T, preferred_element_type=jnp.float32).astype(low)
    d_rolled = contract_rows(d_logits, picked_turned)
    grad_embed = jnp.where(same_row, d_rolled[:-1], d_rolled[1:]).reshape(-1)[:embed_here]

    step_float = float(ADAM_STEP)
    step_mats = adam_step(layer_mats, grad_mats, mom1_mats, mom2_mats, step_float, decay_rate)
    step_vecs = adam_step(vectors, grad_vecs, mom1_vecs, mom2_vecs, step_float, 0.0)
    step_embed = adam_step(embedding, grad_embed, mom1_embed, mom2_embed, step_float, decay_rate)
    return (grad_input, grad_mats, grad_vecs, grad_embed, step_mats, step_vecs, step_embed)


def solution(mesh):
    fsdp_bits = mesh.shape["fsdp"].bit_length() - 1
    rep_bits = mesh.shape["rep"].bit_length() - 1
    names = tuple(f"f{k}" for k in reversed(range(fsdp_bits)))
    core = names[-1]
    names = names + tuple(f"r{k}" for k in reversed(range(rep_bits)))
    bits = Mesh(mesh.devices.reshape((2,) * len(names)), names)
    seqs = P(names, None, None)
    pairs = P(names, None)
    flat = P(names)
    return jax.shard_map(
        functools.partial(on_device, names, core),
        mesh=bits,
        in_specs=(seqs, flat, pairs, pairs) + (flat,) * 10,
        out_specs=(seqs,) + (flat,) * 6,
        check_vma=False,
    )
```

```python
import functools
import math

import jax
import jax.numpy as jnp
from jax import lax
from jax.experimental import pallas as pl
from jax.experimental.pallas import tpu as pltpu
from jax.sharding import Mesh, PartitionSpec as P

D = 768
FF = 3072
HEAD_DIM = 64
VOCAB = 30522
ADAM_STEP = 10


norm_eps = 1e-12
beta_one = 0.9
beta_two = 0.999
adam_eps = 1e-06
decay_rate = 0.01


def split_mats(flat):
    first = 3 * D * D
    second = first + D * D
    third = second + D * FF
    return (
        flat[:first].reshape(D, 3 * D),
        flat[first:second].reshape(D, D),
        flat[second:third].reshape(D, FF),
        flat[third:].reshape(FF, D),
    )


def split_vecs(flat):
    widths_list = [D, D, D, D, D, FF, D, D, D]
    pieces = []
    offset = 0
    for piece_width in widths_list:
        pieces.append(flat[offset : offset + piece_width].astype(jnp.float32))
        offset = offset + piece_width
    return pieces


def center_scale(resid):
    center = resid - jnp.mean(resid, axis=-1, keepdims=True)
    inverse = lax.rsqrt(jnp.mean(center * center, axis=-1, keepdims=True) + norm_eps)
    return (center * inverse, inverse)


def norm_back(d_normed, normed, inverse):
    return inverse * (
        d_normed
        - jnp.mean(d_normed, axis=-1, keepdims=True)
        - normed * jnp.mean(d_normed * normed, axis=-1, keepdims=True)
    )


def gelu_slope(value):
    return (
        0.5 * (1.0 + lax.erf(value * 0.7071067811865476))
        + value * jnp.exp(-0.5 * value * value) * 0.3989422804014327
    )


def contract_rows(left, right):
    return lax.dot_general(
        left, right, (((0,), (0,)), ((), ())), preferred_element_type=jnp.float32
    )


def contract_cols(left, right):
    return lax.dot_general(
        left, right, (((1,), (1,)), ((), ())), preferred_element_type=jnp.float32
    )


def adam_step(weight, grad, first, second, step_float, decay):
    first_new = beta_one * first + (1.0 - beta_one) * grad
    second_new = beta_two * second + (1.0 - beta_two) * grad * grad
    first_hat = first_new / (1.0 - beta_one**step_float)
    second_hat = second_new / (1.0 - beta_two**step_float)
    return first_hat / (jnp.sqrt(second_hat) + adam_eps) + decay * weight


def flip(value, name):
    return lax.ppermute(value, name, [(0, 1), (1, 0)])


def gather_bits(shard, order, names):
    grown = shard
    for name in order:
        other = flip(grown, name)
        first = lax.axis_index(name) == 0
        grown = jnp.stack([jnp.where(first, grown, other), jnp.where(first, other, grown)])
    axes = list(reversed(order))
    rank = len(axes)
    turn = [axes.index(name) for name in names] + list(range(rank, grown.ndim))
    return grown.transpose(turn).reshape((2**rank,) + shard.shape)


def reduce_bits(blocks, order, names):
    left = list(names)
    held = blocks.reshape((2,) * len(left) + blocks.shape[1:])
    for name in order:
        axis = left.index(name)
        here = lax.axis_index(name)
        send = lax.dynamic_index_in_dim(held, 1 - here, axis, keepdims=False)
        keep = lax.dynamic_index_in_dim(held, here, axis, keepdims=False)
        other = flip(send, name)
        held = (keep.astype(jnp.float32) + other.astype(jnp.float32)).astype(blocks.dtype)
        left.remove(name)
    return held


def bit_orders(names, core):
    outer = [name for name in names if name != core]
    count = len(outer)
    if count == 4:
        picks = ((0, 3, 2, 1), (0, 2, 3, 1), (0, 2, 1, 3))
        return [[outer[k] for k in pick] + [core] for pick in picks]
    step = max(1, count // 3)
    return [outer[step * k :] + outer[: step * k] + [core] for k in range(3)]


def device_mask(name, names):
    return 1 << (len(names) - 1 - names.index(name))


def gather_relative(shard, order, names):
    grown, masks = shard[None], [0]
    for name in order[:-2]:
        grown = jnp.concatenate([grown, flip(grown, name)])
        masks = masks + [mask | device_mask(name, names) for mask in masks]
    pieces = [(grown, masks)]
    for name in order[-2:]:
        bit = device_mask(name, names)
        pieces = pieces + [(flip(piece, name), [mask | bit for mask in own]) for piece, own in pieces]
    return pieces


def reduce_relative(keep, send, order):
    for name in order:
        other = flip(send, name)
        half = keep.shape[0] // 2
        total = [
            keep[part].astype(jnp.float32) + other[part].astype(jnp.float32)
            for part in ((slice(half, None), slice(0, half)) if half else (slice(0, None),))
        ]
        if half:
            send, keep = (value.astype(keep.dtype) for value in total)
    return total[0][0]


def dot_nn(left, right):
    return lax.dot_general(
        left, right, (((1,), (0,)), ((), ())), preferred_element_type=jnp.float32
    )


def interleave(count, rows):
    span = rows // count
    to = lax.broadcasted_iota(jnp.int32, (rows, rows), 0)
    source = lax.broadcasted_iota(jnp.int32, (rows, rows), 1)
    return (source == count * lax.rem(to, span) + lax.div(to, span)).astype(jnp.bfloat16)


def valid_rows(len_ref, rows, seq_here):
    length = rows // seq_here
    row = lax.broadcasted_iota(jnp.int32, (rows, 1), 0)
    valid = jnp.zeros((rows, 1), jnp.float32)
    for seq in range(seq_here):
        inside = (row >= seq * length) & (row < seq * length + len_ref[seq])
        valid = jnp.where(inside, 1.0, valid)
    return valid


def stack_pair(value):
    lane = lax.broadcasted_iota(jnp.int32, value.shape, 1)
    zero = jnp.zeros_like(value)
    left = lane < HEAD_DIM
    return jnp.concatenate([jnp.where(left, value, zero), jnp.where(left, zero, value)], axis=0)


def join_pair(stacked):
    half = stacked.shape[0] // 2
    lane = lax.broadcasted_iota(jnp.int32, (half, stacked.shape[1]), 1)
    return jnp.where(lane < HEAD_DIM, stacked[:half], stacked[half:])


def pair_scores(stacked, keys, limit):
    raw = contract_cols(stacked, keys) * HEAD_DIM ** (-0.5)
    column = lax.broadcasted_iota(jnp.int32, raw.shape, 1)
    return jnp.where(column < limit, raw, -1e30)


def center_rows(resid):
    center = resid - jnp.mean(resid, axis=-1, keepdims=True)
    inverse = lax.rsqrt(jnp.mean(center * center, axis=-1, keepdims=True) + norm_eps)
    return center * inverse, inverse


def gelu_phi(value):
    return 0.5 * (1.0 + lax.erf(value * 0.7071067811865476))


def forward_kernel(plan, seq_here, *refs):
    me_ref, len_ref, place_ref, x_ref, vec_ref = refs[:5]
    blocks = refs[5 : 5 + len(plan)]
    heads_ref, wall_ref, qkv_ref, att_ref, n1_ref, pre_ref, n2_ref, stat_ref = refs[
        5 + len(plan) : 13 + len(plan)
    ]
    raw, turned, in_sem, out_sem = refs[13 + len(plan) :]
    rows, width = x_ref.shape
    length = rows // seq_here
    pairs = width // (2 * HEAD_DIM)
    me = me_ref[0]
    for (part, unit, masks), block in zip(plan, blocks):
        for place, mask in enumerate(masks):
            row = pl.multiple_of((3 * (me ^ mask) + part) * unit, 16)
            pltpu.make_async_copy(block.at[place], raw.at[pl.ds(row, unit)], in_sem).start()
    valid = valid_rows(len_ref, rows, seq_here)
    x = (x_ref[...].astype(jnp.float32) * valid).astype(jnp.bfloat16)
    pltpu.make_async_copy(raw, raw, in_sem).wait()

    split3, split4 = interleave(3, 384), interleave(4, 256)
    for b in range(width // 128):
        block = dot_nn(split3, raw[384 * b : 384 * b + 384, :]).astype(jnp.bfloat16)
        for p in range(3):
            turned[width * p + 128 * b : width * p + 128 * b + 128, :] = block[
                128 * p : 128 * p + 128
            ]
    up = 4 * width
    for b in range(width // 64):
        block = dot_nn(split4, raw[up + 256 * b : up + 256 * b + 256, :]).astype(jnp.bfloat16)
        for p in range(4):
            row = width * (3 + p) + 64 * b
            turned[row : row + 64, :] = block[64 * p : 64 * p + 64]
    saves = [
        pltpu.make_async_copy(source, target, out_sem.at[k])
        for k, (source, target) in enumerate(
            (
                (turned.at[0 : 3 * width], wall_ref.at[0 : 3 * width]),
                (raw.at[3 * width : up], wall_ref.at[3 * width : up]),
                (turned.at[3 * width : 7 * width], wall_ref.at[up : 2 * up]),
                (raw.at[2 * up : 3 * up], wall_ref.at[2 * up : 3 * up]),
            )
        )
    ]
    for save in saves:
        save.start()

    for p, bias in ((0, 0), (1, None), (2, 1)):
        value = dot_nn(x, turned[width * p : width * (p + 1), :])
        if bias is not None:
            value = value + vec_ref[bias : bias + 1, :]
        qkv_ref[:, width * p : width * (p + 1)] = value.astype(jnp.bfloat16)

    stats = jnp.zeros((2 * length, 128), jnp.float32)
    lane = lax.broadcasted_iota(jnp.int32, stats.shape, 1)
    for seq in range(seq_here):
        here = slice(seq * length, (seq + 1) * length)
        for g in range(pairs):
            cols = [slice(width * p + 128 * g, width * p + 128 * g + 128) for p in range(3)]
            query, key, value = (qkv_ref[here, c] for c in cols)
            scores = pair_scores(stack_pair(query), key, len_ref[seq])
            top = jnp.max(scores, axis=-1, keepdims=True)
            expo = jnp.exp(scores - top)
            total = jnp.sum(expo, axis=-1, keepdims=True)
            stats = jnp.where(lane == seq * pairs + g, top + jnp.log(total), stats)
            probs = (expo / total).astype(jnp.bfloat16)
            att_ref[here, 128 * g : 128 * g + 128] = join_pair(dot_nn(probs, value)).astype(
                jnp.bfloat16
            )

    branch = dot_nn(att_ref[...], raw[3 * width : up, :]) + vec_ref[2:3, :]
    normed, inverse = center_rows(x.astype(jnp.float32) + branch)
    n1_ref[...] = normed
    stat_one = seq_here * pairs
    hidden = normed * vec_ref[3:4, :] + vec_ref[4:5, :]
    hidden_low = hidden.astype(jnp.bfloat16)
    total = hidden + vec_ref[9:10, :]
    for p in range(4):
        pre = dot_nn(hidden_low, turned[width * (3 + p) : width * (4 + p), :])
        pre = pre + vec_ref[5 + p : 6 + p, :]
        pre_ref[:, width * p : width * (p + 1)] = pre
        act = (pre * gelu_phi(pre)).astype(jnp.bfloat16)
        total = total + dot_nn(act, raw[2 * up + width * p : 2 * up + width * (p + 1), :])
    normed, inverse_two = center_rows(total)
    n2_ref[...] = normed
    wide = lax.broadcasted_iota(jnp.int32, (rows, 128), 1)
    ends = jnp.where(
        wide == stat_one, inverse, jnp.where(wide == stat_one + 1, inverse_two, 0.0)
    )
    stat_ref[0] = stats
    stat_ref[1] = ends
    output = ((normed * vec_ref[10:11, :] + vec_ref[11:12, :]) * valid).astype(jnp.bfloat16)
    spot = lax.broadcasted_iota(jnp.int32, (place_ref.shape[0], rows), 1)
    choose = (spot == place_ref[...]).astype(jnp.bfloat16)
    heads_ref[...] = dot_nn(choose, output).astype(jnp.bfloat16)
    for save in saves:
        save.wait()


def backward_kernel(plan, unit, seq_here, *refs):
    me_ref, len_ref, place_ref, x_ref, vec_ref, top_ref = refs[:6]
    wall_ref, qkv_ref, att_ref, n1_ref, pre_ref, n2_ref, stat_ref = refs[6:13]
    gin_ref, dvec_ref = refs[13:15]
    sinks = refs[15:21]
    wall, grads, parts, dqkv, in_sem, out_sem = refs[21:]
    rows, width = x_ref.shape
    length = rows // seq_here
    pairs = width // (2 * HEAD_DIM)
    low = jnp.bfloat16
    me = me_ref[0]
    up = 4 * width
    loads = [
        pltpu.make_async_copy(wall_ref.at[a:b], wall.at[a:b], in_sem.at[k])
        for k, (a, b) in enumerate(((2 * up, 3 * up), (up, 2 * up), (0, up)))
    ]
    for load in loads:
        load.start()

    def emit(first, last):
        for u in range(first // unit, last // unit):
            part = u % 3
            relative = (u // 3) ^ me
            spot = jnp.int32(0)
            bits, core_bit = plan[part]
            for k, bit in enumerate(bits):
                spot = spot + jnp.where((relative & bit) != 0, 1 << (len(bits) - 1 - k), 0)
            across = (relative & core_bit) != 0
            source = grads.at[u * unit : (u + 1) * unit]

            @pl.when(across)
            def _(part=part, source=source, spot=spot):
                pltpu.make_async_copy(
                    source, sinks[2 * part + 1].at[spot], out_sem.at[2 * part + 1]
                ).start()

            @pl.when(jnp.logical_not(across))
            def _(part=part, source=source, spot=spot):
                pltpu.make_async_copy(
                    source, sinks[2 * part].at[spot], out_sem.at[2 * part]
                ).start()

    valid = valid_rows(len_ref, rows, seq_here)
    x = (x_ref[...].astype(jnp.float32) * valid).astype(low)
    stat_one = seq_here * pairs
    wide = lax.broadcasted_iota(jnp.int32, (rows, 128), 1)
    ends = stat_ref[1]
    inverse_one = jnp.sum(jnp.where(wide == stat_one, ends, 0.0), axis=-1, keepdims=True)
    inverse_two = jnp.sum(jnp.where(wide == stat_one + 1, ends, 0.0), axis=-1, keepdims=True)

    spot = lax.broadcasted_iota(jnp.int32, (rows, place_ref.shape[1]), 0)
    choose = (spot == place_ref[...]).astype(jnp.float32)
    d_output = valid * lax.dot_general(
        choose,
        top_ref[...],
        (((1,), (0,)), ((), ())),
        precision=lax.Precision.HIGHEST,
        preferred_element_type=jnp.float32,
    )
    normed = n2_ref[...]

    def sums(row, value):
        dvec_ref[row : row + 1, :] = jnp.sum(value, axis=0, keepdims=True)

    sums(10, d_output * normed)
    sums(11, d_output)
    d_resid = norm_back(d_output * vec_ref[10:11, :], normed, inverse_two)
    d_ffn = d_resid.astype(low)
    sums(9, d_ffn.astype(jnp.float32))
    normed = n1_ref[...]
    hidden_low = (normed * vec_ref[3:4, :] + vec_ref[4:5, :]).astype(low)
    d_hidden = d_resid
    for load in loads[:2]:
        load.wait()
    for p in range(4):
        pre = pre_ref[:, width * p : width * (p + 1)]
        phi = gelu_phi(pre)
        act = (pre * phi).astype(low)
        down = slice(2 * up + width * p, 2 * up + width * (p + 1))
        grads[down, :] = contract_rows(act, d_ffn).astype(low)
        slope = phi + pre * jnp.exp(-0.5 * pre * pre) * 0.3989422804014327
        d_pre = (contract_cols(d_ffn, wall[down, :]) * slope).astype(low)
        sums(5 + p, d_pre.astype(jnp.float32))
        parts[width * p : width * (p + 1), :] = contract_rows(hidden_low, d_pre).astype(low)
        d_hidden = d_hidden + contract_cols(d_pre, wall[up + width * p : up + width * (p + 1), :])
    emit(2 * up, 3 * up)
    split4 = interleave(4, 256)
    for b in range(width // 64):
        block = jnp.concatenate(
            [parts[width * p + 64 * b : width * p + 64 * b + 64, :] for p in range(4)], axis=0
        )
        grads[up + 256 * b : up + 256 * b + 256, :] = contract_rows(split4, block).astype(low)
    emit(up, 2 * up)

    sums(3, d_hidden * normed)
    sums(4, d_hidden)
    d_resid = norm_back(d_hidden * vec_ref[3:4, :], normed, inverse_one)
    d_branch = d_resid.astype(low)
    sums(2, d_branch.astype(jnp.float32))
    grads[3 * width : up, :] = contract_rows(att_ref[...], d_branch).astype(low)
    loads[2].wait()
    d_att = contract_cols(d_branch, wall[3 * width : up, :]).astype(low)
    lane = lax.broadcasted_iota(jnp.int32, (2 * length, 128), 1)
    stats = stat_ref[0]
    for seq in range(seq_here):
        here = slice(seq * length, (seq + 1) * length)
        for g in range(pairs):
            cols = [slice(width * p + 128 * g, width * p + 128 * g + 128) for p in range(3)]
            query, key, value = (qkv_ref[here, c] for c in cols)
            query = stack_pair(query)
            log_sum = jnp.sum(
                jnp.where(lane == seq * pairs + g, stats, 0.0), axis=-1, keepdims=True
            )
            probs = jnp.exp(pair_scores(query, key, len_ref[seq]) - log_sum)
            d_heads = stack_pair(d_att[here, 128 * g : 128 * g + 128])
            d_probs = contract_cols(d_heads, value)
            dqkv[here, cols[2]] = contract_rows(probs.astype(low), d_heads).astype(low)
            delta = jnp.sum(d_probs * probs, axis=-1, keepdims=True)
            d_scores = (probs * (d_probs - delta)).astype(low)
            scale = HEAD_DIM ** (-0.5)
            dqkv[here, cols[0]] = (join_pair(dot_nn(d_scores, key)) * scale).astype(low)
            dqkv[here, cols[1]] = (contract_rows(d_scores, query) * scale).astype(low)
    sums(0, dqkv[:, :width].astype(jnp.float32))
    sums(1, dqkv[:, 2 * width :].astype(jnp.float32))
    total = d_resid
    for p in range(3):
        d_part = dqkv[:, width * p : width * (p + 1)]
        parts[width * p : width * (p + 1), :] = contract_rows(x, d_part).astype(low)
        total = total + contract_cols(d_part, wall[width * p : width * (p + 1), :])
    split3 = interleave(3, 384)
    for b in range(width // 128):
        block = jnp.concatenate(
            [parts[width * p + 128 * b : width * p + 128 * b + 128, :] for p in range(3)], axis=0
        )
        grads[384 * b : 384 * b + 384, :] = contract_rows(split3, block).astype(low)
    emit(0, up)
    gin_ref[...] = total * valid
    for k, sink in enumerate(sinks):
        pltpu.make_async_copy(sink, sink, out_sem.at[k]).wait()


def call_forward(me, lengths, places, rows, vecs, gathered, seq_here):
    count, width = rows.shape
    pieces = [(part, piece, masks) for part, own in enumerate(gathered) for piece, masks in own]
    plan = tuple((part, piece.shape[1], tuple(masks)) for part, piece, masks in pieces)
    total = 12 * width
    vmem = pl.BlockSpec(memory_space=pltpu.VMEM)
    smem = pl.BlockSpec(memory_space=pltpu.SMEM)
    hbm = pl.BlockSpec(memory_space=pl.ANY)
    low, full = jnp.bfloat16, jnp.float32
    return pl.pallas_call(
        functools.partial(forward_kernel, plan, seq_here),
        out_shape=[
            jax.ShapeDtypeStruct((places.shape[0], width), low),
            jax.ShapeDtypeStruct((total, width), low),
            jax.ShapeDtypeStruct((count, 3 * width), low),
            jax.ShapeDtypeStruct((count, width), low),
            jax.ShapeDtypeStruct((count, width), full),
            jax.ShapeDtypeStruct((count, 4 * width), full),
            jax.ShapeDtypeStruct((count, width), full),
            jax.ShapeDtypeStruct((2, count, 128), full),
        ],
        in_specs=[smem, smem, vmem, vmem, vmem] + [hbm] * len(pieces),
        out_specs=[vmem, hbm] + [vmem] * 6,
        scratch_shapes=[
            pltpu.VMEM((total, width), low),
            pltpu.VMEM((7 * width, width), low),
            pltpu.SemaphoreType.DMA,
            pltpu.SemaphoreType.DMA((4,)),
        ],
        compiler_params=pltpu.CompilerParams(vmem_limit_bytes=56 * 2**20),
        cost_estimate=pl.CostEstimate(
            flops=2 * count * total * width, bytes_accessed=48 * 2**20, transcendentals=0
        ),
    )(me, lengths, places, rows, vecs, *[piece for _, piece, _ in pieces])


def call_backward(me, lengths, places, rows, vecs, top, saved, plan, unit, seq_here):
    count, width = rows.shape
    total = 12 * width
    vmem = pl.BlockSpec(memory_space=pltpu.VMEM)
    smem = pl.BlockSpec(memory_space=pltpu.SMEM)
    hbm = pl.BlockSpec(memory_space=pl.ANY)
    low, full = jnp.bfloat16, jnp.float32
    half = total // unit // 6
    return pl.pallas_call(
        functools.partial(backward_kernel, plan, unit, seq_here),
        out_shape=[
            jax.ShapeDtypeStruct((count, width), full),
            jax.ShapeDtypeStruct((12, width), full),
        ]
        + [jax.ShapeDtypeStruct((half, unit, width), low)] * 6,
        in_specs=[smem, smem, vmem, vmem, vmem, vmem, hbm] + [vmem] * 6,
        out_specs=[vmem, vmem] + [hbm] * 6,
        scratch_shapes=[
            pltpu.VMEM((total, width), low),
            pltpu.VMEM((total, width), low),
            pltpu.VMEM((4 * width, width), low),
            pltpu.VMEM((count, 3 * width), low),
            pltpu.SemaphoreType.DMA((3,)),
            pltpu.SemaphoreType.DMA((6,)),
        ],
        compiler_params=pltpu.CompilerParams(vmem_limit_bytes=60 * 2**20),
        cost_estimate=pl.CostEstimate(
            flops=4 * count * total * width, bytes_accessed=48 * 2**20, transcendentals=0
        ),
    )(me, lengths, places, rows, vecs, top, *saved)


def plain_forward(mats_all, vecs_all, block_input, span_lengths):
    seq_here, length, width = block_input.shape
    rows_here = seq_here * length
    heads_count = width // HEAD_DIM
    head_scale = HEAD_DIM ** (-0.5)
    low = jnp.bfloat16
    w_qkv, w_out, w_up, w_down = split_mats(mats_all)
    bias_q, bias_v, bias_out, gain_one, shift_one, bias_up, bias_down, gain_two, shift_two = (
        split_vecs(vecs_all)
    )
    valid = jnp.arange(length)[None, :] < span_lengths[:, None]
    valid_col = valid.reshape(rows_here, 1).astype(jnp.float32)
    tok_rows = (block_input * valid[:, :, None].astype(low)).reshape(rows_here, width)
    qkv_bias = jnp.concatenate([bias_q, jnp.zeros((width,), jnp.float32), bias_v])
    projected = (jnp.dot(tok_rows, w_qkv, preferred_element_type=jnp.float32) + qkv_bias).astype(
        low
    )
    shaped = projected.reshape(seq_here, length, 3, heads_count, HEAD_DIM)
    queries = shaped[:, :, 0]
    key_rows = shaped[:, :, 1]
    value_rows = shaped[:, :, 2]
    key_valid = valid[:, None, None, :]

    def make_scores():
        raw = (
            jnp.einsum("sqhd,skhd->shqk", queries, key_rows, preferred_element_type=jnp.float32)
            * head_scale
        )
        return jnp.where(key_valid, raw, -1e30)

    scores = make_scores()
    row_max = jnp.max(scores, axis=-1, keepdims=True)
    expo_vals = jnp.exp(scores - row_max)
    row_sum = jnp.sum(expo_vals, axis=-1, keepdims=True)
    row_lse = row_max + jnp.log(row_sum)
    attn_probs = (expo_vals / row_sum).astype(low)
    attended = (
        jnp.einsum("shqk,skhd->sqhd", attn_probs, value_rows, preferred_element_type=jnp.float32)
        .reshape(rows_here, width)
        .astype(low)
    )
    branch = jnp.dot(attended, w_out, preferred_element_type=jnp.float32) + bias_out
    normed_one, inverse_one = center_scale(tok_rows.astype(jnp.float32) + branch)
    hidden_one = normed_one * gain_one + shift_one
    hidden_low = hidden_one.astype(low)
    pre_act = jnp.dot(hidden_low, w_up, preferred_element_type=jnp.float32) + bias_up
    act_low = jax.nn.gelu(pre_act, approximate=False).astype(low)
    ffn_out = jnp.dot(act_low, w_down, preferred_element_type=jnp.float32) + bias_down
    normed_two, inverse_two = center_scale(hidden_one + ffn_out)
    output = (normed_two * gain_two + shift_two) * valid_col

    def plain_backward(d_output):
        d_gain_two = jnp.sum(d_output * normed_two, axis=0)
        d_shift_two = jnp.sum(d_output, axis=0)
        d_resid_two = norm_back(d_output * gain_two, normed_two, inverse_two)
        d_ffn = d_resid_two.astype(low)
        d_bias_down = jnp.sum(d_ffn.astype(jnp.float32), axis=0)
        d_w_down = contract_rows(act_low, d_ffn)
        d_act = contract_cols(d_ffn, w_down)
        d_pre = (d_act * gelu_slope(pre_act)).astype(low)
        d_bias_up = jnp.sum(d_pre.astype(jnp.float32), axis=0)
        d_w_up = contract_rows(hidden_low, d_pre)
        d_hidden = contract_cols(d_pre, w_up) + d_resid_two
        d_gain_one = jnp.sum(d_hidden * normed_one, axis=0)
        d_shift_one = jnp.sum(d_hidden, axis=0)
        d_resid_one = norm_back(d_hidden * gain_one, normed_one, inverse_one)
        d_branch = d_resid_one.astype(low)
        d_bias_out = jnp.sum(d_branch.astype(jnp.float32), axis=0)
        d_w_out = contract_rows(attended, d_branch)
        d_attended = (
            contract_cols(d_branch, w_out).astype(low).reshape(seq_here, length, heads_count, HEAD_DIM)
        )
        probs_again = jnp.exp(make_scores() - row_lse)
        probs_low = probs_again.astype(low)
        d_probs = jnp.einsum(
            "sqhd,skhd->shqk", d_attended, value_rows, preferred_element_type=jnp.float32
        )
        d_values = jnp.einsum(
            "shqk,sqhd->skhd", probs_low, d_attended, preferred_element_type=jnp.float32
        )
        row_delta = jnp.sum(d_probs * probs_again, axis=-1, keepdims=True)
        d_scores = (probs_again * (d_probs - row_delta)).astype(low)
        d_queries = (
            jnp.einsum("shqk,skhd->sqhd", d_scores, key_rows, preferred_element_type=jnp.float32)
            * head_scale
        )
        d_keys = (
            jnp.einsum("shqk,sqhd->skhd", d_scores, queries, preferred_element_type=jnp.float32)
            * head_scale
        )
        d_qkv = jnp.concatenate(
            [
                d_queries.reshape(rows_here, width),
                d_keys.reshape(rows_here, width),
                d_values.reshape(rows_here, width),
            ],
            axis=1,
        ).astype(low)
        d_qkv_float = d_qkv.astype(jnp.float32)
        d_bias_q = jnp.sum(d_qkv_float[:, :width], axis=0)
        d_bias_v = jnp.sum(d_qkv_float[:, 2 * width :], axis=0)
        d_w_qkv = contract_rows(tok_rows, d_qkv)
        grad_input = ((contract_cols(d_qkv, w_qkv) + d_resid_one) * valid_col).reshape(
            seq_here, length, width
        )
        d_mats = jnp.concatenate(
            [
                piece.astype(low).reshape(-1, width)
                for piece in (d_w_qkv, d_w_out, d_w_up, d_w_down)
            ]
        )
        d_vecs = jnp.concatenate(
            [
                d_bias_q,
                d_bias_v,
                d_bias_out,
                d_gain_one,
                d_shift_one,
                d_bias_up,
                d_bias_down,
                d_gain_two,
                d_shift_two,
            ]
        )
        return grad_input, d_mats, d_vecs

    return output, plain_backward


def on_device(
    names,
    core,
    block_input,
    span_lengths,
    mlm_positions,
    mlm_labels,
    span_pairs,
    layer_mats,
    vectors,
    embedding,
    mom1_mats,
    mom2_mats,
    mom1_vecs,
    mom2_vecs,
    mom1_embed,
    mom2_embed,
):
    seq_here, length, width = block_input.shape
    rows_here = seq_here * length
    devices = 2 ** len(names)
    me = lax.axis_index(names)
    orders = bit_orders(names, core)
    slots = mlm_positions.shape[1]
    picks_here = seq_here * slots
    low = jnp.bfloat16

    third = layer_mats.shape[0] // width // 3
    by_kernel = third % 16 == 0
    vec_here = vectors.shape[0]
    mats_low = layer_mats.astype(low).reshape(3, third, width)

    def pad_row(row):
        return jnp.pad(row, (0, width - row.shape[0])).astype(low)[None]

    labels_flat = mlm_labels.reshape(-1)
    small = jnp.concatenate(
        [
            pad_row(vectors.astype(low)),
            pad_row(labels_flat // 256),
            pad_row(labels_flat % 256),
            pad_row(jnp.concatenate([span_pairs // 256, span_pairs % 256, span_lengths // 4])),
            jnp.zeros((4, width), low),
        ]
    )
    small_all = gather_bits(small, orders[0], names)
    if by_kernel:
        gathered = [gather_relative(mats_low[k], orders[k], names) for k in range(3)]
    else:
        gathered = [gather_bits(mats_low[k], orders[k], names) for k in range(3)]
    vecs_all = small_all[:, 0, :vec_here].reshape(-1)
    labels_all = (
        small_all[:, 1, :picks_here].astype(jnp.int32) * 256
        + small_all[:, 2, :picks_here].astype(jnp.int32)
    ).reshape(-1)
    ints_all = small_all[:, 3, : 3 * seq_here].astype(jnp.int32)
    pairs_all = (ints_all[:, :seq_here] * 256 + ints_all[:, seq_here : 2 * seq_here]).reshape(-1)
    quarter_all = ints_all[:, 2 * seq_here :].reshape(-1)

    embed_here = embedding.shape[0]
    shifted_rows = -(-embed_here // width)
    shift = (me * (embed_here % width)) % width
    first_row = me * (embed_here // width) + (me * (embed_here % width)) // width
    embed_low = embedding.astype(low)
    ring = range(devices)
    from_left = lax.ppermute(embed_low[-width:], names, [(k, (k + 1) % devices) for k in ring])
    from_right = lax.ppermute(embed_low[:width], names, [((k + 1) % devices, k) for k in ring])
    shifted = jnp.concatenate(
        [
            from_left,
            embed_low,
            from_right,
            jnp.zeros((shifted_rows * width - embed_here,), low),
        ]
    ).reshape(shifted_rows + 2, width)
    lanes = jnp.arange(width)
    same_row = (lanes < width - shift)[None, :]
    rolled = jnp.where(same_row, shifted[1:], shifted[:-1])
    turn = ((lanes[:, None] + shift) % width == lanes[None, :]).astype(low)
    table = jnp.dot(rolled, turn, preferred_element_type=jnp.float32).astype(low)
    row_start = jnp.arange(shifted_rows + 1) * width - shift
    owned = (row_start >= 0) & (row_start < embed_here)
    touched = (row_start + width > 0) & (row_start < embed_here)
    table_owned = jnp.where(owned[:, None], table, 0)

    heads_pad = -(picks_here + seq_here) % 8
    seq_start = jnp.arange(seq_here, dtype=jnp.int32) * length
    if by_kernel:
        lone = me.astype(jnp.int32).reshape(1)
        tok_rows = block_input.reshape(rows_here, width)
        vec_rows = vecs_all.astype(jnp.float32).reshape(-1, width)
        places = jnp.concatenate(
            [
                (mlm_positions + seq_start[:, None]).reshape(-1),
                seq_start,
                jnp.full((heads_pad,), -1, jnp.int32),
            ]
        )
        heads_rows, *saved = call_forward(
            lone, span_lengths, places[:, None], tok_rows, vec_rows, gathered, seq_here
        )
    else:
        mats_all = jnp.stack(gathered, axis=1).reshape(-1)
        output, plain_backward = plain_forward(mats_all, vecs_all, block_input, span_lengths)
        output_seq = output.reshape(seq_here, length, width)
        picked_here = jnp.take_along_axis(output_seq, mlm_positions[:, :, None], axis=1)
        heads_rows = jnp.concatenate(
            [
                picked_here.reshape(-1, width),
                output_seq[:, 0, :],
                jnp.zeros((heads_pad, width), jnp.float32),
            ]
        ).astype(low)

    cut = width // 3
    heads_all = jnp.concatenate(
        [
            gather_bits(heads_rows[:, k * cut : (k + 1) * cut], orders[k], names)
            for k in range(3)
        ],
        axis=2,
    )
    picked = heads_all[:, :picks_here, :].reshape(-1, width)
    cls_all = heads_all[:, picks_here : picks_here + seq_here, :].reshape(-1, width)

    logits = contract_cols(picked, table)
    masked = jnp.where(owned[None, :], logits, -jnp.inf)
    part_max = jnp.max(masked, axis=-1)
    part_sum = jnp.sum(jnp.exp(masked - part_max[:, None]), axis=-1)
    stats = jnp.stack([part_max, part_sum]).reshape(1, -1, 128)
    stats_all = lax.all_to_all(
        jnp.broadcast_to(stats, (devices,) + stats.shape[1:]), names, 0, 0, tiled=True
    ).reshape(devices, 2, -1)
    full_max = jnp.max(stats_all[:, 0], axis=0)
    full_sum = jnp.sum(stats_all[:, 1] * jnp.exp(stats_all[:, 0] - full_max), axis=0)
    row_of = labels_all - first_row
    hot = row_of[:, None] == jnp.arange(shifted_rows + 1)[None, :]
    used = (jnp.arange(slots)[None, :] < quarter_all[:, None]).reshape(-1, 1)
    probs = jnp.exp(logits - full_max[:, None]) / full_sum[:, None]
    d_logits = jnp.where(
        used & touched[None, :], probs - hot.astype(jnp.float32), 0.0
    ).astype(low)
    d_picked_part = jnp.dot(d_logits, table_owned, preferred_element_type=jnp.float32).astype(low)
    blocks = d_picked_part.reshape(devices, picks_here, width)
    d_picked = jnp.concatenate(
        [
            reduce_bits(blocks[:, :, k * cut : (k + 1) * cut], orders[k][::-1], names)
            for k in range(3)
        ],
        axis=1,
    ).astype(jnp.float32)

    span_scale = 2.0 / math.sqrt(width)
    columns = jnp.arange(cls_all.shape[0])
    sims = contract_cols(cls_all, cls_all) * span_scale
    sims = jnp.where(columns[None, :] == columns[:, None], -1e30, sims)
    partner_hot = (columns[None, :] == pairs_all[:, None]).astype(jnp.float32)
    d_sims = (jax.nn.softmax(sims, axis=-1) - partner_hot).astype(low)
    mine = me * seq_here
    d_sims_rows = lax.dynamic_slice_in_dim(d_sims, mine, seq_here, 0)
    d_sims_cols = lax.dynamic_slice_in_dim(d_sims, mine, seq_here, 1)
    d_cls = (
        jnp.dot(d_sims_rows, cls_all, preferred_element_type=jnp.float32)
        + contract_rows(d_sims_cols, cls_all)
    ) * span_scale
    if by_kernel:
        top = jnp.concatenate([d_picked, d_cls, jnp.zeros((heads_pad, width), jnp.float32)])
        back_orders = [order[::-1] for order in orders]
        plan = tuple(
            (
                tuple(device_mask(name, names) for name in order[1:]),
                device_mask(order[0], names),
            )
            for order in back_orders
        )
        grad_input, d_vecs, *sinks = call_backward(
            lone, span_lengths, places[None], tok_rows, vec_rows, top, saved, plan, third, seq_here
        )
        grad_input = grad_input.reshape(seq_here, length, width)
        summed = [
            reduce_relative(sinks[2 * k], sinks[2 * k + 1], back_orders[k]) for k in range(3)
        ]
    else:
        select = (mlm_positions[:, :, None] == jnp.arange(length)[None, None, :]).astype(
            jnp.float32
        )
        d_output_seq = jnp.einsum(
            "gor,gon->grn",
            select,
            d_picked.reshape(seq_here, slots, width),
            precision=lax.Precision.HIGHEST,
        )
        d_output_seq = d_output_seq.at[:, 0, :].add(d_cls)
        valid = jnp.arange(length)[None, :] < span_lengths[:, None]
        d_output = d_output_seq.reshape(rows_here, width) * valid.reshape(rows_here, 1)
        grad_input, d_mats, d_vecs = plain_backward(d_output)
        d_mats = d_mats.reshape(devices, 3, third, width)
        summed = [
            reduce_bits(d_mats[:, k], orders[k][::-1], names).astype(jnp.float32)
            for k in range(3)
        ]
    grad_mats = jnp.concatenate(summed).reshape(-1)
    grad_vecs = reduce_bits(d_vecs.reshape(devices, vec_here), orders[0][::-1], names)

    picked_turned = jnp.dot(picked, turn.T, preferred_element_type=jnp.float32).astype(low)
    d_rolled = contract_rows(d_logits, picked_turned)
    grad_embed = jnp.where(same_row, d_rolled[:-1], d_rolled[1:]).reshape(-1)[:embed_here]

    step_float = float(ADAM_STEP)
    step_mats = adam_step(layer_mats, grad_mats, mom1_mats, mom2_mats, step_float, decay_rate)
    step_vecs = adam_step(vectors, grad_vecs, mom1_vecs, mom2_vecs, step_float, 0.0)
    step_embed = adam_step(embedding, grad_embed, mom1_embed, mom2_embed, step_float, decay_rate)
    return (grad_input, grad_mats, grad_vecs, grad_embed, step_mats, step_vecs, step_embed)


def solution(mesh):
    fsdp_bits = mesh.shape["fsdp"].bit_length() - 1
    rep_bits = mesh.shape["rep"].bit_length() - 1
    names = tuple(f"f{k}" for k in reversed(range(fsdp_bits)))
    core = names[-1]
    names = names + tuple(f"r{k}" for k in reversed(range(rep_bits)))
    bits = Mesh(mesh.devices.reshape((2,) * len(names)), names)
    seqs = P(names, None, None)
    pairs = P(names, None)
    flat = P(names)
    return jax.shard_map(
        functools.partial(on_device, names, core),
        mesh=bits,
        in_specs=(seqs, flat, pairs, pairs) + (flat,) * 10,
        out_specs=(seqs,) + (flat,) * 6,
        check_vma=False,
    )
```

```python
import functools
import math

import jax
import jax.numpy as jnp
from jax import lax
from jax.experimental import pallas as pl
from jax.experimental.pallas import tpu as pltpu
from jax.sharding import Mesh, PartitionSpec as P

D = 768
FF = 3072
HEAD_DIM = 64
VOCAB = 30522
ADAM_STEP = 10


norm_eps = 1e-12
beta_one = 0.9
beta_two = 0.999
adam_eps = 1e-06
decay_rate = 0.01


def split_mats(flat):
    first = 3 * D * D
    second = first + D * D
    third = second + D * FF
    return (
        flat[:first].reshape(D, 3 * D),
        flat[first:second].reshape(D, D),
        flat[second:third].reshape(D, FF),
        flat[third:].reshape(FF, D),
    )


def split_vecs(flat):
    widths_list = [D, D, D, D, D, FF, D, D, D]
    pieces = []
    offset = 0
    for piece_width in widths_list:
        pieces.append(flat[offset : offset + piece_width].astype(jnp.float32))
        offset = offset + piece_width
    return pieces


def center_scale(resid):
    center = resid - jnp.mean(resid, axis=-1, keepdims=True)
    inverse = lax.rsqrt(jnp.mean(center * center, axis=-1, keepdims=True) + norm_eps)
    return (center * inverse, inverse)


def norm_back(d_normed, normed, inverse):
    return inverse * (
        d_normed
        - jnp.mean(d_normed, axis=-1, keepdims=True)
        - normed * jnp.mean(d_normed * normed, axis=-1, keepdims=True)
    )


def gelu_slope(value):
    return (
        0.5 * (1.0 + lax.erf(value * 0.7071067811865476))
        + value * jnp.exp(-0.5 * value * value) * 0.3989422804014327
    )


def contract_rows(left, right):
    return lax.dot_general(
        left, right, (((0,), (0,)), ((), ())), preferred_element_type=jnp.float32
    )


def contract_cols(left, right):
    return lax.dot_general(
        left, right, (((1,), (1,)), ((), ())), preferred_element_type=jnp.float32
    )


def adam_step(weight, grad, first, second, step_float, decay):
    first_new = beta_one * first + (1.0 - beta_one) * grad
    second_new = beta_two * second + (1.0 - beta_two) * grad * grad
    first_hat = first_new / (1.0 - beta_one**step_float)
    second_hat = second_new / (1.0 - beta_two**step_float)
    return first_hat / (jnp.sqrt(second_hat) + adam_eps) + decay * weight


def flip(value, name):
    return lax.ppermute(value, name, [(0, 1), (1, 0)])


def gather_bits(shard, order, names):
    grown = shard
    for name in order:
        other = flip(grown, name)
        first = lax.axis_index(name) == 0
        grown = jnp.stack([jnp.where(first, grown, other), jnp.where(first, other, grown)])
    axes = list(reversed(order))
    rank = len(axes)
    turn = [axes.index(name) for name in names] + list(range(rank, grown.ndim))
    return grown.transpose(turn).reshape((2**rank,) + shard.shape)


def reduce_bits(blocks, order, names):
    left = list(names)
    held = blocks.reshape((2,) * len(left) + blocks.shape[1:])
    for name in order:
        axis = left.index(name)
        here = lax.axis_index(name)
        send = lax.dynamic_index_in_dim(held, 1 - here, axis, keepdims=False)
        keep = lax.dynamic_index_in_dim(held, here, axis, keepdims=False)
        other = flip(send, name)
        held = (keep.astype(jnp.float32) + other.astype(jnp.float32)).astype(blocks.dtype)
        left.remove(name)
    return held


def bit_orders(names, core):
    outer = [name for name in names if name != core]
    count = len(outer)
    if count == 4:
        picks = ((0, 3, 2, 1), (0, 2, 1, 3), (0, 1, 3, 2))
        return [[outer[k] for k in pick] + [core] for pick in picks]
    step = max(1, count // 3)
    return [outer[step * k :] + outer[: step * k] + [core] for k in range(3)]


def device_mask(name, names):
    return 1 << (len(names) - 1 - names.index(name))


def gather_relative(shards, orders, names, early=(), work=None):
    held = []
    for shard, order in zip(shards, orders):
        grown, masks = shard[None], [0]
        for name in order[:-2]:
            grown = jnp.concatenate([grown, flip(grown, name)])
            masks = masks + [mask | device_mask(name, names) for mask in masks]
        held.append((grown, masks))
    grown_all = [grown for grown, _ in held]
    others = [flip(grown, order[-2]) for grown, order in zip(grown_all, orders)]
    if work is not None:
        grown_late, early = lax.optimization_barrier((grown_all, early))
        grown_all, early = lax.optimization_barrier((grown_late, work(*early)))
    gathered = []
    for grown, other, (_, masks), order in zip(grown_all, others, held, orders):
        bit = device_mask(order[-2], names)
        pieces = [(grown, masks), (other, [mask | bit for mask in masks])]
        bit = device_mask(order[-1], names)
        pieces = pieces + [
            (flip(piece, order[-1]), [mask | bit for mask in own]) for piece, own in pieces
        ]
        gathered.append(pieces)
    return gathered, early


def add_terms(terms):
    total = terms[0].astype(jnp.float32)
    for term in terms[1:]:
        total = total + term.astype(jnp.float32)
    return total


def reduce_relative(keeps, sends, orders, late):
    terms_all = [[keep] for keep in keeps]
    sends = list(sends)
    for step in range(len(orders[0])):
        for k, order in enumerate(orders):
            terms = terms_all[k] + [flip(sends[k], order[step])]
            half = terms[0].shape[0] // 2
            if half:
                sends[k] = add_terms([term[half:] for term in terms]).astype(terms[0].dtype)
                terms = [term[:half] for term in terms]
            terms_all[k] = terms
        if step == 0 and late:
            sends[-1], late = lax.optimization_barrier((sends[-1], late))
    return [add_terms(terms)[0] for terms in terms_all], late


def dot_nn(left, right):
    return lax.dot_general(
        left, right, (((1,), (0,)), ((), ())), preferred_element_type=jnp.float32
    )


def interleave(count, rows):
    span = rows // count
    to = lax.broadcasted_iota(jnp.int32, (rows, rows), 0)
    source = lax.broadcasted_iota(jnp.int32, (rows, rows), 1)
    return (source == count * lax.rem(to, span) + lax.div(to, span)).astype(jnp.bfloat16)


def valid_rows(len_ref, rows, seq_here):
    length = rows // seq_here
    row = lax.broadcasted_iota(jnp.int32, (rows, 1), 0)
    valid = jnp.zeros((rows, 1), jnp.float32)
    for seq in range(seq_here):
        inside = (row >= seq * length) & (row < seq * length + len_ref[seq])
        valid = jnp.where(inside, 1.0, valid)
    return valid


def stack_pair(value):
    lane = lax.broadcasted_iota(jnp.int32, value.shape, 1)
    zero = jnp.zeros_like(value)
    left = lane < HEAD_DIM
    return jnp.concatenate([jnp.where(left, value, zero), jnp.where(left, zero, value)], axis=0)


def join_pair(stacked):
    half = stacked.shape[0] // 2
    lane = lax.broadcasted_iota(jnp.int32, (half, stacked.shape[1]), 1)
    return jnp.where(lane < HEAD_DIM, stacked[:half], stacked[half:])


def pair_scores(stacked, keys, limit):
    raw = contract_cols(stacked, keys) * HEAD_DIM ** (-0.5)
    column = lax.broadcasted_iota(jnp.int32, raw.shape, 1)
    return jnp.where(column < limit, raw, -1e30)


def center_rows(resid):
    center = resid - jnp.mean(resid, axis=-1, keepdims=True)
    inverse = lax.rsqrt(jnp.mean(center * center, axis=-1, keepdims=True) + norm_eps)
    return center * inverse, inverse


def gelu_phi(value):
    return 0.5 * (1.0 + lax.erf(value * 0.7071067811865476))


def forward_kernel(plan, seq_here, *refs):
    me_ref, len_ref, place_ref, x_ref, vec_ref = refs[:5]
    blocks = refs[5 : 5 + len(plan)]
    heads_ref, wall_ref, qkv_ref, att_ref, n1_ref, pre_ref, n2_ref, stat_ref = refs[
        5 + len(plan) : 13 + len(plan)
    ]
    raw, turned, in_sem, out_sem = refs[13 + len(plan) :]
    rows, width = x_ref.shape
    length = rows // seq_here
    pairs = width // (2 * HEAD_DIM)
    me = me_ref[0]
    for (part, unit, masks), block in zip(plan, blocks):
        for place, mask in enumerate(masks):
            row = pl.multiple_of((3 * (me ^ mask) + part) * unit, 16)
            pltpu.make_async_copy(block.at[place], raw.at[pl.ds(row, unit)], in_sem).start()
    valid = valid_rows(len_ref, rows, seq_here)
    x = (x_ref[...].astype(jnp.float32) * valid).astype(jnp.bfloat16)
    pltpu.make_async_copy(raw, raw, in_sem).wait()

    split3, split4 = interleave(3, 384), interleave(4, 256)
    for b in range(width // 128):
        block = dot_nn(split3, raw[384 * b : 384 * b + 384, :]).astype(jnp.bfloat16)
        for p in range(3):
            turned[width * p + 128 * b : width * p + 128 * b + 128, :] = block[
                128 * p : 128 * p + 128
            ]
    up = 4 * width
    for b in range(width // 64):
        block = dot_nn(split4, raw[up + 256 * b : up + 256 * b + 256, :]).astype(jnp.bfloat16)
        for p in range(4):
            row = width * (3 + p) + 64 * b
            turned[row : row + 64, :] = block[64 * p : 64 * p + 64]
    saves = [
        pltpu.make_async_copy(source, target, out_sem.at[k])
        for k, (source, target) in enumerate(
            (
                (turned.at[0 : 3 * width], wall_ref.at[0 : 3 * width]),
                (raw.at[3 * width : up], wall_ref.at[3 * width : up]),
                (turned.at[3 * width : 7 * width], wall_ref.at[up : 2 * up]),
                (raw.at[2 * up : 3 * up], wall_ref.at[2 * up : 3 * up]),
            )
        )
    ]
    for save in saves:
        save.start()

    for p, bias in ((0, 0), (1, None), (2, 1)):
        value = dot_nn(x, turned[width * p : width * (p + 1), :])
        if bias is not None:
            value = value + vec_ref[bias : bias + 1, :]
        qkv_ref[:, width * p : width * (p + 1)] = value.astype(jnp.bfloat16)

    stats = jnp.zeros((2 * length, 128), jnp.float32)
    lane = lax.broadcasted_iota(jnp.int32, stats.shape, 1)
    for seq in range(seq_here):
        here = slice(seq * length, (seq + 1) * length)
        for g in range(pairs):
            cols = [slice(width * p + 128 * g, width * p + 128 * g + 128) for p in range(3)]
            query, key, value = (qkv_ref[here, c] for c in cols)
            scores = pair_scores(stack_pair(query), key, len_ref[seq])
            top = jnp.max(scores, axis=-1, keepdims=True)
            expo = jnp.exp(scores - top)
            total = jnp.sum(expo, axis=-1, keepdims=True)
            stats = jnp.where(lane == seq * pairs + g, top + jnp.log(total), stats)
            probs = (expo / total).astype(jnp.bfloat16)
            att_ref[here, 128 * g : 128 * g + 128] = join_pair(dot_nn(probs, value)).astype(
                jnp.bfloat16
            )

    branch = dot_nn(att_ref[...], raw[3 * width : up, :]) + vec_ref[2:3, :]
    normed, inverse = center_rows(x.astype(jnp.float32) + branch)
    n1_ref[...] = normed
    stat_one = seq_here * pairs
    hidden = normed * vec_ref[3:4, :] + vec_ref[4:5, :]
    hidden_low = hidden.astype(jnp.bfloat16)
    total = hidden + vec_ref[9:10, :]
    for p in range(4):
        pre = dot_nn(hidden_low, turned[width * (3 + p) : width * (4 + p), :])
        pre = pre + vec_ref[5 + p : 6 + p, :]
        pre_ref[:, width * p : width * (p + 1)] = pre
        act = (pre * gelu_phi(pre)).astype(jnp.bfloat16)
        total = total + dot_nn(act, raw[2 * up + width * p : 2 * up + width * (p + 1), :])
    normed, inverse_two = center_rows(total)
    n2_ref[...] = normed
    wide = lax.broadcasted_iota(jnp.int32, (rows, 128), 1)
    ends = jnp.where(
        wide == stat_one, inverse, jnp.where(wide == stat_one + 1, inverse_two, 0.0)
    )
    stat_ref[0] = stats
    stat_ref[1] = ends
    output = ((normed * vec_ref[10:11, :] + vec_ref[11:12, :]) * valid).astype(jnp.bfloat16)
    spot = lax.broadcasted_iota(jnp.int32, (place_ref.shape[0], rows), 1)
    choose = (spot == place_ref[...]).astype(jnp.bfloat16)
    heads_ref[...] = dot_nn(choose, output).astype(jnp.bfloat16)
    for save in saves:
        save.wait()


def backward_kernel(plan, unit, seq_here, *refs):
    me_ref, len_ref, place_ref, x_ref, vec_ref, top_ref = refs[:6]
    wall_ref, qkv_ref, att_ref, n1_ref, pre_ref, n2_ref, stat_ref = refs[6:13]
    gin_ref, dvec_ref = refs[13:15]
    sinks = refs[15:21]
    wall, grads, parts, dqkv, in_sem, out_sem = refs[21:]
    rows, width = x_ref.shape
    length = rows // seq_here
    pairs = width // (2 * HEAD_DIM)
    low = jnp.bfloat16
    me = me_ref[0]
    up = 4 * width
    loads = [
        pltpu.make_async_copy(wall_ref.at[a:b], wall.at[a:b], in_sem.at[k])
        for k, (a, b) in enumerate(((2 * up, 3 * up), (up, 2 * up), (0, up)))
    ]
    for load in loads:
        load.start()

    def emit(first, last):
        for u in range(first // unit, last // unit):
            part = u % 3
            relative = (u // 3) ^ me
            bits, core_bit = plan[part]
            spot = sink_spot(relative, bits)
            across = (relative & core_bit) != 0
            source = grads.at[u * unit : (u + 1) * unit]

            @pl.when(across)
            def _(part=part, source=source, spot=spot):
                pltpu.make_async_copy(
                    source, sinks[2 * part + 1].at[spot], out_sem.at[2 * part + 1]
                ).start()

            @pl.when(jnp.logical_not(across))
            def _(part=part, source=source, spot=spot):
                pltpu.make_async_copy(
                    source, sinks[2 * part].at[spot], out_sem.at[2 * part]
                ).start()

    valid = valid_rows(len_ref, rows, seq_here)
    x = (x_ref[...].astype(jnp.float32) * valid).astype(low)
    stat_one = seq_here * pairs
    wide = lax.broadcasted_iota(jnp.int32, (rows, 128), 1)
    ends = stat_ref[1]
    inverse_one = jnp.sum(jnp.where(wide == stat_one, ends, 0.0), axis=-1, keepdims=True)
    inverse_two = jnp.sum(jnp.where(wide == stat_one + 1, ends, 0.0), axis=-1, keepdims=True)

    spot = lax.broadcasted_iota(jnp.int32, (rows, place_ref.shape[1]), 0)
    choose = (spot == place_ref[...]).astype(jnp.float32)
    d_output = valid * lax.dot_general(
        choose,
        top_ref[...],
        (((1,), (0,)), ((), ())),
        precision=lax.Precision.HIGHEST,
        preferred_element_type=jnp.float32,
    )
    normed = n2_ref[...]

    def sums(row, value):
        dvec_ref[row : row + 1, :] = jnp.sum(value, axis=0, keepdims=True)

    sums(10, d_output * normed)
    sums(11, d_output)
    d_resid = norm_back(d_output * vec_ref[10:11, :], normed, inverse_two)
    d_ffn = d_resid.astype(low)
    sums(9, d_ffn.astype(jnp.float32))
    normed = n1_ref[...]
    hidden_low = (normed * vec_ref[3:4, :] + vec_ref[4:5, :]).astype(low)
    d_hidden = d_resid
    for load in loads[:2]:
        load.wait()
    for p in range(4):
        pre = pre_ref[:, width * p : width * (p + 1)]
        phi = gelu_phi(pre)
        act = (pre * phi).astype(low)
        down = slice(2 * up + width * p, 2 * up + width * (p + 1))
        grads[down, :] = contract_rows(act, d_ffn).astype(low)
        slope = phi + pre * jnp.exp(-0.5 * pre * pre) * 0.3989422804014327
        d_pre = (contract_cols(d_ffn, wall[down, :]) * slope).astype(low)
        sums(5 + p, d_pre.astype(jnp.float32))
        parts[width * p : width * (p + 1), :] = contract_rows(hidden_low, d_pre).astype(low)
        d_hidden = d_hidden + contract_cols(d_pre, wall[up + width * p : up + width * (p + 1), :])
    emit(2 * up, 3 * up)
    split4 = interleave(4, 256)
    for b in range(width // 64):
        block = jnp.concatenate(
            [parts[width * p + 64 * b : width * p + 64 * b + 64, :] for p in range(4)], axis=0
        )
        grads[up + 256 * b : up + 256 * b + 256, :] = contract_rows(split4, block).astype(low)
    emit(up, 2 * up)

    sums(3, d_hidden * normed)
    sums(4, d_hidden)
    d_resid = norm_back(d_hidden * vec_ref[3:4, :], normed, inverse_one)
    d_branch = d_resid.astype(low)
    sums(2, d_branch.astype(jnp.float32))
    grads[3 * width : up, :] = contract_rows(att_ref[...], d_branch).astype(low)
    loads[2].wait()
    d_att = contract_cols(d_branch, wall[3 * width : up, :]).astype(low)
    lane = lax.broadcasted_iota(jnp.int32, (2 * length, 128), 1)
    stats = stat_ref[0]
    for seq in range(seq_here):
        here = slice(seq * length, (seq + 1) * length)
        for g in range(pairs):
            cols = [slice(width * p + 128 * g, width * p + 128 * g + 128) for p in range(3)]
            query, key, value = (qkv_ref[here, c] for c in cols)
            query = stack_pair(query)
            log_sum = jnp.sum(
                jnp.where(lane == seq * pairs + g, stats, 0.0), axis=-1, keepdims=True
            )
            probs = jnp.exp(pair_scores(query, key, len_ref[seq]) - log_sum)
            d_heads = stack_pair(d_att[here, 128 * g : 128 * g + 128])
            d_probs = contract_cols(d_heads, value)
            dqkv[here, cols[2]] = contract_rows(probs.astype(low), d_heads).astype(low)
            delta = jnp.sum(d_probs * probs, axis=-1, keepdims=True)
            d_scores = (probs * (d_probs - delta)).astype(low)
            scale = HEAD_DIM ** (-0.5)
            dqkv[here, cols[0]] = (join_pair(dot_nn(d_scores, key)) * scale).astype(low)
            dqkv[here, cols[1]] = (contract_rows(d_scores, query) * scale).astype(low)
    sums(0, dqkv[:, :width].astype(jnp.float32))
    sums(1, dqkv[:, 2 * width :].astype(jnp.float32))
    total = d_resid
    for p in range(3):
        d_part = dqkv[:, width * p : width * (p + 1)]
        parts[width * p : width * (p + 1), :] = contract_rows(x, d_part).astype(low)
        total = total + contract_cols(d_part, wall[width * p : width * (p + 1), :])
    split3 = interleave(3, 384)
    for b in range(width // 128):
        block = jnp.concatenate(
            [parts[width * p + 128 * b : width * p + 128 * b + 128, :] for p in range(3)], axis=0
        )
        grads[384 * b : 384 * b + 384, :] = contract_rows(split3, block).astype(low)
    emit(0, up)
    gin_ref[...] = total * valid
    for k, sink in enumerate(sinks):
        pltpu.make_async_copy(sink, sink, out_sem.at[k]).wait()


def call_forward(me, lengths, places, rows, vecs, gathered, seq_here):
    count, width = rows.shape
    pieces = [(part, piece, masks) for part, own in enumerate(gathered) for piece, masks in own]
    plan = tuple((part, piece.shape[1], tuple(masks)) for part, piece, masks in pieces)
    total = 12 * width
    vmem = pl.BlockSpec(memory_space=pltpu.VMEM)
    smem = pl.BlockSpec(memory_space=pltpu.SMEM)
    hbm = pl.BlockSpec(memory_space=pl.ANY)
    low, full = jnp.bfloat16, jnp.float32
    return pl.pallas_call(
        functools.partial(forward_kernel, plan, seq_here),
        out_shape=[
            jax.ShapeDtypeStruct((places.shape[0], width), low),
            jax.ShapeDtypeStruct((total, width), low),
            jax.ShapeDtypeStruct((count, 3 * width), low),
            jax.ShapeDtypeStruct((count, width), low),
            jax.ShapeDtypeStruct((count, width), full),
            jax.ShapeDtypeStruct((count, 4 * width), full),
            jax.ShapeDtypeStruct((count, width), full),
            jax.ShapeDtypeStruct((2, count, 128), full),
        ],
        in_specs=[smem, smem, vmem, vmem, vmem] + [hbm] * len(pieces),
        out_specs=[vmem, hbm] + [vmem] * 6,
        scratch_shapes=[
            pltpu.VMEM((total, width), low),
            pltpu.VMEM((7 * width, width), low),
            pltpu.SemaphoreType.DMA,
            pltpu.SemaphoreType.DMA((4,)),
        ],
        compiler_params=pltpu.CompilerParams(vmem_limit_bytes=56 * 2**20),
        cost_estimate=pl.CostEstimate(
            flops=2 * count * total * width, bytes_accessed=48 * 2**20, transcendentals=0
        ),
    )(me, lengths, places, rows, vecs, *[piece for _, piece, _ in pieces])


def call_backward(me, lengths, places, rows, vecs, top, saved, plan, unit, seq_here):
    count, width = rows.shape
    total = 12 * width
    vmem = pl.BlockSpec(memory_space=pltpu.VMEM)
    smem = pl.BlockSpec(memory_space=pltpu.SMEM)
    hbm = pl.BlockSpec(memory_space=pl.ANY)
    low, full = jnp.bfloat16, jnp.float32
    half = total // unit // 6
    return pl.pallas_call(
        functools.partial(backward_kernel, plan, unit, seq_here),
        out_shape=[
            jax.ShapeDtypeStruct((count, width), full),
            jax.ShapeDtypeStruct((12, width), full),
        ]
        + [jax.ShapeDtypeStruct((half, unit, width), low)] * 6,
        in_specs=[smem, smem, vmem, vmem, vmem, vmem, hbm] + [vmem] * 6,
        out_specs=[vmem, vmem] + [hbm] * 6,
        scratch_shapes=[
            pltpu.VMEM((total, width), low),
            pltpu.VMEM((total, width), low),
            pltpu.VMEM((4 * width, width), low),
            pltpu.VMEM((count, 3 * width), low),
            pltpu.SemaphoreType.DMA((3,)),
            pltpu.SemaphoreType.DMA((6,)),
        ],
        compiler_params=pltpu.CompilerParams(vmem_limit_bytes=60 * 2**20),
        cost_estimate=pl.CostEstimate(
            flops=4 * count * total * width, bytes_accessed=48 * 2**20, transcendentals=0
        ),
    )(me, lengths, places, rows, vecs, top, *saved)


def turn_lanes(shift, width):
    source = lax.broadcasted_iota(jnp.int32, (width, width), 0) + shift
    source = jnp.where(source >= width, source - width, source)
    return (source == lax.broadcasted_iota(jnp.int32, (width, width), 1)).astype(jnp.bfloat16)


def table_kernel(embed_here, shift_ref, rows_ref, ends_ref, table_ref, owned_ref, tall):
    count, width = table_ref.shape
    here = rows_ref.shape[0]
    shift = shift_ref[0]
    tall[here:, :] = jnp.zeros((tall.shape[0] - here, width), jnp.float32)
    tall[8 : 8 + here, :] = rows_ref[...].astype(jnp.float32)
    tall[7:8, :] = ends_ref[0:1, :]
    tall[7 + here : 8 + here, :] = tall[7 + here : 8 + here, :] + ends_ref[1:2, :]
    tall[8 + here : 9 + here, :] = ends_ref[2:3, :]
    lane = lax.broadcasted_iota(jnp.int32, (count, width), 1)
    rolled = jnp.where(lane < width - shift, tall[8 : 8 + count, :], tall[7 : 7 + count, :])
    table = dot_nn(rolled.astype(jnp.bfloat16), turn_lanes(shift, width))
    start = lax.broadcasted_iota(jnp.int32, (count, 1), 0) * width - shift
    owned = (start >= 0) & (start < embed_here)
    table_ref[...] = table.astype(jnp.bfloat16)
    owned_ref[...] = jnp.where(owned, table, 0.0).astype(jnp.bfloat16)


def call_table(shift, rows, ends, count, embed_here):
    width = rows.shape[1]
    vmem = pl.BlockSpec(memory_space=pltpu.VMEM)
    smem = pl.BlockSpec(memory_space=pltpu.SMEM)
    return pl.pallas_call(
        functools.partial(table_kernel, embed_here),
        out_shape=[jax.ShapeDtypeStruct((count, width), jnp.bfloat16)] * 2,
        in_specs=[smem, vmem, vmem],
        out_specs=[vmem] * 2,
        scratch_shapes=[pltpu.VMEM((count + 16, width), jnp.float32)],
        compiler_params=pltpu.CompilerParams(vmem_limit_bytes=32 * 2**20),
        cost_estimate=pl.CostEstimate(
            flops=32 * count * width * width, bytes_accessed=40 * 2**20, transcendentals=0
        ),
    )(shift, rows, ends)


def logits_kernel(plan, embed_here, picks, span, *refs):
    me_ref, shift_ref, table_ref = refs[:3]
    blocks = refs[3 : 3 + len(plan)]
    picked, first, expo_ref, stat_ref, in_sem = refs[3 + len(plan) :]
    count, width = table_ref.shape
    me, shift = me_ref[0], shift_ref[0]
    extra = first.shape[1]
    for (part, masks), block in zip(plan, blocks):
        cut = block.shape[2]
        cols = pl.ds(part * cut, cut)
        for place, mask in enumerate(masks):
            device = me ^ mask
            row = pl.multiple_of(device * picks, 16)
            pltpu.make_async_copy(
                block.at[place, pl.ds(0, picks)], picked.at[pl.ds(row, picks), cols], in_sem.at[0]
            ).start()
            pltpu.make_async_copy(
                block.at[place, pl.ds(picks, extra)], first.at[device, :, cols], in_sem.at[1]
            ).start()
    start = lax.broadcasted_iota(jnp.int32, (count, 1), 0) * width - shift
    owned = (start >= 0) & (start < embed_here)
    touched = (start > -width) & (start < embed_here)
    pltpu.make_async_copy(first, first, in_sem.at[1]).wait()
    pltpu.make_async_copy(picked, picked, in_sem.at[0]).wait()
    chunks = picked.shape[0] // span
    for k in range(chunks):
        here = slice(k * span, (k + 1) * span)
        logits = jnp.where(touched, contract_cols(table_ref[...], picked[here, :]), -1e30)
        top = jnp.max(logits, axis=0, keepdims=True)
        expo = jnp.where(touched, jnp.exp(logits - top), 0.0)
        total = jnp.sum(jnp.where(owned, expo, 0.0), axis=0, keepdims=True)
        expo_ref[:, here] = expo
        copies = stat_ref.shape[0]
        stat_ref[:, k : k + 1, :] = jnp.broadcast_to(top[None], (copies, 1, span))
        stat_ref[:, chunks + k : chunks + k + 1, :] = jnp.broadcast_to(
            total[None], (copies, 1, span)
        )


def call_logits(me, shift, table, gathered, picks, embed_here, devices):
    count, width = table.shape
    pieces = [(part, piece, masks) for part, own in enumerate(gathered) for piece, masks in own]
    plan = tuple((part, tuple(masks)) for part, _, masks in pieces)
    extra = pieces[0][1].shape[1] - picks
    rows = devices * picks
    span = rows // 4
    vmem = pl.BlockSpec(memory_space=pltpu.VMEM)
    smem = pl.BlockSpec(memory_space=pltpu.SMEM)
    hbm = pl.BlockSpec(memory_space=pl.ANY)
    low, full = jnp.bfloat16, jnp.float32
    return pl.pallas_call(
        functools.partial(logits_kernel, plan, embed_here, picks, span),
        out_shape=[
            jax.ShapeDtypeStruct((rows, width), low),
            jax.ShapeDtypeStruct((devices, extra, width), low),
            jax.ShapeDtypeStruct((count, rows), full),
            jax.ShapeDtypeStruct((devices, 8, span), full),
        ],
        in_specs=[smem, smem, vmem] + [hbm] * len(pieces),
        out_specs=[vmem] * 4,
        scratch_shapes=[pltpu.SemaphoreType.DMA((2,))],
        compiler_params=pltpu.CompilerParams(vmem_limit_bytes=48 * 2**20),
        cost_estimate=pl.CostEstimate(
            flops=2 * rows * count * width, bytes_accessed=16 * 2**20, transcendentals=0
        ),
    )(me, shift, table, *[piece for _, piece, _ in pieces])


def sink_spot(relative, bits):
    spot = jnp.int32(0)
    for k, bit in enumerate(bits):
        spot = spot + jnp.where((relative & bit) != 0, 1 << (len(bits) - 1 - k), 0)
    return spot


def picked_kernel(plan, embed_here, picks, *refs):
    me_ref, shift_ref, stat_ref, expo_ref, label_ref, owned_ref, dlog_ref = refs[:7]
    sinks = refs[7:13]
    terms, out_sem = refs[13:]
    count, width = owned_ref.shape
    me, shift = me_ref[0], shift_ref[0]
    span = stat_ref.shape[2]
    chunks = expo_ref.shape[1] // span
    start = lax.broadcasted_iota(jnp.int32, (count, 1), 0) * width - shift
    touched = (start > -width) & (start < embed_here)
    row = lax.broadcasted_iota(jnp.int32, (count, span), 0)
    mine = stat_ref[pl.ds(me, 1)]
    for k in range(chunks):
        here = slice(k * span, (k + 1) * span)
        tops = stat_ref[:, k : k + 1, :]
        top = jnp.max(tops, axis=0)
        total = jnp.sum(
            stat_ref[:, chunks + k : chunks + k + 1, :] * jnp.exp(tops - top[None]), axis=0
        )
        scale = jnp.exp(mine[0, k : k + 1, :] - top) / total
        hot = (row == label_ref[0:1, here]) & touched
        used = label_ref[1:2, here] > 0
        probs = expo_ref[:, here] * scale
        d_logits = jnp.where(used, jnp.where(hot, probs - 1.0, probs), 0.0).astype(jnp.bfloat16)
        dlog_ref[:, here] = d_logits
        terms[here, :] = contract_rows(d_logits, owned_ref[...]).astype(jnp.bfloat16)
        for b in range(span // picks):
            device = k * (span // picks) + b
            for part, (bits, core_bit) in enumerate(plan):
                relative = device ^ me
                spot = sink_spot(relative, bits)
                across = (relative & core_bit) != 0
                cut = width // len(plan)
                source = terms.at[
                    device * picks : (device + 1) * picks, part * cut : (part + 1) * cut
                ]

                @pl.when(across)
                def _(part=part, source=source, spot=spot):
                    pltpu.make_async_copy(
                        source, sinks[2 * part + 1].at[spot], out_sem.at[2 * part + 1]
                    ).start()

                @pl.when(jnp.logical_not(across))
                def _(part=part, source=source, spot=spot):
                    pltpu.make_async_copy(
                        source, sinks[2 * part].at[spot], out_sem.at[2 * part]
                    ).start()

    for k, sink in enumerate(sinks):
        pltpu.make_async_copy(sink, sink, out_sem.at[k]).wait()


def call_picked(me, shift, stats, expo, labels, owned, plan, picks, embed_here):
    count, width = owned.shape
    devices, rows = stats.shape[0], expo.shape[1]
    vmem = pl.BlockSpec(memory_space=pltpu.VMEM)
    smem = pl.BlockSpec(memory_space=pltpu.SMEM)
    hbm = pl.BlockSpec(memory_space=pl.ANY)
    low = jnp.bfloat16
    return pl.pallas_call(
        functools.partial(picked_kernel, plan, embed_here, picks),
        out_shape=[jax.ShapeDtypeStruct((count, rows), low)]
        + [jax.ShapeDtypeStruct((devices // 2, picks, width // 3), low)] * 6,
        in_specs=[smem, smem, vmem, vmem, vmem, vmem],
        out_specs=[vmem] + [hbm] * 6,
        scratch_shapes=[pltpu.VMEM((rows, width), low), pltpu.SemaphoreType.DMA((6,))],
        compiler_params=pltpu.CompilerParams(vmem_limit_bytes=48 * 2**20),
        cost_estimate=pl.CostEstimate(
            flops=2 * rows * count * width, bytes_accessed=16 * 2**20, transcendentals=0
        ),
    )(me, shift, stats, expo, labels, owned)


def embed_kernel(shift_ref, dlog_ref, picked_ref, out_ref, wide):
    here, width = out_ref.shape
    shift = shift_ref[0]
    turned = contract_cols(picked_ref[...], turn_lanes(shift, width)).astype(jnp.bfloat16)
    wide[...] = dot_nn(dlog_ref[...], turned)
    lane = lax.broadcasted_iota(jnp.int32, (here, width), 1)
    out_ref[...] = jnp.where(lane < width - shift, wide[:here, :], wide[1 : here + 1, :])


def call_embed(shift, dlog, picked, here):
    count, rows = dlog.shape
    width = picked.shape[1]
    vmem = pl.BlockSpec(memory_space=pltpu.VMEM)
    smem = pl.BlockSpec(memory_space=pltpu.SMEM)
    return pl.pallas_call(
        embed_kernel,
        out_shape=jax.ShapeDtypeStruct((here, width), jnp.float32),
        in_specs=[smem, vmem, vmem],
        out_specs=vmem,
        scratch_shapes=[pltpu.VMEM((count, width), jnp.float32)],
        compiler_params=pltpu.CompilerParams(vmem_limit_bytes=40 * 2**20),
        cost_estimate=pl.CostEstimate(
            flops=16 * rows * count * width, bytes_accessed=64 * 2**20, transcendentals=0
        ),
    )(shift, dlog, picked)


def plain_forward(mats_all, vecs_all, block_input, span_lengths):
    seq_here, length, width = block_input.shape
    rows_here = seq_here * length
    heads_count = width // HEAD_DIM
    head_scale = HEAD_DIM ** (-0.5)
    low = jnp.bfloat16
    w_qkv, w_out, w_up, w_down = split_mats(mats_all)
    bias_q, bias_v, bias_out, gain_one, shift_one, bias_up, bias_down, gain_two, shift_two = (
        split_vecs(vecs_all)
    )
    valid = jnp.arange(length)[None, :] < span_lengths[:, None]
    valid_col = valid.reshape(rows_here, 1).astype(jnp.float32)
    tok_rows = (block_input * valid[:, :, None].astype(low)).reshape(rows_here, width)
    qkv_bias = jnp.concatenate([bias_q, jnp.zeros((width,), jnp.float32), bias_v])
    projected = (jnp.dot(tok_rows, w_qkv, preferred_element_type=jnp.float32) + qkv_bias).astype(
        low
    )
    shaped = projected.reshape(seq_here, length, 3, heads_count, HEAD_DIM)
    queries = shaped[:, :, 0]
    key_rows = shaped[:, :, 1]
    value_rows = shaped[:, :, 2]
    key_valid = valid[:, None, None, :]

    def make_scores():
        raw = (
            jnp.einsum("sqhd,skhd->shqk", queries, key_rows, preferred_element_type=jnp.float32)
            * head_scale
        )
        return jnp.where(key_valid, raw, -1e30)

    scores = make_scores()
    row_max = jnp.max(scores, axis=-1, keepdims=True)
    expo_vals = jnp.exp(scores - row_max)
    row_sum = jnp.sum(expo_vals, axis=-1, keepdims=True)
    row_lse = row_max + jnp.log(row_sum)
    attn_probs = (expo_vals / row_sum).astype(low)
    attended = (
        jnp.einsum("shqk,skhd->sqhd", attn_probs, value_rows, preferred_element_type=jnp.float32)
        .reshape(rows_here, width)
        .astype(low)
    )
    branch = jnp.dot(attended, w_out, preferred_element_type=jnp.float32) + bias_out
    normed_one, inverse_one = center_scale(tok_rows.astype(jnp.float32) + branch)
    hidden_one = normed_one * gain_one + shift_one
    hidden_low = hidden_one.astype(low)
    pre_act = jnp.dot(hidden_low, w_up, preferred_element_type=jnp.float32) + bias_up
    act_low = jax.nn.gelu(pre_act, approximate=False).astype(low)
    ffn_out = jnp.dot(act_low, w_down, preferred_element_type=jnp.float32) + bias_down
    normed_two, inverse_two = center_scale(hidden_one + ffn_out)
    output = (normed_two * gain_two + shift_two) * valid_col

    def plain_backward(d_output):
        d_gain_two = jnp.sum(d_output * normed_two, axis=0)
        d_shift_two = jnp.sum(d_output, axis=0)
        d_resid_two = norm_back(d_output * gain_two, normed_two, inverse_two)
        d_ffn = d_resid_two.astype(low)
        d_bias_down = jnp.sum(d_ffn.astype(jnp.float32), axis=0)
        d_w_down = contract_rows(act_low, d_ffn)
        d_act = contract_cols(d_ffn, w_down)
        d_pre = (d_act * gelu_slope(pre_act)).astype(low)
        d_bias_up = jnp.sum(d_pre.astype(jnp.float32), axis=0)
        d_w_up = contract_rows(hidden_low, d_pre)
        d_hidden = contract_cols(d_pre, w_up) + d_resid_two
        d_gain_one = jnp.sum(d_hidden * normed_one, axis=0)
        d_shift_one = jnp.sum(d_hidden, axis=0)
        d_resid_one = norm_back(d_hidden * gain_one, normed_one, inverse_one)
        d_branch = d_resid_one.astype(low)
        d_bias_out = jnp.sum(d_branch.astype(jnp.float32), axis=0)
        d_w_out = contract_rows(attended, d_branch)
        d_attended = (
            contract_cols(d_branch, w_out).astype(low).reshape(seq_here, length, heads_count, HEAD_DIM)
        )
        probs_again = jnp.exp(make_scores() - row_lse)
        probs_low = probs_again.astype(low)
        d_probs = jnp.einsum(
            "sqhd,skhd->shqk", d_attended, value_rows, preferred_element_type=jnp.float32
        )
        d_values = jnp.einsum(
            "shqk,sqhd->skhd", probs_low, d_attended, preferred_element_type=jnp.float32
        )
        row_delta = jnp.sum(d_probs * probs_again, axis=-1, keepdims=True)
        d_scores = (probs_again * (d_probs - row_delta)).astype(low)
        d_queries = (
            jnp.einsum("shqk,skhd->sqhd", d_scores, key_rows, preferred_element_type=jnp.float32)
            * head_scale
        )
        d_keys = (
            jnp.einsum("shqk,sqhd->skhd", d_scores, queries, preferred_element_type=jnp.float32)
            * head_scale
        )
        d_qkv = jnp.concatenate(
            [
                d_queries.reshape(rows_here, width),
                d_keys.reshape(rows_here, width),
                d_values.reshape(rows_here, width),
            ],
            axis=1,
        ).astype(low)
        d_qkv_float = d_qkv.astype(jnp.float32)
        d_bias_q = jnp.sum(d_qkv_float[:, :width], axis=0)
        d_bias_v = jnp.sum(d_qkv_float[:, 2 * width :], axis=0)
        d_w_qkv = contract_rows(tok_rows, d_qkv)
        grad_input = ((contract_cols(d_qkv, w_qkv) + d_resid_one) * valid_col).reshape(
            seq_here, length, width
        )
        d_mats = jnp.concatenate(
            [
                piece.astype(low).reshape(-1, width)
                for piece in (d_w_qkv, d_w_out, d_w_up, d_w_down)
            ]
        )
        d_vecs = jnp.concatenate(
            [
                d_bias_q,
                d_bias_v,
                d_bias_out,
                d_gain_one,
                d_shift_one,
                d_bias_up,
                d_bias_down,
                d_gain_two,
                d_shift_two,
            ]
        )
        return grad_input, d_mats, d_vecs

    return output, plain_backward


def on_device(
    names,
    core,
    block_input,
    span_lengths,
    mlm_positions,
    mlm_labels,
    span_pairs,
    layer_mats,
    vectors,
    embedding,
    mom1_mats,
    mom2_mats,
    mom1_vecs,
    mom2_vecs,
    mom1_embed,
    mom2_embed,
):
    seq_here, length, width = block_input.shape
    rows_here = seq_here * length
    devices = 2 ** len(names)
    me = lax.axis_index(names)
    orders = bit_orders(names, core)
    slots = mlm_positions.shape[1]
    picks_here = seq_here * slots
    low = jnp.bfloat16

    third = layer_mats.shape[0] // width // 3
    by_kernel = third % 16 == 0
    vec_here = vectors.shape[0]
    mats_low = layer_mats.astype(low).reshape(3, third, width)

    def pad_row(row):
        return jnp.pad(row, (0, width - row.shape[0])).astype(low)[None]

    labels_flat = mlm_labels.reshape(-1)
    small = jnp.concatenate(
        [
            pad_row(vectors.astype(low)),
            pad_row(labels_flat // 256),
            pad_row(labels_flat % 256),
            pad_row(jnp.concatenate([span_pairs // 256, span_pairs % 256, span_lengths // 4])),
            embedding[-width:].astype(low)[None],
            embedding[:width].astype(low)[None],
            jnp.zeros((2, width), low),
        ]
    )
    small_all = lax.all_to_all(
        jnp.broadcast_to(small, (devices,) + small.shape), names, 0, 0, tiled=True
    )
    embed_here = embedding.shape[0]
    shifted_rows = -(-embed_here // width)
    over = shifted_rows * width - embed_here
    shift = (me * (embed_here % width)) % width
    first_row = me * (embed_here // width) + (me * (embed_here % width)) // width
    shifted = jnp.pad(embedding.astype(low), (0, over)).reshape(shifted_rows, width)
    from_left = lax.dynamic_index_in_dim(small_all[:, 4], (me + devices - 1) % devices, 0, False)
    from_right = lax.dynamic_index_in_dim(small_all[:, 5], (me + 1) % devices, 0, False)
    right_rows = jnp.pad(from_right, (width - over, over)).reshape(2, width)
    vec_rows = small_all[:, 0, :vec_here].reshape(-1).astype(jnp.float32).reshape(-1, width)
    labels_all = (
        small_all[:, 1, :picks_here].astype(jnp.int32) * 256
        + small_all[:, 2, :picks_here].astype(jnp.int32)
    ).reshape(-1)
    ints_all = small_all[:, 3, : 3 * seq_here].astype(jnp.int32)
    pairs_all = (ints_all[:, :seq_here] * 256 + ints_all[:, seq_here : 2 * seq_here]).reshape(-1)
    quarter_all = ints_all[:, 2 * seq_here :].reshape(-1)
    row_of = labels_all - first_row
    used = (jnp.arange(slots)[None, :] < quarter_all[:, None]).reshape(-1)
    seq_start = jnp.arange(seq_here, dtype=jnp.int32) * length

    def span_terms(cls_all):
        span_scale = 2.0 / math.sqrt(width)
        columns = jnp.arange(cls_all.shape[0])
        sims = contract_cols(cls_all, cls_all) * span_scale
        sims = jnp.where(columns[None, :] == columns[:, None], -1e30, sims)
        partner_hot = (columns[None, :] == pairs_all[:, None]).astype(jnp.float32)
        d_sims = (jax.nn.softmax(sims, axis=-1) - partner_hot).astype(low)
        mine = me * seq_here
        d_sims_rows = lax.dynamic_slice_in_dim(d_sims, mine, seq_here, 0)
        d_sims_cols = lax.dynamic_slice_in_dim(d_sims, mine, seq_here, 1)
        return (
            jnp.dot(d_sims_rows, cls_all, preferred_element_type=jnp.float32)
            + contract_rows(d_sims_cols, cls_all)
        ) * span_scale

    step_float = float(ADAM_STEP)
    cut = width // 3
    columns = [slice(k * cut, (k + 1) * cut) for k in range(3)]
    back_orders = [order[::-1] for order in orders]
    if by_kernel:
        lone = me.astype(jnp.int32).reshape(1)
        lone_shift = shift.astype(jnp.int32).reshape(1)
        tok_rows = block_input.reshape(rows_here, width)
        head_rows = picks_here + 16
        places = jnp.concatenate(
            [
                (mlm_positions + seq_start[:, None]).reshape(-1),
                seq_start,
                jnp.full((16 - seq_here,), -1, jnp.int32),
            ]
        )
        ends = jnp.pad(
            jnp.concatenate([from_left[None], right_rows]).astype(jnp.float32), ((0, 5), (0, 0))
        )
        table_rows = -(-(shifted_rows + 1) // 16) * 16
        labels = jnp.pad(
            jnp.stack([row_of, used.astype(jnp.int32)]).astype(jnp.int32), ((0, 6), (0, 0))
        )

        def prepare(shifted, ends, vec_rows, labels):
            table, owned = call_table(lone_shift, shifted, ends, table_rows, embed_here)
            return table, owned, vec_rows, labels

        gathered, (table, owned, vec_rows, labels) = gather_relative(
            mats_low, orders, names, (shifted, ends, vec_rows, labels), prepare
        )
        heads, *saved = call_forward(
            lone, span_lengths, places[:, None], tok_rows, vec_rows, gathered, seq_here
        )
        heads_all, _ = gather_relative([heads[:, c] for c in columns], orders, names)
        picked, cls_rows, expo, stats = call_logits(
            lone, lone_shift, table, heads_all, picks_here, embed_here, devices
        )
        stats = lax.all_to_all(stats, names, 0, 0, tiled=True)
        plan = tuple(
            (tuple(device_mask(name, names) for name in order[1:]), device_mask(order[0], names))
            for order in back_orders
        )
        d_logits, *sinks = call_picked(
            lone, lone_shift, stats, expo, labels, owned, plan, picks_here, embed_here
        )
        d_cls = span_terms(cls_rows[:, :seq_here].reshape(-1, width))
        d_parts, _ = reduce_relative(sinks[0::2], sinks[1::2], back_orders, ())
        top = jnp.concatenate(
            [jnp.concatenate(d_parts, axis=1), jnp.pad(d_cls, ((0, 16 - seq_here), (0, 0)))]
        )
        grad_input, d_vecs, *sinks = call_backward(
            lone, span_lengths, places[None], tok_rows, vec_rows, top, saved, plan, third, seq_here
        )
        grad_input = grad_input.reshape(seq_here, length, width)
        summed, (d_logits, picked, d_vecs) = reduce_relative(
            sinks[0::2], sinks[1::2], back_orders, (d_logits, picked, d_vecs)
        )
        grad_embed = call_embed(lone_shift, d_logits, picked, shifted_rows)
    else:
        same_row = (jnp.arange(width) < width - shift)[None, :]
        tall = jnp.concatenate([from_left[None], shifted, jnp.zeros((1, width), low)])
        tall = tall.at[shifted_rows : shifted_rows + 2].add(right_rows)
        lanes = jnp.arange(width)
        turn = ((lanes[:, None] + shift) % width == lanes[None, :]).astype(low)
        rolled = jnp.where(same_row, tall[1:], tall[:-1])
        table = jnp.dot(rolled, turn, preferred_element_type=jnp.float32).astype(low)
        row_start = jnp.arange(shifted_rows + 1) * width - shift
        owned = (row_start >= 0) & (row_start < embed_here)
        touched = (row_start + width > 0) & (row_start < embed_here)
        gathered = [gather_bits(mats_low[k], orders[k], names) for k in range(3)]
        mats_all = jnp.stack(gathered, axis=1).reshape(-1)
        output, plain_backward = plain_forward(
            mats_all, vec_rows.reshape(-1), block_input, span_lengths
        )
        output_seq = output.reshape(seq_here, length, width)
        picked_here = jnp.take_along_axis(output_seq, mlm_positions[:, :, None], axis=1)
        heads = jnp.concatenate([picked_here.reshape(-1, width), output_seq[:, 0, :]]).astype(low)
        heads_all = jnp.concatenate(
            [gather_bits(heads[:, c], order, names) for c, order in zip(columns, orders)], axis=2
        )
        picked = heads_all[:, :picks_here, :].reshape(-1, width)
        logits = contract_cols(picked, table)
        masked = jnp.where(owned[None, :], logits, -jnp.inf)
        part_max = jnp.max(masked, axis=-1)
        part_sum = jnp.sum(jnp.exp(masked - part_max[:, None]), axis=-1)
        full_max = lax.pmax(part_max, names)
        full_sum = lax.psum(part_sum * jnp.exp(part_max - full_max), names)
        hot = row_of[:, None] == jnp.arange(shifted_rows + 1)[None, :]
        probs = jnp.exp(logits - full_max[:, None]) / full_sum[:, None]
        d_logits = jnp.where(
            used[:, None] & touched[None, :], probs - hot.astype(jnp.float32), 0.0
        ).astype(low)
        d_picked = jnp.dot(
            d_logits, jnp.where(owned[:, None], table, 0), preferred_element_type=jnp.float32
        )
        blocks = d_picked.astype(low).reshape(devices, picks_here, width)
        d_picked = jnp.concatenate(
            [
                reduce_bits(blocks[:, :, c], order, names)
                for c, order in zip(columns, back_orders)
            ],
            axis=1,
        ).astype(jnp.float32)
        select = (mlm_positions[:, :, None] == jnp.arange(length)[None, None, :]).astype(
            jnp.float32
        )
        d_output_seq = jnp.einsum(
            "gor,gon->grn",
            select,
            d_picked.reshape(seq_here, slots, width),
            precision=lax.Precision.HIGHEST,
        )
        d_cls = span_terms(heads_all[:, picks_here:, :].reshape(-1, width))
        d_output_seq = d_output_seq.at[:, 0, :].add(d_cls)
        valid = jnp.arange(length)[None, :] < span_lengths[:, None]
        d_output = d_output_seq.reshape(rows_here, width) * valid.reshape(rows_here, 1)
        grad_input, d_mats, d_vecs = plain_backward(d_output)
        d_mats = d_mats.reshape(devices, 3, third, width)
        summed = [
            reduce_bits(d_mats[:, k], back_orders[k], names).astype(jnp.float32) for k in range(3)
        ]
        picked_turned = jnp.dot(picked, turn.T, preferred_element_type=jnp.float32).astype(low)
        d_rolled = contract_rows(d_logits, picked_turned)
        grad_embed = jnp.where(same_row, d_rolled[:-1], d_rolled[1:])
    grad_embed = grad_embed.reshape(-1)[:embed_here]
    grad_mats = jnp.concatenate(summed).reshape(-1)
    vec_terms = jnp.pad(d_vecs.reshape(devices, vec_here), ((0, 0), (0, -vec_here % 128)))
    vec_terms = lax.all_to_all(
        vec_terms.reshape(devices, -1, 128), names, 0, 0, tiled=True
    ).reshape(devices, -1)
    grad_vecs = jnp.sum(vec_terms, axis=0)[:vec_here]
    step_mats = adam_step(layer_mats, grad_mats, mom1_mats, mom2_mats, step_float, decay_rate)
    step_vecs = adam_step(vectors, grad_vecs, mom1_vecs, mom2_vecs, step_float, 0.0)
    step_embed = adam_step(embedding, grad_embed, mom1_embed, mom2_embed, step_float, decay_rate)
    return (grad_input, grad_mats, grad_vecs, grad_embed, step_mats, step_vecs, step_embed)


def solution(mesh):
    fsdp_bits = mesh.shape["fsdp"].bit_length() - 1
    rep_bits = mesh.shape["rep"].bit_length() - 1
    names = tuple(f"f{k}" for k in reversed(range(fsdp_bits)))
    core = names[-1]
    names = names + tuple(f"r{k}" for k in reversed(range(rep_bits)))
    bits = Mesh(mesh.devices.reshape((2,) * len(names)), names)
    seqs = P(names, None, None)
    pairs = P(names, None)
    flat = P(names)
    return jax.shard_map(
        functools.partial(on_device, names, core),
        mesh=bits,
        in_specs=(seqs, flat, pairs, pairs) + (flat,) * 10,
        out_specs=(seqs,) + (flat,) * 6,
        check_vma=False,
    )
```

```python
import functools
import math

import jax
import jax.numpy as jnp
from jax import lax
from jax.experimental import pallas as pl
from jax.experimental.pallas import tpu as pltpu
from jax.sharding import Mesh, PartitionSpec as P

D = 768
FF = 3072
HEAD_DIM = 64
VOCAB = 30522
ADAM_STEP = 10


norm_eps = 1e-12
beta_one = 0.9
beta_two = 0.999
adam_eps = 1e-06
decay_rate = 0.01


def split_mats(flat):
    first = 3 * D * D
    second = first + D * D
    third = second + D * FF
    return (
        flat[:first].reshape(D, 3 * D),
        flat[first:second].reshape(D, D),
        flat[second:third].reshape(D, FF),
        flat[third:].reshape(FF, D),
    )


def split_vecs(flat):
    widths_list = [D, D, D, D, D, FF, D, D, D]
    pieces = []
    offset = 0
    for piece_width in widths_list:
        pieces.append(flat[offset : offset + piece_width].astype(jnp.float32))
        offset = offset + piece_width
    return pieces


def center_scale(resid):
    center = resid - jnp.mean(resid, axis=-1, keepdims=True)
    inverse = lax.rsqrt(jnp.mean(center * center, axis=-1, keepdims=True) + norm_eps)
    return (center * inverse, inverse)


def norm_back(d_normed, normed, inverse):
    return inverse * (
        d_normed
        - jnp.mean(d_normed, axis=-1, keepdims=True)
        - normed * jnp.mean(d_normed * normed, axis=-1, keepdims=True)
    )


def gelu_slope(value):
    return (
        0.5 * (1.0 + lax.erf(value * 0.7071067811865476))
        + value * jnp.exp(-0.5 * value * value) * 0.3989422804014327
    )


def contract_rows(left, right):
    return lax.dot_general(
        left, right, (((0,), (0,)), ((), ())), preferred_element_type=jnp.float32
    )


def contract_cols(left, right):
    return lax.dot_general(
        left, right, (((1,), (1,)), ((), ())), preferred_element_type=jnp.float32
    )


def adam_step(weight, grad, first, second, step_float, decay):
    first_new = beta_one * first + (1.0 - beta_one) * grad
    second_new = beta_two * second + (1.0 - beta_two) * grad * grad
    first_hat = first_new / (1.0 - beta_one**step_float)
    second_hat = second_new / (1.0 - beta_two**step_float)
    return first_hat / (jnp.sqrt(second_hat) + adam_eps) + decay * weight


def flip(value, name):
    return lax.ppermute(value, name, [(0, 1), (1, 0)])


def gather_bits(shard, order, names):
    grown = shard
    for name in order:
        other = flip(grown, name)
        first = lax.axis_index(name) == 0
        grown = jnp.stack([jnp.where(first, grown, other), jnp.where(first, other, grown)])
    axes = list(reversed(order))
    rank = len(axes)
    turn = [axes.index(name) for name in names] + list(range(rank, grown.ndim))
    return grown.transpose(turn).reshape((2**rank,) + shard.shape)


def reduce_bits(blocks, order, names):
    left = list(names)
    held = blocks.reshape((2,) * len(left) + blocks.shape[1:])
    for name in order:
        axis = left.index(name)
        here = lax.axis_index(name)
        send = lax.dynamic_index_in_dim(held, 1 - here, axis, keepdims=False)
        keep = lax.dynamic_index_in_dim(held, here, axis, keepdims=False)
        other = flip(send, name)
        held = (keep.astype(jnp.float32) + other.astype(jnp.float32)).astype(blocks.dtype)
        left.remove(name)
    return held


def bit_orders(names, core):
    outer = [name for name in names if name != core]
    count = len(outer)
    if count == 4:
        picks = ((0, 3, 2, 1), (0, 2, 1, 3), (0, 1, 3, 2))
        return [[outer[k] for k in pick] + [core] for pick in picks]
    step = max(1, count // 3)
    return [outer[step * k :] + outer[: step * k] + [core] for k in range(3)]


def device_mask(name, names):
    return 1 << (len(names) - 1 - names.index(name))


def gather_relative(shards, orders, names, early=(), work=None):
    held = []
    for shard, order in zip(shards, orders):
        grown, masks = shard[None], [0]
        for name in order[:-2]:
            grown = lax.optimization_barrier(jnp.concatenate([grown, flip(grown, name)]))
            masks = masks + [mask | device_mask(name, names) for mask in masks]
        held.append((grown, masks))
    grown_all = [grown for grown, _ in held]
    others = [flip(grown, order[-2]) for grown, order in zip(grown_all, orders)]
    if work is not None:
        late, early = lax.optimization_barrier((grown_all, early))
        grown_all, early = lax.optimization_barrier((late, work(*early)))
    gathered = []
    for grown, other, (_, masks), order in zip(grown_all, others, held, orders):
        bit = device_mask(order[-2], names)
        pieces = [(grown, masks), (other, [mask | bit for mask in masks])]
        bit = device_mask(order[-1], names)
        pieces = pieces + [
            (flip(piece, order[-1]), [mask | bit for mask in own]) for piece, own in pieces
        ]
        gathered.append(pieces)
    return gathered, early


def add_terms(terms):
    total = terms[0].astype(jnp.float32)
    for term in terms[1:]:
        total = total + term.astype(jnp.float32)
    return total


def reduce_relative(keeps, sends, orders, state=None, works=()):
    works = dict(works)
    sends = list(sends)
    terms_all = [[keep] for keep in keeps]
    for step in range(len(orders[0])):
        for k, order in enumerate(orders):
            half = terms_all[k][0].shape[0] // 2
            if step == 0:
                urgent, rest = (flip(send, order[step]) for send in sends[k])
            else:
                other = flip(sends[k], order[step])
                urgent, rest = other[half:], other[:half]
            if half:
                upper = [term[half:] for term in terms_all[k]] + [urgent]
                sends[k] = add_terms(upper).astype(urgent.dtype)
                terms_all[k] = [term[:half] for term in terms_all[k]] + [rest]
            else:
                terms_all[k] = terms_all[k] + [urgent]
        if step in works:
            sends[-1], state = lax.optimization_barrier((sends[-1], state))
            state = works[step](state)
    return [add_terms(terms)[0] for terms in terms_all], state


def dot_nn(left, right):
    return lax.dot_general(
        left, right, (((1,), (0,)), ((), ())), preferred_element_type=jnp.float32
    )


def interleave(count, rows):
    span = rows // count
    to = lax.broadcasted_iota(jnp.int32, (rows, rows), 0)
    source = lax.broadcasted_iota(jnp.int32, (rows, rows), 1)
    return (source == count * lax.rem(to, span) + lax.div(to, span)).astype(jnp.bfloat16)


def deinterleave(count, rows):
    span = rows // count
    source = lax.broadcasted_iota(jnp.int32, (rows, rows), 1)
    to = lax.broadcasted_iota(jnp.int32, (rows, rows), 0)
    return (to == count * lax.rem(source, span) + lax.div(source, span)).astype(jnp.bfloat16)


def valid_rows(len_ref, rows, seq_here):
    length = rows // seq_here
    row = lax.broadcasted_iota(jnp.int32, (rows, 1), 0)
    valid = jnp.zeros((rows, 1), jnp.float32)
    for seq in range(seq_here):
        inside = (row >= seq * length) & (row < seq * length + len_ref[seq])
        valid = jnp.where(inside, 1.0, valid)
    return valid


def stack_pair(value):
    lane = lax.broadcasted_iota(jnp.int32, value.shape, 1)
    zero = jnp.zeros_like(value)
    left = lane < HEAD_DIM
    return jnp.concatenate([jnp.where(left, value, zero), jnp.where(left, zero, value)], axis=0)


def join_pair(stacked):
    half = stacked.shape[0] // 2
    lane = lax.broadcasted_iota(jnp.int32, (half, stacked.shape[1]), 1)
    return jnp.where(lane < HEAD_DIM, stacked[:half], stacked[half:])


def pair_scores(stacked, keys, limit):
    raw = contract_cols(stacked, keys) * HEAD_DIM ** (-0.5)
    column = lax.broadcasted_iota(jnp.int32, raw.shape, 1)
    return jnp.where(column < limit, raw, -1e30)


def center_rows(resid):
    center = resid - jnp.mean(resid, axis=-1, keepdims=True)
    inverse = lax.rsqrt(jnp.mean(center * center, axis=-1, keepdims=True) + norm_eps)
    return center * inverse, inverse


def gelu_phi(value):
    return 0.5 * (1.0 + lax.erf(value * 0.7071067811865476))


def forward_kernel(plan, planes, seq_here, *refs):
    me_ref, len_ref, place_ref, x_ref, vec_ref = refs[:5]
    blocks = refs[5 : 5 + len(plan)]
    heads_ref, wall_ref, qkv_ref, att_ref, n1_ref, pre_ref, n2_ref, stat_ref = refs[
        5 + len(plan) : 13 + len(plan)
    ]
    raw, turned, qkv, att, n1, pre_all, in_sem, out_sem = refs[13 + len(plan) :]
    rows, width = x_ref.shape
    length = rows // seq_here
    pairs = width // (2 * HEAD_DIM)
    up = 4 * width
    me = me_ref[0]
    for first in (True, False):
        for (part, unit, masks), block in zip(plan, blocks):
            for place, mask in enumerate(masks):
                device = me ^ mask
                early = device < planes

                @pl.when(early if first else jnp.logical_not(early))
                def _(device=device, part=part, unit=unit, block=block, place=place, first=first):
                    row = pl.multiple_of((3 * device + part) * unit, 16)
                    pltpu.make_async_copy(
                        block.at[place], raw.at[pl.ds(row, unit)], in_sem.at[0 if first else 1]
                    ).start()

    copies = []

    def save(source, target):
        copy = pltpu.make_async_copy(source, target, out_sem.at[len(copies)])
        copy.start()
        copies.append(copy)

    valid = valid_rows(len_ref, rows, seq_here)
    x = (x_ref[...].astype(jnp.float32) * valid).astype(jnp.bfloat16)
    split3, split4 = interleave(3, 384), interleave(4, 256)
    arrived = raw.at[0 : 3 * width]
    pltpu.make_async_copy(arrived, arrived, in_sem.at[0]).wait()

    for b in range(width // 128):
        block = dot_nn(split3, raw[384 * b : 384 * b + 384, :]).astype(jnp.bfloat16)
        for p in range(3):
            turned[width * p + 128 * b : width * p + 128 * b + 128, :] = block[
                128 * p : 128 * p + 128
            ]
    save(turned.at[0 : 3 * width], wall_ref.at[0 : 3 * width])
    for p, bias in ((0, 0), (1, None), (2, 1)):
        value = dot_nn(x, turned[width * p : width * (p + 1), :])
        if bias is not None:
            value = value + vec_ref[bias : bias + 1, :]
        qkv[:, width * p : width * (p + 1)] = value.astype(jnp.bfloat16)
    save(qkv, qkv_ref)

    stats = jnp.zeros((2 * length, 128), jnp.float32)
    lane = lax.broadcasted_iota(jnp.int32, stats.shape, 1)
    for seq in range(seq_here):
        here = slice(seq * length, (seq + 1) * length)
        for g in range(pairs):
            cols = [slice(width * p + 128 * g, width * p + 128 * g + 128) for p in range(3)]
            query, key, value = (qkv[here, c] for c in cols)
            scores = pair_scores(stack_pair(query), key, len_ref[seq])
            top = jnp.max(scores, axis=-1, keepdims=True)
            expo = jnp.exp(scores - top)
            total = jnp.sum(expo, axis=-1, keepdims=True)
            stats = jnp.where(lane == seq * pairs + g, top + jnp.log(total), stats)
            probs = (expo / total).astype(jnp.bfloat16)
            att[here, 128 * g : 128 * g + 128] = join_pair(dot_nn(probs, value)).astype(
                jnp.bfloat16
            )
    save(att, att_ref)
    arrived = raw.at[3 * width : 3 * up]
    pltpu.make_async_copy(arrived, arrived, in_sem.at[1]).wait()
    save(raw.at[3 * width : up], wall_ref.at[3 * width : up])
    save(raw.at[2 * up : 3 * up], wall_ref.at[2 * up : 3 * up])

    branch = dot_nn(att[...], raw[3 * width : up, :]) + vec_ref[2:3, :]
    for b in range(width // 64):
        block = dot_nn(split4, raw[up + 256 * b : up + 256 * b + 256, :]).astype(jnp.bfloat16)
        for p in range(4):
            row = width * (3 + p) + 64 * b
            turned[row : row + 64, :] = block[64 * p : 64 * p + 64]
    save(turned.at[3 * width : 7 * width], wall_ref.at[up : 2 * up])
    normed, inverse = center_rows(x.astype(jnp.float32) + branch)
    n1[...] = normed
    save(n1, n1_ref)
    stat_one = seq_here * pairs
    hidden = normed * vec_ref[3:4, :] + vec_ref[4:5, :]
    hidden_low = hidden.astype(jnp.bfloat16)
    total = hidden + vec_ref[9:10, :]
    for p in range(4):
        pre = dot_nn(hidden_low, turned[width * (3 + p) : width * (4 + p), :])
        pre = pre + vec_ref[5 + p : 6 + p, :]
        pre_all[p] = pre
        save(pre_all.at[p], pre_ref.at[p])
        act = (pre * gelu_phi(pre)).astype(jnp.bfloat16)
        total = total + dot_nn(act, raw[2 * up + width * p : 2 * up + width * (p + 1), :])
    normed, inverse_two = center_rows(total)
    n2_ref[...] = normed
    wide = lax.broadcasted_iota(jnp.int32, (rows, 128), 1)
    ends = jnp.where(
        wide == stat_one, inverse, jnp.where(wide == stat_one + 1, inverse_two, 0.0)
    )
    stat_ref[0] = stats
    stat_ref[1] = ends
    output = ((normed * vec_ref[10:11, :] + vec_ref[11:12, :]) * valid).astype(jnp.bfloat16)
    spot = lax.broadcasted_iota(jnp.int32, (place_ref.shape[0], rows), 1)
    choose = (spot == place_ref[...]).astype(jnp.bfloat16)
    heads_ref[...] = dot_nn(choose, output).astype(jnp.bfloat16)
    for copy in copies:
        copy.wait()


def send_block(source, sinks, spots, device, part, out_sem):
    spot = spots[3 * device + part]
    half = sinks[0].shape[0]

    def copy(sink, place):
        pltpu.make_async_copy(source, sink.at[place], out_sem).start()

    keep, urgent, rest = sinks[3 * part : 3 * part + 3]
    pl.when(spot < half)(functools.partial(copy, keep, spot))
    pl.when((spot >= half) & (spot < half + half // 2))(
        functools.partial(copy, rest, spot - half)
    )
    pl.when(spot >= half + half // 2)(functools.partial(copy, urgent, spot - half - half // 2))


def sink_shapes(devices, block, dtype):
    half = devices // 2
    return [
        jax.ShapeDtypeStruct((count,) + block, dtype)
        for _ in range(3)
        for count in (half, half // 2, half // 2)
    ]


def wait_sinks(sinks, out_sem):
    for sink in sinks:
        pltpu.make_async_copy(sink, sink, out_sem).wait()


def backward_kernel(unit, seq_here, *refs):
    len_ref, spots, place_ref, x_ref, vec_ref, top_ref = refs[:6]
    wall_ref, qkv_ref, att_ref, n1_ref, pre_ref, n2_ref, stat_ref = refs[6:13]
    gin_ref, dvec_ref = refs[13:15]
    sinks = refs[15:24]
    wall, grads, parts, dqkv, qkv, att, n1, pre_all, in_sem, out_sem = refs[24:]
    rows, width = x_ref.shape
    length = rows // seq_here
    pairs = width // (2 * HEAD_DIM)
    low = jnp.bfloat16
    up = 4 * width
    loads = [
        pltpu.make_async_copy(source, target, in_sem.at[k])
        for k, (source, target) in enumerate(
            (
                (pre_ref, pre_all),
                (wall_ref.at[2 * up : 3 * up], wall.at[2 * up : 3 * up]),
                (n1_ref, n1),
                (wall_ref.at[up : 2 * up], wall.at[up : 2 * up]),
                (att_ref, att),
                (wall_ref.at[3 * width : up], wall.at[3 * width : up]),
                (qkv_ref, qkv),
                (wall_ref.at[0 : 3 * width], wall.at[0 : 3 * width]),
            )
        )
    ]
    for load in loads:
        load.start()

    def emit(first, last):
        for u in range(first // unit, last // unit):
            block = grads.at[u * unit : (u + 1) * unit]
            send_block(block, sinks, spots, u // 3, u % 3, out_sem)

    valid = valid_rows(len_ref, rows, seq_here)
    x = (x_ref[...].astype(jnp.float32) * valid).astype(low)
    stat_one = seq_here * pairs
    wide = lax.broadcasted_iota(jnp.int32, (rows, 128), 1)
    ends = stat_ref[1]
    inverse_one = jnp.sum(jnp.where(wide == stat_one, ends, 0.0), axis=-1, keepdims=True)
    inverse_two = jnp.sum(jnp.where(wide == stat_one + 1, ends, 0.0), axis=-1, keepdims=True)

    spot = lax.broadcasted_iota(jnp.int32, (rows, place_ref.shape[1]), 0)
    choose = (spot == place_ref[...]).astype(jnp.float32)
    d_output = valid * lax.dot_general(
        choose,
        top_ref[...],
        (((1,), (0,)), ((), ())),
        precision=lax.Precision.HIGHEST,
        preferred_element_type=jnp.float32,
    )
    normed = n2_ref[...]

    def sums(row, value):
        dvec_ref[row : row + 1, :] = jnp.sum(value, axis=0, keepdims=True)

    sums(10, d_output * normed)
    sums(11, d_output)
    d_resid = norm_back(d_output * vec_ref[10:11, :], normed, inverse_two)
    d_ffn = d_resid.astype(low)
    sums(9, d_ffn.astype(jnp.float32))
    d_hidden = d_resid
    for load in loads[:4]:
        load.wait()
    normed = n1[...]
    hidden_low = (normed * vec_ref[3:4, :] + vec_ref[4:5, :]).astype(low)
    for p in range(4):
        pre = pre_all[p]
        phi = gelu_phi(pre)
        act = (pre * phi).astype(low)
        down = slice(2 * up + width * p, 2 * up + width * (p + 1))
        grads[down, :] = contract_rows(act, d_ffn).astype(low)
        emit(down.start, down.stop)
        slope = phi + pre * jnp.exp(-0.5 * pre * pre) * 0.3989422804014327
        d_pre = (contract_cols(d_ffn, wall[down, :]) * slope).astype(low)
        sums(5 + p, d_pre.astype(jnp.float32))
        parts[width * p : width * (p + 1), :] = contract_rows(hidden_low, d_pre).astype(low)
        d_hidden = d_hidden + contract_cols(d_pre, wall[up + width * p : up + width * (p + 1), :])
    merge4 = deinterleave(4, 256)
    for b in range(width // 64):
        block = jnp.concatenate(
            [parts[width * p + 64 * b : width * p + 64 * b + 64, :] for p in range(4)], axis=0
        )
        grads[up + 256 * b : up + 256 * b + 256, :] = dot_nn(merge4, block).astype(low)
        if b % 3 == 2:
            emit(up + 256 * (b - 2), up + 256 * (b + 1))

    sums(3, d_hidden * normed)
    sums(4, d_hidden)
    d_resid = norm_back(d_hidden * vec_ref[3:4, :], normed, inverse_one)
    d_branch = d_resid.astype(low)
    sums(2, d_branch.astype(jnp.float32))
    for load in loads[4:]:
        load.wait()
    grads[3 * width : up, :] = contract_rows(att[...], d_branch).astype(low)
    emit(3 * width, up)
    d_att = contract_cols(d_branch, wall[3 * width : up, :]).astype(low)
    lane = lax.broadcasted_iota(jnp.int32, (2 * length, 128), 1)
    stats = stat_ref[0]
    for seq in range(seq_here):
        here = slice(seq * length, (seq + 1) * length)
        for g in range(pairs):
            cols = [slice(width * p + 128 * g, width * p + 128 * g + 128) for p in range(3)]
            query, key, value = (qkv[here, c] for c in cols)
            query = stack_pair(query)
            log_sum = jnp.sum(
                jnp.where(lane == seq * pairs + g, stats, 0.0), axis=-1, keepdims=True
            )
            probs = jnp.exp(pair_scores(query, key, len_ref[seq]) - log_sum)
            d_heads = stack_pair(d_att[here, 128 * g : 128 * g + 128])
            d_probs = contract_cols(d_heads, value)
            dqkv[here, cols[2]] = contract_rows(probs.astype(low), d_heads).astype(low)
            delta = jnp.sum(d_probs * probs, axis=-1, keepdims=True)
            d_scores = (probs * (d_probs - delta)).astype(low)
            scale = HEAD_DIM ** (-0.5)
            dqkv[here, cols[0]] = (join_pair(dot_nn(d_scores, key)) * scale).astype(low)
            dqkv[here, cols[1]] = (contract_rows(d_scores, query) * scale).astype(low)
    sums(0, dqkv[:, :width].astype(jnp.float32))
    sums(1, dqkv[:, 2 * width :].astype(jnp.float32))
    for p in range(3):
        d_part = dqkv[:, width * p : width * (p + 1)]
        parts[width * p : width * (p + 1), :] = contract_rows(x, d_part).astype(low)
    merge3 = deinterleave(3, 384)
    for b in range(width // 128):
        block = jnp.concatenate(
            [parts[width * p + 128 * b : width * p + 128 * b + 128, :] for p in range(3)], axis=0
        )
        grads[384 * b : 384 * b + 384, :] = dot_nn(merge3, block).astype(low)
        if b % 2 == 1:
            emit(384 * (b - 1), 384 * (b + 1))
    total = d_resid
    for p in range(3):
        d_part = dqkv[:, width * p : width * (p + 1)]
        total = total + contract_cols(d_part, wall[width * p : width * (p + 1), :])
    gin_ref[...] = total * valid
    wait_sinks(sinks, out_sem)


def call_forward(me, lengths, places, rows, vecs, gathered, devices, seq_here):
    count, width = rows.shape
    pieces = [(part, piece, masks) for part, own in enumerate(gathered) for piece, masks in own]
    plan = tuple((part, piece.shape[1], tuple(masks)) for part, piece, masks in pieces)
    total = 12 * width
    vmem = pl.BlockSpec(memory_space=pltpu.VMEM)
    smem = pl.BlockSpec(memory_space=pltpu.SMEM)
    hbm = pl.BlockSpec(memory_space=pl.ANY)
    low, full = jnp.bfloat16, jnp.float32
    return pl.pallas_call(
        functools.partial(forward_kernel, plan, devices // 4, seq_here),
        out_shape=[
            jax.ShapeDtypeStruct((places.shape[0], width), low),
            jax.ShapeDtypeStruct((total, width), low),
            jax.ShapeDtypeStruct((count, 3 * width), low),
            jax.ShapeDtypeStruct((count, width), low),
            jax.ShapeDtypeStruct((count, width), full),
            jax.ShapeDtypeStruct((4, count, width), full),
            jax.ShapeDtypeStruct((count, width), full),
            jax.ShapeDtypeStruct((2, count, 128), full),
        ],
        in_specs=[smem, smem, vmem, vmem, vmem] + [hbm] * len(pieces),
        out_specs=[vmem] + [hbm] * 5 + [vmem] * 2,
        scratch_shapes=[
            pltpu.VMEM((total, width), low),
            pltpu.VMEM((7 * width, width), low),
            pltpu.VMEM((count, 3 * width), low),
            pltpu.VMEM((count, width), low),
            pltpu.VMEM((count, width), full),
            pltpu.VMEM((4, count, width), full),
            pltpu.SemaphoreType.DMA((2,)),
            pltpu.SemaphoreType.DMA((11,)),
        ],
        compiler_params=pltpu.CompilerParams(vmem_limit_bytes=58 * 2**20),
        cost_estimate=pl.CostEstimate(
            flops=2 * count * total * width, bytes_accessed=48 * 2**20, transcendentals=0
        ),
    )(me, lengths, places, rows, vecs, *[piece for _, piece, _ in pieces])


def call_backward(lengths, spots, places, rows, vecs, top, saved, unit, seq_here):
    count, width = rows.shape
    total = 12 * width
    vmem = pl.BlockSpec(memory_space=pltpu.VMEM)
    smem = pl.BlockSpec(memory_space=pltpu.SMEM)
    hbm = pl.BlockSpec(memory_space=pl.ANY)
    low, full = jnp.bfloat16, jnp.float32
    return pl.pallas_call(
        functools.partial(backward_kernel, unit, seq_here),
        out_shape=[
            jax.ShapeDtypeStruct((count, width), full),
            jax.ShapeDtypeStruct((12, width), full),
        ]
        + sink_shapes(total // unit // 3, (unit, width), low),
        in_specs=[smem, smem, vmem, vmem, vmem, vmem] + [hbm] * 5 + [vmem] * 2,
        out_specs=[vmem, vmem] + [hbm] * 9,
        scratch_shapes=[
            pltpu.VMEM((total, width), low),
            pltpu.VMEM((total, width), low),
            pltpu.VMEM((4 * width, width), low),
            pltpu.VMEM((count, 3 * width), low),
            pltpu.VMEM((count, 3 * width), low),
            pltpu.VMEM((count, width), low),
            pltpu.VMEM((count, width), full),
            pltpu.VMEM((4, count, width), full),
            pltpu.SemaphoreType.DMA((8,)),
            pltpu.SemaphoreType.DMA,
        ],
        compiler_params=pltpu.CompilerParams(vmem_limit_bytes=58 * 2**20),
        cost_estimate=pl.CostEstimate(
            flops=4 * count * total * width, bytes_accessed=48 * 2**20, transcendentals=0
        ),
    )(lengths, spots, places, rows, vecs, top, *saved)


def turn_lanes(shift, width):
    source = lax.broadcasted_iota(jnp.int32, (width, width), 0) + shift
    source = jnp.where(source >= width, source - width, source)
    return (source == lax.broadcasted_iota(jnp.int32, (width, width), 1)).astype(jnp.bfloat16)


def table_kernel(
    embed_here, shift_ref, rows_ref, ends_ref, label_ref, table_ref, owned_ref, columns_ref, tall
):
    eye = eye_mask()
    narrow = lax.broadcasted_iota(jnp.int32, (128, 2), 1)
    for k in range(0, columns_ref.shape[0], 128):
        label, used = (to_column(label_ref[row : row + 1, k : k + 128], eye) for row in (0, 1))
        columns_ref[k : k + 128, :] = jnp.where(narrow == 0, label, used)
    count, width = table_ref.shape
    here = rows_ref.shape[0]
    shift = shift_ref[0]
    tall[here:, :] = jnp.zeros((tall.shape[0] - here, width), jnp.float32)
    tall[8 : 8 + here, :] = rows_ref[...].astype(jnp.float32)
    tall[7:8, :] = ends_ref[0:1, :]
    tall[7 + here : 8 + here, :] = tall[7 + here : 8 + here, :] + ends_ref[1:2, :]
    tall[8 + here : 9 + here, :] = ends_ref[2:3, :]
    lane = lax.broadcasted_iota(jnp.int32, (count, width), 1)
    rolled = jnp.where(lane < width - shift, tall[8 : 8 + count, :], tall[7 : 7 + count, :])
    table = dot_nn(rolled.astype(jnp.bfloat16), turn_lanes(shift, width))
    start = lax.broadcasted_iota(jnp.int32, (count, 1), 0) * width - shift
    owned = (start >= 0) & (start < embed_here)
    table_ref[...] = table.astype(jnp.bfloat16)
    owned_ref[...] = jnp.where(owned, table, 0.0).astype(jnp.bfloat16)


def call_table(shift, rows, ends, labels, count, embed_here):
    width = rows.shape[1]
    vmem = pl.BlockSpec(memory_space=pltpu.VMEM)
    smem = pl.BlockSpec(memory_space=pltpu.SMEM)
    return pl.pallas_call(
        functools.partial(table_kernel, embed_here),
        out_shape=[jax.ShapeDtypeStruct((count, width), jnp.bfloat16)] * 2
        + [jax.ShapeDtypeStruct((labels.shape[1], 2), jnp.float32)],
        in_specs=[smem, vmem, vmem, vmem],
        out_specs=[vmem] * 3,
        scratch_shapes=[pltpu.VMEM((count + 16, width), jnp.float32)],
        compiler_params=pltpu.CompilerParams(vmem_limit_bytes=22 * 2**20),
        cost_estimate=pl.CostEstimate(
            flops=32 * count * width * width, bytes_accessed=40 * 2**20, transcendentals=0
        ),
    )(shift, rows, ends, labels)


def eye_mask():
    return lax.broadcasted_iota(jnp.int32, (128, 128), 0) == lax.broadcasted_iota(
        jnp.int32, (128, 128), 1
    )


def to_row(column, eye):
    return jnp.concatenate(
        [
            jnp.sum(jnp.where(eye, column[k : k + 128], 0.0), axis=0, keepdims=True)
            for k in range(0, column.shape[0], 128)
        ],
        axis=1,
    )


def to_column(row, eye):
    return jnp.concatenate(
        [
            jnp.sum(jnp.where(eye, row[:, k : k + 128], 0.0), axis=1, keepdims=True)
            for k in range(0, row.shape[1], 128)
        ],
        axis=0,
    )


def logits_kernel(plan, embed_here, picks, span, *refs):
    me_ref, shift_ref, table_ref = refs[:3]
    blocks = refs[3 : 3 + len(plan)]
    picked_ref, first, expo_ref, stat_ref, picked, expo_all, in_sem, out_sem = refs[3 + len(plan) :]
    count, width = table_ref.shape
    me, shift = me_ref[0], shift_ref[0]
    extra = first.shape[1]
    for (part, masks), block in zip(plan, blocks):
        cut = block.shape[2]
        cols = pl.ds(part * cut, cut)
        for place, mask in enumerate(masks):
            device = me ^ mask
            row = pl.multiple_of(device * picks, 16)
            pltpu.make_async_copy(
                block.at[place, pl.ds(0, picks)], picked.at[pl.ds(row, picks), cols], in_sem.at[0]
            ).start()
            pltpu.make_async_copy(
                block.at[place, pl.ds(picks, extra)], first.at[device, :, cols], in_sem.at[1]
            ).start()
    whole = embed_here // width // 128 * 128
    eye = eye_mask()
    pltpu.make_async_copy(first, first, in_sem.at[1]).wait()
    pltpu.make_async_copy(picked, picked, in_sem.at[0]).wait()
    copies = [pltpu.make_async_copy(picked, picked_ref, out_sem.at[0])]
    copies[0].start()
    chunks = picked.shape[0] // span
    step = span // 2
    row_start = lax.broadcasted_iota(jnp.int32, (1, count), 1) * width - shift
    touched = (row_start < embed_here)[:, whole:]
    owned = (row_start >= 0)[:, :128]
    tops, totals = [], []
    for k in range(0, picked.shape[0], step):
        here = slice(k, k + step)
        logits = contract_cols(picked[here, :], table_ref[...])
        logits = jnp.concatenate(
            [logits[:, :whole], jnp.where(touched, logits[:, whole:], -1e30)], axis=1
        )
        top = jnp.max(logits, axis=1, keepdims=True)
        expo = jnp.exp(logits - top)
        expo_all[here, :] = expo
        copies.append(
            pltpu.make_async_copy(
                expo_all.at[here], expo_ref.at[here], out_sem.at[1 + k // step]
            )
        )
        copies[-1].start()
        ends = jnp.where(owned, expo[:, :128], 0.0)
        total = jnp.sum(jnp.concatenate([ends, expo[:, 128:]], axis=1), axis=1, keepdims=True)
        tops.append(to_row(top, eye))
        totals.append(to_row(total, eye))
    rows = [
        jnp.concatenate(own[2 * k : 2 * k + 2], axis=1)
        for own in (tops, totals)
        for k in range(chunks)
    ]
    stats = jnp.concatenate(rows, axis=0)
    for device in range(stat_ref.shape[0]):
        stat_ref[device] = stats
    for copy in copies:
        copy.wait()


def call_logits(me, shift, table, gathered, picks, embed_here, devices):
    count, width = table.shape
    pieces = [(part, piece, masks) for part, own in enumerate(gathered) for piece, masks in own]
    plan = tuple((part, tuple(masks)) for part, _, masks in pieces)
    extra = pieces[0][1].shape[1] - picks
    rows = devices * picks
    span = rows // 4
    vmem = pl.BlockSpec(memory_space=pltpu.VMEM)
    smem = pl.BlockSpec(memory_space=pltpu.SMEM)
    hbm = pl.BlockSpec(memory_space=pl.ANY)
    low, full = jnp.bfloat16, jnp.float32
    return pl.pallas_call(
        functools.partial(logits_kernel, plan, embed_here, picks, span),
        out_shape=[
            jax.ShapeDtypeStruct((rows, width), low),
            jax.ShapeDtypeStruct((devices, extra, width), low),
            jax.ShapeDtypeStruct((rows, count), full),
            jax.ShapeDtypeStruct((devices, 8, span), full),
        ],
        in_specs=[smem, smem, vmem] + [hbm] * len(pieces),
        out_specs=[hbm, vmem, hbm, vmem],
        scratch_shapes=[
            pltpu.VMEM((rows, width), low),
            pltpu.VMEM((rows, count), full),
            pltpu.SemaphoreType.DMA((2,)),
            pltpu.SemaphoreType.DMA((9,)),
        ],
        compiler_params=pltpu.CompilerParams(vmem_limit_bytes=58 * 2**20),
        cost_estimate=pl.CostEstimate(
            flops=2 * rows * count * width, bytes_accessed=16 * 2**20, transcendentals=0
        ),
    )(me, shift, table, *[piece for _, piece, _ in pieces])


def mix_kernel(expo_ref, column_ref, owned_ref, mix_ref, row_ref, own_ref):
    rows, count = expo_ref.shape
    step = min(rows, 256)
    lane = lax.broadcasted_iota(jnp.int32, (step, count), 1)
    for k in range(0, rows, step):
        here = slice(k, k + step)
        expo = expo_ref[here, :]
        hot = lane == column_ref[here, 0:1].astype(jnp.int32)
        own_ref[here, :] = jnp.sum(jnp.where(hot, expo, 0.0), axis=1, keepdims=True)
        others = jnp.where(hot, 0.0, expo).astype(jnp.bfloat16)
        mix_ref[here, :] = dot_nn(others, owned_ref[...]).astype(jnp.bfloat16)
        row_ref[here, :] = dot_nn(hot.astype(jnp.bfloat16), owned_ref[...]).astype(jnp.bfloat16)


def call_mix(expo, columns, owned):
    rows, count = expo.shape
    width = owned.shape[1]
    low = jnp.bfloat16
    step = rows // 4

    def tile(lanes):
        return pl.BlockSpec((step, lanes), lambda k: (k, 0))

    return pl.pallas_call(
        mix_kernel,
        grid=(4,),
        out_shape=[
            jax.ShapeDtypeStruct((rows, width), low),
            jax.ShapeDtypeStruct((rows, width), low),
            jax.ShapeDtypeStruct((rows, 1), jnp.float32),
        ],
        in_specs=[tile(count), tile(2), pl.BlockSpec((count, width), lambda k: (0, 0))],
        out_specs=[tile(width), tile(width), tile(1)],
        compiler_params=pltpu.CompilerParams(vmem_limit_bytes=48 * 2**20),
        cost_estimate=pl.CostEstimate(
            flops=16 * rows * count * width, bytes_accessed=64 * 2**20, transcendentals=0
        ),
    )(expo, columns, owned)


def terms_kernel(picks, *refs):
    me_ref, spots, stat_ref, mix_ref, row_ref, own_ref, column_ref, scale_ref = refs[:8]
    sinks = refs[8:17]
    terms, out_sem = refs[17:]
    span, width = mix_ref.shape
    chunks = terms.shape[0]
    chunk = pl.program_id(0)
    mine = stat_ref[pl.ds(me_ref[0], 1), pl.ds(chunk, 1), :][0]
    tops = stat_ref[:, pl.ds(chunk, 1), :]
    top = jnp.max(tops, axis=0)
    totals = stat_ref[:, pl.ds(chunks + chunk, 1), :]
    total = jnp.sum(totals * jnp.exp(tops - top[None]), axis=0)
    scale = to_column(jnp.exp(mine - top) / total, eye_mask())
    scale_ref[...] = scale
    used = column_ref[:, 1:2]
    label = (own_ref[...] * scale - 1.0).astype(jnp.bfloat16).astype(jnp.float32)
    terms[chunk] = (
        mix_ref[...].astype(jnp.float32) * (scale * used)
        + row_ref[...].astype(jnp.float32) * (label * used)
    ).astype(jnp.bfloat16)
    cut = width // 3
    for b in range(span // picks):
        for part in range(3):
            source = terms.at[
                chunk, b * picks : (b + 1) * picks, part * cut : (part + 1) * cut
            ]
            send_block(source, sinks, spots, chunk * (span // picks) + b, part, out_sem)

    @pl.when(chunk == chunks - 1)
    def _():
        wait_sinks(sinks, out_sem)


def call_terms(me, spots, stats, mix, label_rows, own, columns, picks):
    rows, width = mix.shape
    devices, _, span = stats.shape
    smem = pl.BlockSpec(memory_space=pltpu.SMEM)
    hbm = pl.BlockSpec(memory_space=pl.ANY)
    low = jnp.bfloat16

    def tile(lanes):
        return pl.BlockSpec((span, lanes), lambda k: (k, 0))

    return pl.pallas_call(
        functools.partial(terms_kernel, picks),
        grid=(rows // span,),
        out_shape=[jax.ShapeDtypeStruct((rows, 1), jnp.float32)]
        + sink_shapes(devices, (picks, width // 3), low),
        in_specs=[
            smem,
            smem,
            pl.BlockSpec(stats.shape, lambda k: (0, 0, 0)),
            tile(width),
            tile(width),
            tile(1),
            tile(2),
        ],
        out_specs=[tile(1)] + [hbm] * 9,
        scratch_shapes=[
            pltpu.VMEM((rows // span, span, width), low),
            pltpu.SemaphoreType.DMA,
        ],
        compiler_params=pltpu.CompilerParams(vmem_limit_bytes=48 * 2**20),
        cost_estimate=pl.CostEstimate(
            flops=8 * rows * width, bytes_accessed=10 * 2**20, transcendentals=0
        ),
    )(me, spots, stats, mix, label_rows, own, columns)


def embed_kernel(shift_ref, expo_ref, scale_ref, column_ref, picked_ref, out_ref, wide):
    here, width = out_ref.shape
    rows, count = expo_ref.shape
    shift = shift_ref[0]
    chunk = pl.program_id(0)
    probs = expo_ref[...] * scale_ref[...]
    lane = lax.broadcasted_iota(jnp.int32, (rows, count), 1)
    hot = lane == column_ref[:, 0:1].astype(jnp.int32)
    terms = (jnp.where(hot, probs - 1.0, probs) * column_ref[:, 1:2]).astype(jnp.bfloat16)
    turned = contract_cols(picked_ref[...], turn_lanes(shift, width)).astype(jnp.bfloat16)
    total = contract_rows(terms, turned)

    @pl.when(chunk == 0)
    def _():
        wide[...] = total

    @pl.when(chunk > 0)
    def _():
        wide[...] = wide[...] + total

    @pl.when(chunk == pl.num_programs(0) - 1)
    def _():
        lane = lax.broadcasted_iota(jnp.int32, (here, width), 1)
        out_ref[...] = jnp.where(lane < width - shift, wide[:here, :], wide[1 : here + 1, :])


def call_embed(shift, expo, scale, columns, picked, here):
    rows, count = expo.shape
    width = picked.shape[1]
    smem = pl.BlockSpec(memory_space=pltpu.SMEM)
    step = rows // 8

    def tile(lanes):
        return pl.BlockSpec((step, lanes), lambda k: (k, 0))

    return pl.pallas_call(
        embed_kernel,
        grid=(8,),
        out_shape=jax.ShapeDtypeStruct((here, width), jnp.float32),
        in_specs=[smem, tile(count), tile(1), tile(2), tile(width)],
        out_specs=pl.BlockSpec((here, width), lambda k: (0, 0)),
        scratch_shapes=[pltpu.VMEM((count, width), jnp.float32)],
        compiler_params=pltpu.CompilerParams(vmem_limit_bytes=20 * 2**20),
        cost_estimate=pl.CostEstimate(
            flops=16 * rows * count * width, bytes_accessed=64 * 2**20, transcendentals=0
        ),
    )(shift, expo, scale, columns, picked)


def plain_forward(mats_all, vecs_all, block_input, span_lengths):
    seq_here, length, width = block_input.shape
    rows_here = seq_here * length
    heads_count = width // HEAD_DIM
    head_scale = HEAD_DIM ** (-0.5)
    low = jnp.bfloat16
    w_qkv, w_out, w_up, w_down = split_mats(mats_all)
    bias_q, bias_v, bias_out, gain_one, shift_one, bias_up, bias_down, gain_two, shift_two = (
        split_vecs(vecs_all)
    )
    valid = jnp.arange(length)[None, :] < span_lengths[:, None]
    valid_col = valid.reshape(rows_here, 1).astype(jnp.float32)
    tok_rows = (block_input * valid[:, :, None].astype(low)).reshape(rows_here, width)
    qkv_bias = jnp.concatenate([bias_q, jnp.zeros((width,), jnp.float32), bias_v])
    projected = (jnp.dot(tok_rows, w_qkv, preferred_element_type=jnp.float32) + qkv_bias).astype(
        low
    )
    shaped = projected.reshape(seq_here, length, 3, heads_count, HEAD_DIM)
    queries = shaped[:, :, 0]
    key_rows = shaped[:, :, 1]
    value_rows = shaped[:, :, 2]
    key_valid = valid[:, None, None, :]

    def make_scores():
        raw = (
            jnp.einsum("sqhd,skhd->shqk", queries, key_rows, preferred_element_type=jnp.float32)
            * head_scale
        )
        return jnp.where(key_valid, raw, -1e30)

    scores = make_scores()
    row_max = jnp.max(scores, axis=-1, keepdims=True)
    expo_vals = jnp.exp(scores - row_max)
    row_sum = jnp.sum(expo_vals, axis=-1, keepdims=True)
    row_lse = row_max + jnp.log(row_sum)
    attn_probs = (expo_vals / row_sum).astype(low)
    attended = (
        jnp.einsum("shqk,skhd->sqhd", attn_probs, value_rows, preferred_element_type=jnp.float32)
        .reshape(rows_here, width)
        .astype(low)
    )
    branch = jnp.dot(attended, w_out, preferred_element_type=jnp.float32) + bias_out
    normed_one, inverse_one = center_scale(tok_rows.astype(jnp.float32) + branch)
    hidden_one = normed_one * gain_one + shift_one
    hidden_low = hidden_one.astype(low)
    pre_act = jnp.dot(hidden_low, w_up, preferred_element_type=jnp.float32) + bias_up
    act_low = jax.nn.gelu(pre_act, approximate=False).astype(low)
    ffn_out = jnp.dot(act_low, w_down, preferred_element_type=jnp.float32) + bias_down
    normed_two, inverse_two = center_scale(hidden_one + ffn_out)
    output = (normed_two * gain_two + shift_two) * valid_col

    def plain_backward(d_output):
        d_gain_two = jnp.sum(d_output * normed_two, axis=0)
        d_shift_two = jnp.sum(d_output, axis=0)
        d_resid_two = norm_back(d_output * gain_two, normed_two, inverse_two)
        d_ffn = d_resid_two.astype(low)
        d_bias_down = jnp.sum(d_ffn.astype(jnp.float32), axis=0)
        d_w_down = contract_rows(act_low, d_ffn)
        d_act = contract_cols(d_ffn, w_down)
        d_pre = (d_act * gelu_slope(pre_act)).astype(low)
        d_bias_up = jnp.sum(d_pre.astype(jnp.float32), axis=0)
        d_w_up = contract_rows(hidden_low, d_pre)
        d_hidden = contract_cols(d_pre, w_up) + d_resid_two
        d_gain_one = jnp.sum(d_hidden * normed_one, axis=0)
        d_shift_one = jnp.sum(d_hidden, axis=0)
        d_resid_one = norm_back(d_hidden * gain_one, normed_one, inverse_one)
        d_branch = d_resid_one.astype(low)
        d_bias_out = jnp.sum(d_branch.astype(jnp.float32), axis=0)
        d_w_out = contract_rows(attended, d_branch)
        d_attended = (
            contract_cols(d_branch, w_out).astype(low).reshape(seq_here, length, heads_count, HEAD_DIM)
        )
        probs_again = jnp.exp(make_scores() - row_lse)
        probs_low = probs_again.astype(low)
        d_probs = jnp.einsum(
            "sqhd,skhd->shqk", d_attended, value_rows, preferred_element_type=jnp.float32
        )
        d_values = jnp.einsum(
            "shqk,sqhd->skhd", probs_low, d_attended, preferred_element_type=jnp.float32
        )
        row_delta = jnp.sum(d_probs * probs_again, axis=-1, keepdims=True)
        d_scores = (probs_again * (d_probs - row_delta)).astype(low)
        d_queries = (
            jnp.einsum("shqk,skhd->sqhd", d_scores, key_rows, preferred_element_type=jnp.float32)
            * head_scale
        )
        d_keys = (
            jnp.einsum("shqk,sqhd->skhd", d_scores, queries, preferred_element_type=jnp.float32)
            * head_scale
        )
        d_qkv = jnp.concatenate(
            [
                d_queries.reshape(rows_here, width),
                d_keys.reshape(rows_here, width),
                d_values.reshape(rows_here, width),
            ],
            axis=1,
        ).astype(low)
        d_qkv_float = d_qkv.astype(jnp.float32)
        d_bias_q = jnp.sum(d_qkv_float[:, :width], axis=0)
        d_bias_v = jnp.sum(d_qkv_float[:, 2 * width :], axis=0)
        d_w_qkv = contract_rows(tok_rows, d_qkv)
        grad_input = ((contract_cols(d_qkv, w_qkv) + d_resid_one) * valid_col).reshape(
            seq_here, length, width
        )
        d_mats = jnp.concatenate(
            [
                piece.astype(low).reshape(-1, width)
                for piece in (d_w_qkv, d_w_out, d_w_up, d_w_down)
            ]
        )
        d_vecs = jnp.concatenate(
            [
                d_bias_q,
                d_bias_v,
                d_bias_out,
                d_gain_one,
                d_shift_one,
                d_bias_up,
                d_bias_down,
                d_gain_two,
                d_shift_two,
            ]
        )
        return grad_input, d_mats, d_vecs

    return output, plain_backward


def on_device(
    names,
    core,
    block_input,
    span_lengths,
    mlm_positions,
    mlm_labels,
    span_pairs,
    layer_mats,
    vectors,
    embedding,
    mom1_mats,
    mom2_mats,
    mom1_vecs,
    mom2_vecs,
    mom1_embed,
    mom2_embed,
):
    seq_here, length, width = block_input.shape
    rows_here = seq_here * length
    devices = 2 ** len(names)
    me = lax.axis_index(names)
    orders = bit_orders(names, core)
    slots = mlm_positions.shape[1]
    picks_here = seq_here * slots
    low = jnp.bfloat16

    third = layer_mats.shape[0] // width // 3
    by_kernel = third % 16 == 0
    vec_here = vectors.shape[0]
    mats_low = layer_mats.astype(low).reshape(3, third, width)

    labels_flat = mlm_labels.reshape(-1)
    common = jnp.concatenate(
        [
            value.astype(low)
            for value in (
                vectors,
                labels_flat // 256,
                labels_flat % 256,
                span_pairs // 256,
                span_pairs % 256,
                span_lengths // 4,
            )
        ]
    )
    ends = [vec_here, picks_here, picks_here, seq_here, seq_here, seq_here]
    common = jnp.pad(common, (0, width - common.shape[0]))
    others = jnp.arange(devices)[:, None]
    right, left = (me + 1) % devices, (me + devices - 1) % devices
    border = jnp.where(
        others == right,
        embedding[-width:].astype(low),
        jnp.where(others == left, embedding[:width].astype(low), jnp.zeros((), low)),
    )
    small = jnp.stack([jnp.broadcast_to(common, border.shape), border], axis=1)
    small_all = lax.all_to_all(small, names, 0, 0, tiled=True)
    starts = [sum(ends[:k]) for k in range(len(ends))]
    vecs_all, labels_high, labels_low, pairs_high, pairs_low, quarter_all = (
        small_all[:, 0, start : start + size] for start, size in zip(starts, ends)
    )

    embed_here = embedding.shape[0]
    shifted_rows = -(-embed_here // width)
    over = shifted_rows * width - embed_here
    shift = (me * (embed_here % width)) % width
    first_row = me * (embed_here // width) + (me * (embed_here % width)) // width

    def table_shard(embedding):
        return jnp.pad(embedding.astype(low), (0, over)).reshape(shifted_rows, width)

    from_left = lax.dynamic_index_in_dim(small_all[:, 1], left, 0, False)
    from_right = lax.dynamic_index_in_dim(small_all[:, 1], right, 0, False)
    right_rows = jnp.pad(from_right, (width - over, over)).reshape(2, width)
    vec_rows = vecs_all.reshape(-1).astype(jnp.float32).reshape(-1, width)

    def whole(high, small):
        return (high.astype(jnp.int32) * 256 + small.astype(jnp.int32)).reshape(-1)

    labels_all = whole(labels_high, labels_low)
    pairs_all = whole(pairs_high, pairs_low)
    quarter_all = quarter_all.astype(jnp.int32).reshape(-1)
    row_of = labels_all - first_row
    used = (jnp.arange(slots)[None, :] < quarter_all[:, None]).reshape(-1)
    seq_start = jnp.arange(seq_here, dtype=jnp.int32) * length

    def span_terms(cls_all):
        span_scale = 2.0 / math.sqrt(width)
        columns = jnp.arange(cls_all.shape[0])
        sims = contract_cols(cls_all, cls_all) * span_scale
        sims = jnp.where(columns[None, :] == columns[:, None], -1e30, sims)
        partner_hot = (columns[None, :] == pairs_all[:, None]).astype(jnp.float32)
        d_sims = (jax.nn.softmax(sims, axis=-1) - partner_hot).astype(low)
        mine = me * seq_here
        d_sims_rows = lax.dynamic_slice_in_dim(d_sims, mine, seq_here, 0)
        d_sims_cols = lax.dynamic_slice_in_dim(d_sims, mine, seq_here, 1)
        return (
            jnp.dot(d_sims_rows, cls_all, preferred_element_type=jnp.float32)
            + contract_rows(d_sims_cols, cls_all)
        ) * span_scale

    step_float = float(ADAM_STEP)

    def embed_step(grad_rows):
        grad = grad_rows.reshape(-1)[:embed_here]
        return grad, adam_step(embedding, grad, mom1_embed, mom2_embed, step_float, decay_rate)

    def sum_vectors(d_vecs):
        terms = d_vecs.reshape(devices, 1, vec_here)
        terms = lax.all_to_all(terms, names, 0, 0, tiled=True)
        return jnp.sum(terms, axis=(0, 1))

    cut = width // 3
    columns = [slice(k * cut, (k + 1) * cut) for k in range(3)]
    back_orders = [order[::-1] for order in orders]
    if by_kernel:
        lone = me.astype(jnp.int32).reshape(1)
        lone_shift = shift.astype(jnp.int32).reshape(1)
        tok_rows = block_input.reshape(rows_here, width)
        relative = jnp.arange(devices, dtype=jnp.int32) ^ me.astype(jnp.int32)
        spots = jnp.stack(
            [
                sum(
                    ((relative & device_mask(name, names)) != 0).astype(jnp.int32)
                    << (len(names) - 1 - k)
                    for k, name in enumerate(order)
                )
                for order in back_orders
            ],
            axis=1,
        ).reshape(-1)
        places = jnp.concatenate(
            [
                (mlm_positions + seq_start[:, None]).reshape(-1),
                seq_start,
                jnp.full((16 - seq_here,), -1, jnp.int32),
            ]
        )
        ends = jnp.pad(
            jnp.concatenate([from_left[None], right_rows]).astype(jnp.float32), ((0, 5), (0, 0))
        )
        table_rows = -(-(shifted_rows + 1) // 128) * 128
        labels = jnp.pad(
            jnp.stack([row_of.astype(jnp.float32), used.astype(jnp.float32)]), ((0, 6), (0, 0))
        )

        def prepare(embedding, ends, labels, *others):
            shifted = table_shard(embedding)
            table = call_table(lone_shift, shifted, ends, labels, table_rows, embed_here)
            return *table, *others

        gathered, (table, owned, columns_all, vec_rows) = gather_relative(
            mats_low, orders, names, (embedding, ends, labels, vec_rows), prepare
        )
        heads, *saved = call_forward(
            lone, span_lengths, places[:, None], tok_rows, vec_rows, gathered, devices, seq_here
        )
        heads_all, _ = gather_relative([heads[:, c] for c in columns], orders, names)
        picked, cls_rows, expo, stats = call_logits(
            lone, lone_shift, table, heads_all, picks_here, embed_here, devices
        )
        stats = lax.all_to_all(stats, names, 0, 0, tiled=True)
        mix, hot_rows, own = call_mix(expo, columns_all, owned)
        scale, *sinks = call_terms(
            lone, spots, stats, mix, hot_rows, own, columns_all, picks_here
        )
        d_cls = span_terms(cls_rows[:, :seq_here].reshape(-1, width))
        d_parts, _ = reduce_relative(
            sinks[0::3], list(zip(sinks[1::3], sinks[2::3])), back_orders
        )
        top = jnp.concatenate(
            [jnp.concatenate(d_parts, axis=1), jnp.pad(d_cls, ((0, 16 - seq_here), (0, 0)))]
        )
        grad_input, d_vecs, *sinks = call_backward(
            span_lengths, spots, places[None], tok_rows, vec_rows, top, saved, third, seq_here
        )
        grad_input = grad_input.reshape(seq_here, length, width)
        def table_grad(state):
            expo, picked, d_vecs = state
            grad_embed = call_embed(
                lone_shift, expo, scale, columns_all, picked, shifted_rows
            )
            grad_embed, d_vecs = lax.optimization_barrier((grad_embed, d_vecs))
            return grad_embed, sum_vectors(d_vecs)

        def table_step(state):
            grad_embed, grad_vecs = state
            return *embed_step(grad_embed), grad_vecs

        summed, (grad_embed, step_embed, grad_vecs) = reduce_relative(
            sinks[0::3],
            list(zip(sinks[1::3], sinks[2::3])),
            back_orders,
            (expo, picked, d_vecs),
            {0: table_grad, len(names) - 2: table_step},
        )
    else:
        same_row = (jnp.arange(width) < width - shift)[None, :]
        tall = jnp.concatenate(
            [from_left[None], table_shard(embedding), jnp.zeros((1, width), low)]
        )
        tall = tall.at[shifted_rows : shifted_rows + 2].add(right_rows)
        lanes = jnp.arange(width)
        turn = ((lanes[:, None] + shift) % width == lanes[None, :]).astype(low)
        rolled = jnp.where(same_row, tall[1:], tall[:-1])
        table = jnp.dot(rolled, turn, preferred_element_type=jnp.float32).astype(low)
        row_start = jnp.arange(shifted_rows + 1) * width - shift
        owned = (row_start >= 0) & (row_start < embed_here)
        touched = (row_start + width > 0) & (row_start < embed_here)
        gathered = [gather_bits(mats_low[k], orders[k], names) for k in range(3)]
        mats_all = jnp.stack(gathered, axis=1).reshape(-1)
        output, plain_backward = plain_forward(
            mats_all, vec_rows.reshape(-1), block_input, span_lengths
        )
        output_seq = output.reshape(seq_here, length, width)
        picked_here = jnp.take_along_axis(output_seq, mlm_positions[:, :, None], axis=1)
        heads = jnp.concatenate([picked_here.reshape(-1, width), output_seq[:, 0, :]]).astype(low)
        heads_all = jnp.concatenate(
            [gather_bits(heads[:, c], order, names) for c, order in zip(columns, orders)], axis=2
        )
        picked = heads_all[:, :picks_here, :].reshape(-1, width)
        logits = contract_cols(picked, table)
        masked = jnp.where(owned[None, :], logits, -jnp.inf)
        part_max = jnp.max(masked, axis=-1)
        part_sum = jnp.sum(jnp.exp(masked - part_max[:, None]), axis=-1)
        full_max = lax.pmax(part_max, names)
        full_sum = lax.psum(part_sum * jnp.exp(part_max - full_max), names)
        hot = row_of[:, None] == jnp.arange(shifted_rows + 1)[None, :]
        probs = jnp.exp(logits - full_max[:, None]) / full_sum[:, None]
        d_logits = jnp.where(
            used[:, None] & touched[None, :], probs - hot.astype(jnp.float32), 0.0
        ).astype(low)
        d_picked = jnp.dot(
            d_logits, jnp.where(owned[:, None], table, 0), preferred_element_type=jnp.float32
        )
        blocks = d_picked.astype(low).reshape(devices, picks_here, width)
        d_picked = jnp.concatenate(
            [
                reduce_bits(blocks[:, :, c], order, names)
                for c, order in zip(columns, back_orders)
            ],
            axis=1,
        ).astype(jnp.float32)
        select = (mlm_positions[:, :, None] == jnp.arange(length)[None, None, :]).astype(
            jnp.float32
        )
        d_output_seq = jnp.einsum(
            "gor,gon->grn",
            select,
            d_picked.reshape(seq_here, slots, width),
            precision=lax.Precision.HIGHEST,
        )
        d_cls = span_terms(heads_all[:, picks_here:, :].reshape(-1, width))
        d_output_seq = d_output_seq.at[:, 0, :].add(d_cls)
        valid = jnp.arange(length)[None, :] < span_lengths[:, None]
        d_output = d_output_seq.reshape(rows_here, width) * valid.reshape(rows_here, 1)
        grad_input, d_mats, d_vecs = plain_backward(d_output)
        d_mats = d_mats.reshape(devices, 3, third, width)
        summed = [
            reduce_bits(d_mats[:, k], back_orders[k], names).astype(jnp.float32) for k in range(3)
        ]
        picked_turned = jnp.dot(picked, turn.T, preferred_element_type=jnp.float32).astype(low)
        d_rolled = contract_rows(d_logits, picked_turned)
        grad_embed, step_embed = embed_step(jnp.where(same_row, d_rolled[:-1], d_rolled[1:]))
        grad_vecs = sum_vectors(d_vecs)
    grad_mats = jnp.concatenate(summed).reshape(-1)
    step_mats = adam_step(layer_mats, grad_mats, mom1_mats, mom2_mats, step_float, decay_rate)
    step_vecs = adam_step(vectors, grad_vecs, mom1_vecs, mom2_vecs, step_float, 0.0)
    return (grad_input, grad_mats, grad_vecs, grad_embed, step_mats, step_vecs, step_embed)


def solution(mesh):
    fsdp_bits = mesh.shape["fsdp"].bit_length() - 1
    rep_bits = mesh.shape["rep"].bit_length() - 1
    names = tuple(f"f{k}" for k in reversed(range(fsdp_bits)))
    core = names[-1]
    names = names + tuple(f"r{k}" for k in reversed(range(rep_bits)))
    bits = Mesh(mesh.devices.reshape((2,) * len(names)), names)
    seqs = P(names, None, None)
    pairs = P(names, None)
    flat = P(names)
    return jax.shard_map(
        functools.partial(on_device, names, core),
        mesh=bits,
        in_specs=(seqs, flat, pairs, pairs) + (flat,) * 10,
        out_specs=(seqs,) + (flat,) * 6,
        check_vma=False,
    )
```

```python
import functools
import math

import jax
import jax.numpy as jnp
from jax import lax
from jax.experimental import pallas as pl
from jax.experimental.pallas import tpu as pltpu
from jax.sharding import Mesh, PartitionSpec as P

D = 768
FF = 3072
HEAD_DIM = 64
VOCAB = 30522
ADAM_STEP = 10


norm_eps = 1e-12
beta_one = 0.9
beta_two = 0.999
adam_eps = 1e-06
decay_rate = 0.01


def split_mats(flat):
    first = 3 * D * D
    second = first + D * D
    third = second + D * FF
    return (
        flat[:first].reshape(D, 3 * D),
        flat[first:second].reshape(D, D),
        flat[second:third].reshape(D, FF),
        flat[third:].reshape(FF, D),
    )


def split_vecs(flat):
    widths_list = [D, D, D, D, D, FF, D, D, D]
    pieces = []
    offset = 0
    for piece_width in widths_list:
        pieces.append(flat[offset : offset + piece_width].astype(jnp.float32))
        offset = offset + piece_width
    return pieces


def center_scale(resid):
    center = resid - jnp.mean(resid, axis=-1, keepdims=True)
    inverse = lax.rsqrt(jnp.mean(center * center, axis=-1, keepdims=True) + norm_eps)
    return (center * inverse, inverse)


def norm_back(d_normed, normed, inverse):
    return inverse * (
        d_normed
        - jnp.mean(d_normed, axis=-1, keepdims=True)
        - normed * jnp.mean(d_normed * normed, axis=-1, keepdims=True)
    )


def gelu_slope(value):
    return (
        0.5 * (1.0 + lax.erf(value * 0.7071067811865476))
        + value * jnp.exp(-0.5 * value * value) * 0.3989422804014327
    )


def contract_rows(left, right):
    return lax.dot_general(
        left, right, (((0,), (0,)), ((), ())), preferred_element_type=jnp.float32
    )


def contract_cols(left, right):
    return lax.dot_general(
        left, right, (((1,), (1,)), ((), ())), preferred_element_type=jnp.float32
    )


def adam_step(weight, grad, first, second, step_float, decay):
    first_new = beta_one * first + (1.0 - beta_one) * grad
    second_new = beta_two * second + (1.0 - beta_two) * grad * grad
    first_hat = first_new / (1.0 - beta_one**step_float)
    second_hat = second_new / (1.0 - beta_two**step_float)
    return first_hat / (jnp.sqrt(second_hat) + adam_eps) + decay * weight


def flip(value, name):
    return lax.ppermute(value, name, [(0, 1), (1, 0)])


def gather_bits(shard, order, names):
    grown = shard
    for name in order:
        other = flip(grown, name)
        first = lax.axis_index(name) == 0
        grown = jnp.stack([jnp.where(first, grown, other), jnp.where(first, other, grown)])
    axes = list(reversed(order))
    rank = len(axes)
    turn = [axes.index(name) for name in names] + list(range(rank, grown.ndim))
    return grown.transpose(turn).reshape((2**rank,) + shard.shape)


def reduce_bits(blocks, order, names):
    left = list(names)
    held = blocks.reshape((2,) * len(left) + blocks.shape[1:])
    for name in order:
        axis = left.index(name)
        here = lax.axis_index(name)
        send = lax.dynamic_index_in_dim(held, 1 - here, axis, keepdims=False)
        keep = lax.dynamic_index_in_dim(held, here, axis, keepdims=False)
        other = flip(send, name)
        held = (keep.astype(jnp.float32) + other.astype(jnp.float32)).astype(blocks.dtype)
        left.remove(name)
    return held


def bit_orders(names, core):
    outer = [name for name in names if name != core]
    count = len(outer)
    if count == 4:
        picks = ((0, 3, 2, 1), (0, 2, 1, 3), (0, 1, 3, 2))
        return [[outer[k] for k in pick] + [core] for pick in picks]
    step = max(1, count // 3)
    return [outer[step * k :] + outer[: step * k] + [core] for k in range(3)]


def device_mask(name, names):
    return 1 << (len(names) - 1 - names.index(name))


def gather_relative(shards, orders, names, early=(), work=None):
    held = []
    for shard, order in zip(shards, orders):
        grown, masks = shard, [0]
        for name in order[:-2]:
            grown = lax.optimization_barrier(jnp.concatenate([grown, flip(grown, name)]))
            masks = masks + [mask | device_mask(name, names) for mask in masks]
        held.append((grown, masks))
    grown_all = [grown for grown, _ in held]
    others = [flip(grown, order[-2]) for grown, order in zip(grown_all, orders)]
    if work is not None:
        late, early = lax.optimization_barrier((grown_all, early))
        grown_all, early = lax.optimization_barrier((late, work(*early)))
    gathered = []
    for grown, other, (_, masks), order in zip(grown_all, others, held, orders):
        bit = device_mask(order[-2], names)
        pieces = [(grown, masks), (other, [mask | bit for mask in masks])]
        bit = device_mask(order[-1], names)
        pieces = pieces + [
            (flip(piece, order[-1]), [mask | bit for mask in own]) for piece, own in pieces
        ]
        gathered.append(pieces)
    return gathered, early


def add_terms(terms):
    total = terms[0].astype(jnp.float32)
    for term in terms[1:]:
        total = total + term.astype(jnp.float32)
    return total


def reduce_relative(keeps, sends, orders, state=None, works=(), early_sums=None):
    works = dict(works)
    sends = list(sends)
    terms_all = [[keep] for keep in keeps]
    whole_all = [[keep] for keep in keeps]
    for step in range(len(orders[0])):
        for k, order in enumerate(orders):
            half = terms_all[k][0].shape[0] // 2
            if step == 0:
                urgent, rest = (flip(send, order[step]) for send in sends[k])
                whole_all[k].append(rest)
            else:
                other = flip(sends[k], order[step])
                urgent, rest = other[half:], other[:half]
                whole_all[k].append(other)
            if half:
                upper = [term[half:] for term in terms_all[k]] + [urgent]
                sends[k] = add_terms(upper).astype(urgent.dtype)
                terms_all[k] = [term[:half] for term in terms_all[k]] + [rest]
            else:
                terms_all[k] = terms_all[k] + [urgent]
        if step == early_sums:
            left = terms_all[0][0].shape[0]
            for k in range(len(orders)):
                sends[k], terms = lax.optimization_barrier((sends[k], whole_all[k]))
                terms_all[k] = [add_terms([term[:left] for term in terms])]
                whole_all[k] = list(terms_all[k])
        if step in works:
            sends[-1], state = lax.optimization_barrier((sends[-1], state))
            state = works[step](state)
    return whole_all, state


def dot_nn(left, right):
    return lax.dot_general(
        left, right, (((1,), (0,)), ((), ())), preferred_element_type=jnp.float32
    )


def interleave(count, rows):
    span = rows // count
    to = lax.broadcasted_iota(jnp.int32, (rows, rows), 0)
    source = lax.broadcasted_iota(jnp.int32, (rows, rows), 1)
    return (source == count * lax.rem(to, span) + lax.div(to, span)).astype(jnp.bfloat16)


def deinterleave(count, rows):
    span = rows // count
    source = lax.broadcasted_iota(jnp.int32, (rows, rows), 1)
    to = lax.broadcasted_iota(jnp.int32, (rows, rows), 0)
    return (to == count * lax.rem(source, span) + lax.div(source, span)).astype(jnp.bfloat16)


def valid_rows(len_ref, rows, seq_here):
    length = rows // seq_here
    row = lax.broadcasted_iota(jnp.int32, (rows, 1), 0)
    valid = jnp.zeros((rows, 1), jnp.float32)
    for seq in range(seq_here):
        inside = (row >= seq * length) & (row < seq * length + len_ref[seq])
        valid = jnp.where(inside, 1.0, valid)
    return valid


def stack_pair(value):
    lane = lax.broadcasted_iota(jnp.int32, value.shape, 1)
    zero = jnp.zeros_like(value)
    left = lane < HEAD_DIM
    return jnp.concatenate([jnp.where(left, value, zero), jnp.where(left, zero, value)], axis=0)


def join_pair(stacked):
    half = stacked.shape[0] // 2
    lane = lax.broadcasted_iota(jnp.int32, (half, stacked.shape[1]), 1)
    return jnp.where(lane < HEAD_DIM, stacked[:half], stacked[half:])


def pair_scores(stacked, keys, limit):
    raw = contract_cols(stacked, keys) * HEAD_DIM ** (-0.5)
    column = lax.broadcasted_iota(jnp.int32, raw.shape, 1)
    return jnp.where(column < limit, raw, -1e30)


def center_rows(resid):
    center = resid - jnp.mean(resid, axis=-1, keepdims=True)
    inverse = lax.rsqrt(jnp.mean(center * center, axis=-1, keepdims=True) + norm_eps)
    return center * inverse, inverse


def gelu_phi(value):
    return 0.5 * (1.0 + lax.erf(value * 0.7071067811865476))


def forward_kernel(plan, planes, seq_here, *refs):
    me_ref, len_ref, place_ref, x_ref, vec_ref = refs[:5]
    blocks = refs[5 : 5 + len(plan)]
    heads_refs = refs[5 + len(plan) : 8 + len(plan)]
    wall_ref, qkv_ref, att_ref, n1_ref, pre_ref, n2_ref, stat_ref = refs[
        8 + len(plan) : 15 + len(plan)
    ]
    raw, turned, qkv, att, n1, pre_all, in_sem, out_sem = refs[15 + len(plan) :]
    rows, width = x_ref.shape
    length = rows // seq_here
    pairs = width // (2 * HEAD_DIM)
    up = 4 * width
    me = me_ref[0]
    for first in (True, False):
        for (part, unit, masks), block in zip(plan, blocks):
            for place, mask in enumerate(masks):
                device = me ^ mask
                early = device < planes

                @pl.when(early if first else jnp.logical_not(early))
                def _(device=device, part=part, unit=unit, block=block, place=place, first=first):
                    row = pl.multiple_of((3 * device + part) * unit, 16)
                    pltpu.make_async_copy(
                        block.at[place], raw.at[pl.ds(row, unit)], in_sem.at[0 if first else 1]
                    ).start()

    copies = []

    def save(source, target):
        copy = pltpu.make_async_copy(source, target, out_sem.at[len(copies)])
        copy.start()
        copies.append(copy)

    valid = valid_rows(len_ref, rows, seq_here)
    x = (x_ref[...].astype(jnp.float32) * valid).astype(jnp.bfloat16)
    split3, split4 = interleave(3, 384), interleave(4, 256)
    arrived = raw.at[0 : 3 * width]
    pltpu.make_async_copy(arrived, arrived, in_sem.at[0]).wait()

    for b in range(width // 128):
        block = dot_nn(split3, raw[384 * b : 384 * b + 384, :]).astype(jnp.bfloat16)
        for p in range(3):
            turned[width * p + 128 * b : width * p + 128 * b + 128, :] = block[
                128 * p : 128 * p + 128
            ]
    save(turned.at[0 : 3 * width], wall_ref.at[0 : 3 * width])
    for p, bias in ((0, 0), (1, None), (2, 1)):
        value = dot_nn(x, turned[width * p : width * (p + 1), :])
        if bias is not None:
            value = value + vec_ref[bias : bias + 1, :]
        qkv[:, width * p : width * (p + 1)] = value.astype(jnp.bfloat16)
    save(qkv, qkv_ref)

    stats = jnp.zeros((2 * length, 128), jnp.float32)
    lane = lax.broadcasted_iota(jnp.int32, stats.shape, 1)
    for seq in range(seq_here):
        here = slice(seq * length, (seq + 1) * length)
        for g in range(pairs):
            cols = [slice(width * p + 128 * g, width * p + 128 * g + 128) for p in range(3)]
            query, key, value = (qkv[here, c] for c in cols)
            scores = pair_scores(stack_pair(query), key, len_ref[seq])
            top = jnp.max(scores, axis=-1, keepdims=True)
            expo = jnp.exp(scores - top)
            total = jnp.sum(expo, axis=-1, keepdims=True)
            stats = jnp.where(lane == seq * pairs + g, top + jnp.log(total), stats)
            probs = (expo / total).astype(jnp.bfloat16)
            att[here, 128 * g : 128 * g + 128] = join_pair(dot_nn(probs, value)).astype(
                jnp.bfloat16
            )
    save(att, att_ref)
    arrived = raw.at[3 * width : 3 * up]
    pltpu.make_async_copy(arrived, arrived, in_sem.at[1]).wait()
    save(raw.at[3 * width : up], wall_ref.at[3 * width : up])
    save(raw.at[2 * up : 3 * up], wall_ref.at[2 * up : 3 * up])

    branch = dot_nn(att[...], raw[3 * width : up, :]) + vec_ref[2:3, :]
    for b in range(width // 64):
        block = dot_nn(split4, raw[up + 256 * b : up + 256 * b + 256, :]).astype(jnp.bfloat16)
        for p in range(4):
            row = width * (3 + p) + 64 * b
            turned[row : row + 64, :] = block[64 * p : 64 * p + 64]
    save(turned.at[3 * width : 7 * width], wall_ref.at[up : 2 * up])
    normed, inverse = center_rows(x.astype(jnp.float32) + branch)
    n1[...] = normed
    save(n1, n1_ref)
    stat_one = seq_here * pairs
    hidden = normed * vec_ref[3:4, :] + vec_ref[4:5, :]
    hidden_low = hidden.astype(jnp.bfloat16)
    total = hidden + vec_ref[9:10, :]
    for p in range(4):
        pre = dot_nn(hidden_low, turned[width * (3 + p) : width * (4 + p), :])
        pre = pre + vec_ref[5 + p : 6 + p, :]
        pre_all[p] = pre
        save(pre_all.at[p], pre_ref.at[p])
        act = (pre * gelu_phi(pre)).astype(jnp.bfloat16)
        total = total + dot_nn(act, raw[2 * up + width * p : 2 * up + width * (p + 1), :])
    normed, inverse_two = center_rows(total)
    n2_ref[...] = normed
    wide = lax.broadcasted_iota(jnp.int32, (rows, 128), 1)
    ends = jnp.where(
        wide == stat_one, inverse, jnp.where(wide == stat_one + 1, inverse_two, 0.0)
    )
    stat_ref[0] = stats
    stat_ref[1] = ends
    output = ((normed * vec_ref[10:11, :] + vec_ref[11:12, :]) * valid).astype(jnp.bfloat16)
    spot = lax.broadcasted_iota(jnp.int32, (rows, place_ref.shape[1]), 0)
    choose = (spot == place_ref[...]).astype(jnp.bfloat16)
    heads = contract_rows(choose, output).astype(jnp.bfloat16)
    cut = width // 3
    for k, heads_ref in enumerate(heads_refs):
        heads_ref[0] = heads[:, k * cut : (k + 1) * cut]
    for copy in copies:
        copy.wait()


def send_block(source, sinks, spots, device, part, out_sem):
    spot = spots[3 * device + part]
    half = sinks[0].shape[0]

    def copy(sink, place):
        pltpu.make_async_copy(source, sink.at[place], out_sem).start()

    keep, urgent, rest = sinks[3 * part : 3 * part + 3]
    pl.when(spot < half)(functools.partial(copy, keep, spot))
    pl.when((spot >= half) & (spot < half + half // 2))(
        functools.partial(copy, rest, spot - half)
    )
    pl.when(spot >= half + half // 2)(functools.partial(copy, urgent, spot - half - half // 2))


def sink_shapes(devices, block, dtype):
    half = devices // 2
    return [
        jax.ShapeDtypeStruct((count,) + block, dtype)
        for _ in range(3)
        for count in (half, half // 2, half // 2)
    ]


def wait_sinks(sinks, out_sem):
    for sink in sinks:
        pltpu.make_async_copy(sink, sink, out_sem).wait()


def backward_kernel(unit, seq_here, *refs):
    len_ref, spots, place_ref, x_ref, vec_ref, top_ref = refs[:6]
    wall_ref, qkv_ref, att_ref, n1_ref, pre_ref, n2_ref, stat_ref = refs[6:13]
    gin_ref, dvec_ref = refs[13:15]
    sinks = refs[15:24]
    wall, grads, parts, dqkv, qkv, att, n1, pre_all, in_sem, out_sem = refs[24:]
    rows, width = x_ref.shape
    length = rows // seq_here
    pairs = width // (2 * HEAD_DIM)
    low = jnp.bfloat16
    up = 4 * width
    ranges = [(n1_ref, n1)]
    for p in range(4):
        for first in (2 * up, up):
            rows_p = slice(first + width * p, first + width * (p + 1))
            ranges.append((wall_ref.at[rows_p], wall.at[rows_p]))
        ranges.append((pre_ref.at[p], pre_all.at[p]))
    out = slice(3 * width, up)
    ranges += [(att_ref, att), (wall_ref.at[out], wall.at[out]), (qkv_ref, qkv)]
    ranges += [(wall_ref.at[0 : 3 * width], wall.at[0 : 3 * width])]
    loads = [
        pltpu.make_async_copy(source, target, in_sem.at[k])
        for k, (source, target) in enumerate(ranges)
    ]
    for load in loads:
        load.start()

    def emit(first, last):
        for u in range(first // unit, last // unit):
            block = grads.at[u * unit : (u + 1) * unit]
            send_block(block, sinks, spots, u // 3, u % 3, out_sem)

    valid = valid_rows(len_ref, rows, seq_here)
    x = (x_ref[...].astype(jnp.float32) * valid).astype(low)
    stat_one = seq_here * pairs
    wide = lax.broadcasted_iota(jnp.int32, (rows, 128), 1)
    ends = stat_ref[1]
    inverse_one = jnp.sum(jnp.where(wide == stat_one, ends, 0.0), axis=-1, keepdims=True)
    inverse_two = jnp.sum(jnp.where(wide == stat_one + 1, ends, 0.0), axis=-1, keepdims=True)

    spot = lax.broadcasted_iota(jnp.int32, (rows, place_ref.shape[1]), 0)
    choose = (spot == place_ref[...]).astype(jnp.float32)
    d_output = valid * lax.dot_general(
        choose,
        top_ref[...],
        (((1,), (0,)), ((), ())),
        precision=lax.Precision.HIGHEST,
        preferred_element_type=jnp.float32,
    )
    normed = n2_ref[...]

    def sums(row, value):
        dvec_ref[row : row + 1, :] = jnp.sum(value, axis=0, keepdims=True)

    sums(10, d_output * normed)
    sums(11, d_output)
    d_resid = norm_back(d_output * vec_ref[10:11, :], normed, inverse_two)
    d_ffn = d_resid.astype(low)
    sums(9, d_ffn.astype(jnp.float32))
    d_hidden = d_resid
    loads[0].wait()
    normed = n1[...]
    hidden_low = (normed * vec_ref[3:4, :] + vec_ref[4:5, :]).astype(low)
    for p in range(4):
        for load in loads[1 + 3 * p : 4 + 3 * p]:
            load.wait()
        pre = pre_all[p]
        phi = gelu_phi(pre)
        act = (pre * phi).astype(low)
        down = slice(2 * up + width * p, 2 * up + width * (p + 1))
        grads[down, :] = contract_rows(act, d_ffn).astype(low)
        emit(down.start, down.stop)
        slope = phi + pre * jnp.exp(-0.5 * pre * pre) * 0.3989422804014327
        d_pre = (contract_cols(d_ffn, wall[down, :]) * slope).astype(low)
        sums(5 + p, d_pre.astype(jnp.float32))
        parts[width * p : width * (p + 1), :] = contract_rows(hidden_low, d_pre).astype(low)
        d_hidden = d_hidden + contract_cols(d_pre, wall[up + width * p : up + width * (p + 1), :])
    merge4 = deinterleave(4, 256)
    for b in range(width // 64):
        block = jnp.concatenate(
            [parts[width * p + 64 * b : width * p + 64 * b + 64, :] for p in range(4)], axis=0
        )
        grads[up + 256 * b : up + 256 * b + 256, :] = dot_nn(merge4, block).astype(low)
        if b % 3 == 2:
            emit(up + 256 * (b - 2), up + 256 * (b + 1))

    sums(3, d_hidden * normed)
    sums(4, d_hidden)
    d_resid = norm_back(d_hidden * vec_ref[3:4, :], normed, inverse_one)
    d_branch = d_resid.astype(low)
    sums(2, d_branch.astype(jnp.float32))
    for load in loads[13:]:
        load.wait()
    grads[3 * width : up, :] = contract_rows(att[...], d_branch).astype(low)
    emit(3 * width, up)
    d_att = contract_cols(d_branch, wall[3 * width : up, :]).astype(low)
    lane = lax.broadcasted_iota(jnp.int32, (2 * length, 128), 1)
    stats = stat_ref[0]
    for seq in range(seq_here):
        here = slice(seq * length, (seq + 1) * length)
        for g in range(pairs):
            cols = [slice(width * p + 128 * g, width * p + 128 * g + 128) for p in range(3)]
            query, key, value = (qkv[here, c] for c in cols)
            query = stack_pair(query)
            log_sum = jnp.sum(
                jnp.where(lane == seq * pairs + g, stats, 0.0), axis=-1, keepdims=True
            )
            probs = jnp.exp(pair_scores(query, key, len_ref[seq]) - log_sum)
            d_heads = stack_pair(d_att[here, 128 * g : 128 * g + 128])
            d_probs = contract_cols(d_heads, value)
            dqkv[here, cols[2]] = contract_rows(probs.astype(low), d_heads).astype(low)
            delta = jnp.sum(d_probs * probs, axis=-1, keepdims=True)
            d_scores = (probs * (d_probs - delta)).astype(low)
            scale = HEAD_DIM ** (-0.5)
            dqkv[here, cols[0]] = (join_pair(dot_nn(d_scores, key)) * scale).astype(low)
            dqkv[here, cols[1]] = (contract_rows(d_scores, query) * scale).astype(low)
    sums(0, dqkv[:, :width].astype(jnp.float32))
    sums(1, dqkv[:, 2 * width :].astype(jnp.float32))
    for p in range(3):
        d_part = dqkv[:, width * p : width * (p + 1)]
        parts[width * p : width * (p + 1), :] = contract_rows(x, d_part).astype(low)
    merge3 = deinterleave(3, 384)
    for b in range(width // 128):
        block = jnp.concatenate(
            [parts[width * p + 128 * b : width * p + 128 * b + 128, :] for p in range(3)], axis=0
        )
        grads[384 * b : 384 * b + 384, :] = dot_nn(merge3, block).astype(low)
        if b % 2 == 1:
            emit(384 * (b - 1), 384 * (b + 1))
    total = d_resid
    for p in range(3):
        d_part = dqkv[:, width * p : width * (p + 1)]
        total = total + contract_cols(d_part, wall[width * p : width * (p + 1), :])
    gin_ref[...] = total * valid
    wait_sinks(sinks, out_sem)


def call_forward(me, lengths, places, rows, vecs, gathered, devices, seq_here):
    count, width = rows.shape
    pieces = [(part, piece, masks) for part, own in enumerate(gathered) for piece, masks in own]
    plan = tuple((part, piece.shape[1], tuple(masks)) for part, piece, masks in pieces)
    total = 12 * width
    vmem = pl.BlockSpec(memory_space=pltpu.VMEM)
    smem = pl.BlockSpec(memory_space=pltpu.SMEM)
    hbm = pl.BlockSpec(memory_space=pl.ANY)
    low, full = jnp.bfloat16, jnp.float32
    outs = pl.pallas_call(
        functools.partial(forward_kernel, plan, devices // 4, seq_here),
        out_shape=[
            *[jax.ShapeDtypeStruct((1, places.shape[1], width // 3), low)] * 3,
            jax.ShapeDtypeStruct((total, width), low),
            jax.ShapeDtypeStruct((count, 3 * width), low),
            jax.ShapeDtypeStruct((count, width), low),
            jax.ShapeDtypeStruct((count, width), full),
            jax.ShapeDtypeStruct((4, count, width), full),
            jax.ShapeDtypeStruct((count, width), full),
            jax.ShapeDtypeStruct((2, count, 128), full),
        ],
        in_specs=[smem, smem, vmem, vmem, vmem] + [hbm] * len(pieces),
        out_specs=[vmem] * 3 + [hbm] * 5 + [vmem] * 2,
        scratch_shapes=[
            pltpu.VMEM((total, width), low),
            pltpu.VMEM((7 * width, width), low),
            pltpu.VMEM((count, 3 * width), low),
            pltpu.VMEM((count, width), low),
            pltpu.VMEM((count, width), full),
            pltpu.VMEM((4, count, width), full),
            pltpu.SemaphoreType.DMA((2,)),
            pltpu.SemaphoreType.DMA((11,)),
        ],
        compiler_params=pltpu.CompilerParams(vmem_limit_bytes=58 * 2**20),
        cost_estimate=pl.CostEstimate(
            flops=2 * count * total * width, bytes_accessed=48 * 2**20, transcendentals=0
        ),
    )(me, lengths, places, rows, vecs, *[piece for _, piece, _ in pieces])
    return *outs[:3], outs[3:]


def call_backward(lengths, spots, places, rows, vecs, top, saved, unit, seq_here):
    count, width = rows.shape
    total = 12 * width
    vmem = pl.BlockSpec(memory_space=pltpu.VMEM)
    smem = pl.BlockSpec(memory_space=pltpu.SMEM)
    hbm = pl.BlockSpec(memory_space=pl.ANY)
    low, full = jnp.bfloat16, jnp.float32
    return pl.pallas_call(
        functools.partial(backward_kernel, unit, seq_here),
        out_shape=[
            jax.ShapeDtypeStruct((count, width), full),
            jax.ShapeDtypeStruct((12, width), full),
        ]
        + sink_shapes(total // unit // 3, (unit, width), low),
        in_specs=[smem, smem, vmem, vmem, vmem, vmem] + [hbm] * 5 + [vmem] * 2,
        out_specs=[vmem, vmem] + [hbm] * 9,
        scratch_shapes=[
            pltpu.VMEM((total, width), low),
            pltpu.VMEM((total, width), low),
            pltpu.VMEM((4 * width, width), low),
            pltpu.VMEM((count, 3 * width), low),
            pltpu.VMEM((count, 3 * width), low),
            pltpu.VMEM((count, width), low),
            pltpu.VMEM((count, width), full),
            pltpu.VMEM((4, count, width), full),
            pltpu.SemaphoreType.DMA((17,)),
            pltpu.SemaphoreType.DMA,
        ],
        compiler_params=pltpu.CompilerParams(vmem_limit_bytes=58 * 2**20),
        cost_estimate=pl.CostEstimate(
            flops=4 * count * total * width, bytes_accessed=48 * 2**20, transcendentals=0
        ),
    )(lengths, spots, places, rows, vecs, top, *saved)


def turn_lanes(shift, width):
    source = lax.broadcasted_iota(jnp.int32, (width, width), 0) + shift
    source = jnp.where(source >= width, source - width, source)
    return (source == lax.broadcasted_iota(jnp.int32, (width, width), 1)).astype(jnp.bfloat16)


def table_kernel(embed_here, shift_ref, rows_ref, ends_ref, table_ref, owned_ref, tall):
    count, width = table_ref.shape
    here = rows_ref.shape[0]
    shift = shift_ref[0]
    tall[here:, :] = jnp.zeros((tall.shape[0] - here, width), jnp.float32)
    tall[8 : 8 + here, :] = rows_ref[...].astype(jnp.float32)
    tall[7:8, :] = ends_ref[0:1, :]
    tall[7 + here : 8 + here, :] = tall[7 + here : 8 + here, :] + ends_ref[1:2, :]
    tall[8 + here : 9 + here, :] = ends_ref[2:3, :]
    lane = lax.broadcasted_iota(jnp.int32, (count, width), 1)
    rolled = jnp.where(lane < width - shift, tall[8 : 8 + count, :], tall[7 : 7 + count, :])
    table = dot_nn(rolled.astype(jnp.bfloat16), turn_lanes(shift, width))
    start = lax.broadcasted_iota(jnp.int32, (count, 1), 0) * width - shift
    owned = (start >= 0) & (start < embed_here)
    table_ref[...] = table.astype(jnp.bfloat16)
    owned_ref[...] = jnp.where(owned, table, 0.0).astype(jnp.bfloat16)


def call_table(shift, rows, ends, count, embed_here):
    width = rows.shape[1]
    vmem = pl.BlockSpec(memory_space=pltpu.VMEM)
    smem = pl.BlockSpec(memory_space=pltpu.SMEM)
    return pl.pallas_call(
        functools.partial(table_kernel, embed_here),
        out_shape=[jax.ShapeDtypeStruct((count, width), jnp.bfloat16)] * 2,
        in_specs=[smem, vmem, vmem],
        out_specs=[vmem] * 2,
        scratch_shapes=[pltpu.VMEM((count + 16, width), jnp.float32)],
        compiler_params=pltpu.CompilerParams(vmem_limit_bytes=22 * 2**20),
        cost_estimate=pl.CostEstimate(
            flops=32 * count * width * width, bytes_accessed=40 * 2**20, transcendentals=0
        ),
    )(shift, rows, ends)


def eye_mask():
    return lax.broadcasted_iota(jnp.int32, (128, 128), 0) == lax.broadcasted_iota(
        jnp.int32, (128, 128), 1
    )


def to_row(column, eye):
    return jnp.concatenate(
        [
            jnp.sum(jnp.where(eye, column[k : k + 128], 0.0), axis=0, keepdims=True)
            for k in range(0, column.shape[0], 128)
        ],
        axis=1,
    )


def to_column(row, eye):
    return jnp.concatenate(
        [
            jnp.sum(jnp.where(eye, row[:, k : k + 128], 0.0), axis=1, keepdims=True)
            for k in range(0, row.shape[1], 128)
        ],
        axis=0,
    )


def logits_kernel(plan, embed_here, picks, span, *refs):
    me_ref, shift_ref, table_ref = refs[:3]
    blocks = refs[3 : 3 + len(plan)]
    picked_ref, expo_ref, stat_ref, picked, expo_all, in_sem, out_sem = refs[3 + len(plan) :]
    count, width = table_ref.shape
    me, shift = me_ref[0], shift_ref[0]
    group = 4
    for (part, masks), block in zip(plan, blocks):
        cols = pl.ds(part * block.shape[2], block.shape[2])
        for place, mask in enumerate(masks):
            device = me ^ mask
            pltpu.make_async_copy(
                block.at[place], picked.at[device, :, cols], in_sem
            ).start()
    whole = embed_here // width // 128 * 128
    eye = eye_mask()
    row_start = lax.broadcasted_iota(jnp.int32, (1, count), 1) * width - shift
    touched = (row_start < embed_here)[:, whole:]
    owned = (row_start >= 0)[:, :128]
    tops, totals, copies = [], [], []

    def save(source, target):
        copies.append(pltpu.make_async_copy(source, target, out_sem.at[len(copies)]))
        copies[-1].start()

    step = group * picks
    pltpu.make_async_copy(picked, picked, in_sem).wait()
    save(picked, picked_ref)
    for k in range(picked.shape[0] // group):
        here = slice(k * step, (k + 1) * step)
        rows = jnp.concatenate([picked[group * k + d, :picks, :] for d in range(group)], axis=0)
        logits = contract_cols(rows, table_ref[...])
        logits = jnp.concatenate(
            [logits[:, :whole], jnp.where(touched, logits[:, whole:], -1e30)], axis=1
        )
        top = jnp.max(logits, axis=1, keepdims=True)
        expo = jnp.exp(logits - top)
        expo_all[here, :] = expo
        save(expo_all.at[here], expo_ref.at[here])
        ends = jnp.where(owned, expo[:, :128], 0.0)
        total = jnp.sum(jnp.concatenate([ends, expo[:, 128:]], axis=1), axis=1, keepdims=True)
        tops.append(to_row(top, eye))
        totals.append(to_row(total, eye))
    join = span // step
    stats = jnp.concatenate(
        [
            jnp.concatenate(own[k : k + join], axis=1)
            for own in (tops, totals)
            for k in range(0, len(own), join)
        ],
        axis=0,
    )
    for device in range(stat_ref.shape[0]):
        stat_ref[device] = stats
    for copy in copies:
        copy.wait()


def call_logits(me, shift, table, gathered, picks, embed_here, devices):
    count, width = table.shape
    pieces = [(part, piece, masks) for part, own in enumerate(gathered) for piece, masks in own]
    plan = tuple((part, tuple(masks)) for part, _, masks in pieces)
    block = pieces[0][1].shape[1]
    rows = devices * picks
    span = rows // 4
    vmem = pl.BlockSpec(memory_space=pltpu.VMEM)
    smem = pl.BlockSpec(memory_space=pltpu.SMEM)
    hbm = pl.BlockSpec(memory_space=pl.ANY)
    low, full = jnp.bfloat16, jnp.float32
    return pl.pallas_call(
        functools.partial(logits_kernel, plan, embed_here, picks, span),
        out_shape=[
            jax.ShapeDtypeStruct((devices, block, width), low),
            jax.ShapeDtypeStruct((rows, count), full),
            jax.ShapeDtypeStruct((devices, 8, span), full),
        ],
        in_specs=[smem, smem, vmem] + [hbm] * len(pieces),
        out_specs=[hbm, hbm, vmem],
        scratch_shapes=[
            pltpu.VMEM((devices, block, width), low),
            pltpu.VMEM((rows, count), full),
            pltpu.SemaphoreType.DMA,
            pltpu.SemaphoreType.DMA((devices // 4 + 1,)),
        ],
        compiler_params=pltpu.CompilerParams(vmem_limit_bytes=58 * 2**20),
        cost_estimate=pl.CostEstimate(
            flops=2 * rows * count * width, bytes_accessed=16 * 2**20, transcendentals=0
        ),
    )(me, shift, table, *[piece for _, piece, _ in pieces])


def mix_kernel(expo_ref, label_ref, owned_ref, mix_ref, row_ref, own_ref):
    rows, count = expo_ref.shape
    step = min(rows, 256)
    eye = eye_mask()
    lane = lax.broadcasted_iota(jnp.int32, (step, count), 1)
    own = []
    for k in range(0, rows, step):
        here = slice(k, k + step)
        expo = expo_ref[here, :]
        hot = lane == to_column(label_ref[0:1, here], eye).astype(jnp.int32)
        own.append(to_row(jnp.sum(jnp.where(hot, expo, 0.0), axis=1, keepdims=True), eye))
        others = jnp.where(hot, 0.0, expo).astype(jnp.bfloat16)
        mix_ref[here, :] = dot_nn(others, owned_ref[...]).astype(jnp.bfloat16)
        row_ref[here, :] = dot_nn(hot.astype(jnp.bfloat16), owned_ref[...]).astype(jnp.bfloat16)
    own_ref[...] = jnp.broadcast_to(jnp.concatenate(own, axis=1), own_ref.shape)


def call_mix(expo, labels, owned):
    rows, count = expo.shape
    width = owned.shape[1]
    low = jnp.bfloat16
    step = rows // 4

    def tile(lanes):
        return pl.BlockSpec((step, lanes), lambda k: (k, 0))

    row_tile = pl.BlockSpec((8, step), lambda k: (0, k))
    return pl.pallas_call(
        mix_kernel,
        grid=(4,),
        out_shape=[
            jax.ShapeDtypeStruct((rows, width), low),
            jax.ShapeDtypeStruct((rows, width), low),
            jax.ShapeDtypeStruct((8, rows), jnp.float32),
        ],
        in_specs=[tile(count), row_tile, pl.BlockSpec((count, width), lambda k: (0, 0))],
        out_specs=[tile(width), tile(width), row_tile],
        compiler_params=pltpu.CompilerParams(vmem_limit_bytes=48 * 2**20),
        cost_estimate=pl.CostEstimate(
            flops=16 * rows * count * width, bytes_accessed=64 * 2**20, transcendentals=0
        ),
    )(expo, labels, owned)


def terms_kernel(plan, picks, me_ref, *refs):
    stat_ref, mix_ref, row_ref, own_ref, label_ref, scale_ref = refs[:6]
    sinks = refs[6:15]
    terms, out_sem = refs[15:]
    span, width = mix_ref.shape
    chunks = terms.shape[0]
    group = span // picks
    me = me_ref[0]
    step = pl.program_id(0)
    chunk = step ^ lax.div(me, group)
    mine = stat_ref[pl.ds(me, 1), pl.ds(chunk, 1), :][0]
    tops = stat_ref[:, pl.ds(chunk, 1), :]
    top = jnp.max(tops, axis=0)
    totals = stat_ref[:, pl.ds(chunks + chunk, 1), :]
    total = jnp.sum(totals * jnp.exp(tops - top[None]), axis=0)
    scale = jnp.exp(mine - top) / total
    used = label_ref[1:2, :]
    label = (own_ref[0:1, :] * scale - 1.0).astype(jnp.bfloat16).astype(jnp.float32) * used
    scale = scale * used
    scale_ref[...] = jnp.broadcast_to(scale, scale_ref.shape)
    eye = eye_mask()
    terms[step] = (
        mix_ref[...].astype(jnp.float32) * to_column(scale, eye)
        + row_ref[...].astype(jnp.float32) * to_column(label, eye)
    ).astype(jnp.bfloat16)
    cut = width // 3
    half = sinks[0].shape[0]

    def send(now):
        for b in range(group):
            row = pl.multiple_of((b ^ lax.rem(me, group)) * picks, 16)
            for part, bits in enumerate(plan):
                relative = now * group + b
                spot = sum(
                    1 << (len(bits) - 1 - k) for k, bit in enumerate(bits) if relative & bit
                )
                kind = 0 if spot < half else (2 if spot < half + half // 2 else 1)
                spot = spot - (0, half + half // 2, half)[kind]
                pltpu.make_async_copy(
                    terms.at[now, pl.ds(row, picks), part * cut : (part + 1) * cut],
                    sinks[3 * part + kind].at[spot],
                    out_sem,
                ).start()

    for now in range(chunks):
        pl.when(step == now)(functools.partial(send, now))

    @pl.when(step == chunks - 1)
    def _():
        wait_sinks(sinks, out_sem)


def call_terms(me, stats, mix, label_rows, own, labels, plan, picks):
    rows, width = mix.shape
    devices, _, span = stats.shape
    hbm = pl.BlockSpec(memory_space=pl.ANY)
    low = jnp.bfloat16
    group = span // picks

    def tile(lanes):
        return pl.BlockSpec((span, lanes), lambda k, me: (k ^ lax.div(me[0], group), 0))

    row_tile = pl.BlockSpec((8, span), lambda k, me: (0, k ^ lax.div(me[0], group)))
    return pl.pallas_call(
        functools.partial(terms_kernel, plan, picks),
        grid_spec=pltpu.PrefetchScalarGridSpec(
            num_scalar_prefetch=1,
            grid=(rows // span,),
            in_specs=[
                pl.BlockSpec(stats.shape, lambda k, me: (0, 0, 0)),
                tile(width),
                tile(width),
                row_tile,
                row_tile,
            ],
            out_specs=[row_tile] + [hbm] * 9,
            scratch_shapes=[
                pltpu.VMEM((rows // span, span, width), low),
                pltpu.SemaphoreType.DMA,
            ],
        ),
        out_shape=[jax.ShapeDtypeStruct((8, rows), jnp.float32)]
        + sink_shapes(devices, (picks, width // 3), low),
        compiler_params=pltpu.CompilerParams(vmem_limit_bytes=48 * 2**20),
        cost_estimate=pl.CostEstimate(
            flops=8 * rows * width, bytes_accessed=10 * 2**20, transcendentals=0
        ),
    )(me, stats, mix, label_rows, own, labels)


def embed_kernel(picks, shift_ref, expo_ref, scale_ref, label_ref, picked_ref, out_ref, wide, turn):
    here, width = out_ref.shape
    rows, count = expo_ref.shape
    shift = shift_ref[0]
    chunk = pl.program_id(0)

    @pl.when(chunk == 0)
    def _():
        turn[...] = turn_lanes(shift, width)

    eye = eye_mask()
    probs = expo_ref[...] * to_column(scale_ref[0:1, :], eye)
    lane = lax.broadcasted_iota(jnp.int32, (rows, count), 1)
    used = label_ref[1:2, :]
    label = jnp.where(used > 0, label_ref[0:1, :], -1.0)
    hot = lane == to_column(label, eye).astype(jnp.int32)
    terms = jnp.where(hot, probs - 1.0, probs).astype(jnp.bfloat16)
    picked = jnp.concatenate([picked_ref[d, :picks, :] for d in range(rows // picks)], axis=0)
    turned = contract_cols(picked, turn[...]).astype(jnp.bfloat16)
    total = contract_rows(terms, turned)

    @pl.when(chunk == 0)
    def _():
        wide[...] = total

    @pl.when(chunk > 0)
    def _():
        wide[...] = wide[...] + total

    @pl.when(chunk == pl.num_programs(0) - 1)
    def _():
        lane = lax.broadcasted_iota(jnp.int32, (here, width), 1)
        out_ref[...] = jnp.where(lane < width - shift, wide[:here, :], wide[1 : here + 1, :])


def call_embed(shift, expo, scale, labels, picked, picks, here):
    rows, count = expo.shape
    devices, block, width = picked.shape
    smem = pl.BlockSpec(memory_space=pltpu.SMEM)
    step = rows // 8
    row_tile = pl.BlockSpec((8, step), lambda k: (0, k))
    return pl.pallas_call(
        functools.partial(embed_kernel, picks),
        grid=(8,),
        out_shape=jax.ShapeDtypeStruct((here, width), jnp.float32),
        in_specs=[
            smem,
            pl.BlockSpec((step, count), lambda k: (k, 0)),
            row_tile,
            row_tile,
            pl.BlockSpec((devices // 8, block, width), lambda k: (k, 0, 0)),
        ],
        out_specs=pl.BlockSpec((here, width), lambda k: (0, 0)),
        scratch_shapes=[
            pltpu.VMEM((count, width), jnp.float32),
            pltpu.VMEM((width, width), jnp.bfloat16),
        ],
        compiler_params=pltpu.CompilerParams(vmem_limit_bytes=58 * 2**20),
        cost_estimate=pl.CostEstimate(
            flops=16 * rows * count * width, bytes_accessed=64 * 2**20, transcendentals=0
        ),
    )(shift, expo, scale, labels, picked)


def step_kernel(counts, *refs):
    weight_ref, first_ref, second_ref = refs[:3]
    grad_ref, step_ref = refs[-2:]
    start, row = 3, 0
    width = refs[3].shape[2]
    share = width // 128
    for count in counts:
        total = add_terms([ref[0] for ref in refs[start : start + count]])
        rows = total.shape[0]
        for q in range(share):
            grad_ref[pl.ds(share * row + q, rows, stride=share), :] = total[
                :, 128 * q : 128 * q + 128
            ]
        start, row = start + count, row + rows
    step_ref[...] = adam_step(
        weight_ref[...], grad_ref[...], first_ref[...], second_ref[...], float(ADAM_STEP), decay_rate
    )


def call_step(weight, first, second, terms):
    shape = jax.ShapeDtypeStruct((weight.shape[0] // 128, 128), jnp.float32)
    vmem = pl.BlockSpec(memory_space=pltpu.VMEM)
    given = [value.reshape(shape.shape) for value in (weight, first, second)]
    blocks = [term for own in terms for term in own]
    first_block = pl.BlockSpec((1,) + blocks[0].shape[1:], lambda k: (0, 0, 0))
    grad, step = pl.pallas_call(
        functools.partial(step_kernel, [len(own) for own in terms]),
        grid=(1,),
        out_shape=[shape] * 2,
        in_specs=[vmem] * 3 + [first_block] * len(blocks),
        out_specs=[vmem] * 2,
        compiler_params=pltpu.CompilerParams(vmem_limit_bytes=24 * 2**20),
    )(*given, *blocks)
    return grad.reshape(-1), step.reshape(-1)


def plain_forward(mats_all, vecs_all, block_input, span_lengths):
    seq_here, length, width = block_input.shape
    rows_here = seq_here * length
    heads_count = width // HEAD_DIM
    head_scale = HEAD_DIM ** (-0.5)
    low = jnp.bfloat16
    w_qkv, w_out, w_up, w_down = split_mats(mats_all)
    bias_q, bias_v, bias_out, gain_one, shift_one, bias_up, bias_down, gain_two, shift_two = (
        split_vecs(vecs_all)
    )
    valid = jnp.arange(length)[None, :] < span_lengths[:, None]
    valid_col = valid.reshape(rows_here, 1).astype(jnp.float32)
    tok_rows = (block_input * valid[:, :, None].astype(low)).reshape(rows_here, width)
    qkv_bias = jnp.concatenate([bias_q, jnp.zeros((width,), jnp.float32), bias_v])
    projected = (jnp.dot(tok_rows, w_qkv, preferred_element_type=jnp.float32) + qkv_bias).astype(
        low
    )
    shaped = projected.reshape(seq_here, length, 3, heads_count, HEAD_DIM)
    queries = shaped[:, :, 0]
    key_rows = shaped[:, :, 1]
    value_rows = shaped[:, :, 2]
    key_valid = valid[:, None, None, :]

    def make_scores():
        raw = (
            jnp.einsum("sqhd,skhd->shqk", queries, key_rows, preferred_element_type=jnp.float32)
            * head_scale
        )
        return jnp.where(key_valid, raw, -1e30)

    scores = make_scores()
    row_max = jnp.max(scores, axis=-1, keepdims=True)
    expo_vals = jnp.exp(scores - row_max)
    row_sum = jnp.sum(expo_vals, axis=-1, keepdims=True)
    row_lse = row_max + jnp.log(row_sum)
    attn_probs = (expo_vals / row_sum).astype(low)
    attended = (
        jnp.einsum("shqk,skhd->sqhd", attn_probs, value_rows, preferred_element_type=jnp.float32)
        .reshape(rows_here, width)
        .astype(low)
    )
    branch = jnp.dot(attended, w_out, preferred_element_type=jnp.float32) + bias_out
    normed_one, inverse_one = center_scale(tok_rows.astype(jnp.float32) + branch)
    hidden_one = normed_one * gain_one + shift_one
    hidden_low = hidden_one.astype(low)
    pre_act = jnp.dot(hidden_low, w_up, preferred_element_type=jnp.float32) + bias_up
    act_low = jax.nn.gelu(pre_act, approximate=False).astype(low)
    ffn_out = jnp.dot(act_low, w_down, preferred_element_type=jnp.float32) + bias_down
    normed_two, inverse_two = center_scale(hidden_one + ffn_out)
    output = (normed_two * gain_two + shift_two) * valid_col

    def plain_backward(d_output):
        d_gain_two = jnp.sum(d_output * normed_two, axis=0)
        d_shift_two = jnp.sum(d_output, axis=0)
        d_resid_two = norm_back(d_output * gain_two, normed_two, inverse_two)
        d_ffn = d_resid_two.astype(low)
        d_bias_down = jnp.sum(d_ffn.astype(jnp.float32), axis=0)
        d_w_down = contract_rows(act_low, d_ffn)
        d_act = contract_cols(d_ffn, w_down)
        d_pre = (d_act * gelu_slope(pre_act)).astype(low)
        d_bias_up = jnp.sum(d_pre.astype(jnp.float32), axis=0)
        d_w_up = contract_rows(hidden_low, d_pre)
        d_hidden = contract_cols(d_pre, w_up) + d_resid_two
        d_gain_one = jnp.sum(d_hidden * normed_one, axis=0)
        d_shift_one = jnp.sum(d_hidden, axis=0)
        d_resid_one = norm_back(d_hidden * gain_one, normed_one, inverse_one)
        d_branch = d_resid_one.astype(low)
        d_bias_out = jnp.sum(d_branch.astype(jnp.float32), axis=0)
        d_w_out = contract_rows(attended, d_branch)
        d_attended = (
            contract_cols(d_branch, w_out).astype(low).reshape(seq_here, length, heads_count, HEAD_DIM)
        )
        probs_again = jnp.exp(make_scores() - row_lse)
        probs_low = probs_again.astype(low)
        d_probs = jnp.einsum(
            "sqhd,skhd->shqk", d_attended, value_rows, preferred_element_type=jnp.float32
        )
        d_values = jnp.einsum(
            "shqk,sqhd->skhd", probs_low, d_attended, preferred_element_type=jnp.float32
        )
        row_delta = jnp.sum(d_probs * probs_again, axis=-1, keepdims=True)
        d_scores = (probs_again * (d_probs - row_delta)).astype(low)
        d_queries = (
            jnp.einsum("shqk,skhd->sqhd", d_scores, key_rows, preferred_element_type=jnp.float32)
            * head_scale
        )
        d_keys = (
            jnp.einsum("shqk,sqhd->skhd", d_scores, queries, preferred_element_type=jnp.float32)
            * head_scale
        )
        d_qkv = jnp.concatenate(
            [
                d_queries.reshape(rows_here, width),
                d_keys.reshape(rows_here, width),
                d_values.reshape(rows_here, width),
            ],
            axis=1,
        ).astype(low)
        d_qkv_float = d_qkv.astype(jnp.float32)
        d_bias_q = jnp.sum(d_qkv_float[:, :width], axis=0)
        d_bias_v = jnp.sum(d_qkv_float[:, 2 * width :], axis=0)
        d_w_qkv = contract_rows(tok_rows, d_qkv)
        grad_input = ((contract_cols(d_qkv, w_qkv) + d_resid_one) * valid_col).reshape(
            seq_here, length, width
        )
        d_mats = jnp.concatenate(
            [
                piece.astype(low).reshape(-1, width)
                for piece in (d_w_qkv, d_w_out, d_w_up, d_w_down)
            ]
        )
        d_vecs = jnp.concatenate(
            [
                d_bias_q,
                d_bias_v,
                d_bias_out,
                d_gain_one,
                d_shift_one,
                d_bias_up,
                d_bias_down,
                d_gain_two,
                d_shift_two,
            ]
        )
        return grad_input, d_mats, d_vecs

    return output, plain_backward


def on_device(
    names,
    core,
    block_input,
    span_lengths,
    mlm_positions,
    mlm_labels,
    span_pairs,
    layer_mats,
    vectors,
    embedding,
    mom1_mats,
    mom2_mats,
    mom1_vecs,
    mom2_vecs,
    mom1_embed,
    mom2_embed,
):
    seq_here, length, width = block_input.shape
    rows_here = seq_here * length
    devices = 2 ** len(names)
    me = lax.axis_index(names)
    orders = bit_orders(names, core)
    slots = mlm_positions.shape[1]
    picks_here = seq_here * slots
    low = jnp.bfloat16

    third = layer_mats.shape[0] // width // 3
    by_kernel = third % 16 == 0
    vec_here = vectors.shape[0]
    mats_low = layer_mats.astype(low).reshape(3, third, width)

    labels_flat = mlm_labels.reshape(-1)
    common = jnp.concatenate(
        [
            value.astype(low)
            for value in (
                vectors,
                labels_flat // 256,
                labels_flat % 256,
                span_pairs // 256,
                span_pairs % 256,
                span_lengths // 4,
            )
        ]
    )
    ends = [vec_here, picks_here, picks_here, seq_here, seq_here, seq_here]
    common = jnp.pad(common, (0, width - common.shape[0]))
    others = jnp.arange(devices)[:, None]
    right, left = (me + 1) % devices, (me + devices - 1) % devices
    border = jnp.where(
        others == right,
        embedding[-width:].astype(low),
        jnp.where(others == left, embedding[:width].astype(low), jnp.zeros((), low)),
    )
    small = jnp.stack([jnp.broadcast_to(common, border.shape), border], axis=1)
    small_all = lax.all_to_all(small, names, 0, 0, tiled=True)
    starts = [sum(ends[:k]) for k in range(len(ends))]
    vecs_all, labels_high, labels_low, pairs_high, pairs_low, quarter_all = (
        small_all[:, 0, start : start + size] for start, size in zip(starts, ends)
    )

    embed_here = embedding.shape[0]
    shifted_rows = -(-embed_here // width)
    over = shifted_rows * width - embed_here
    shift = (me * (embed_here % width)) % width
    first_row = me * (embed_here // width) + (me * (embed_here % width)) // width

    def table_shard(embedding):
        return jnp.pad(embedding.astype(low), (0, over)).reshape(shifted_rows, width)

    from_left = lax.dynamic_index_in_dim(small_all[:, 1], left, 0, False)
    from_right = lax.dynamic_index_in_dim(small_all[:, 1], right, 0, False)
    right_rows = jnp.pad(from_right, (width - over, over)).reshape(2, width)
    vec_rows = vecs_all.reshape(-1).astype(jnp.float32).reshape(-1, width)

    def whole(high, small):
        return (high.astype(jnp.int32) * 256 + small.astype(jnp.int32)).reshape(-1)

    labels_all = whole(labels_high, labels_low)
    pairs_all = whole(pairs_high, pairs_low)
    quarter_all = quarter_all.astype(jnp.int32).reshape(-1)
    row_of = labels_all - first_row
    used = (jnp.arange(slots)[None, :] < quarter_all[:, None]).reshape(-1)
    seq_start = jnp.arange(seq_here, dtype=jnp.int32) * length

    def span_terms(cls_all):
        span_scale = 2.0 / math.sqrt(width)
        columns = jnp.arange(cls_all.shape[0])
        sims = contract_cols(cls_all, cls_all) * span_scale
        sims = jnp.where(columns[None, :] == columns[:, None], -1e30, sims)
        partner_hot = (columns[None, :] == pairs_all[:, None]).astype(jnp.float32)
        d_sims = (jax.nn.softmax(sims, axis=-1) - partner_hot).astype(low)
        mine = me * seq_here
        d_sims_rows = lax.dynamic_slice_in_dim(d_sims, mine, seq_here, 0)
        d_sims_cols = lax.dynamic_slice_in_dim(d_sims, mine, seq_here, 1)
        return (
            jnp.dot(d_sims_rows, cls_all, preferred_element_type=jnp.float32)
            + contract_rows(d_sims_cols, cls_all)
        ) * span_scale

    step_float = float(ADAM_STEP)

    def embed_step(grad_rows):
        grad = grad_rows.reshape(-1)[:embed_here]
        return grad, adam_step(embedding, grad, mom1_embed, mom2_embed, step_float, decay_rate)

    def vector_terms(d_vecs):
        return lax.all_to_all(d_vecs.reshape(devices, 1, vec_here), names, 0, 0, tiled=True)

    cut = width // 3
    columns = [slice(k * cut, (k + 1) * cut) for k in range(3)]
    back_orders = [order[::-1] for order in orders]
    if by_kernel:
        lone = me.astype(jnp.int32).reshape(1)
        lone_shift = shift.astype(jnp.int32).reshape(1)
        tok_rows = block_input.reshape(rows_here, width)
        relative = jnp.arange(devices, dtype=jnp.int32) ^ me.astype(jnp.int32)
        spots = jnp.stack(
            [
                sum(
                    ((relative & device_mask(name, names)) != 0).astype(jnp.int32)
                    << (len(names) - 1 - k)
                    for k, name in enumerate(order)
                )
                for order in back_orders
            ],
            axis=1,
        ).reshape(-1)
        places = jnp.concatenate(
            [
                (mlm_positions + seq_start[:, None]).reshape(-1),
                seq_start,
                jnp.full((16 - seq_here,), -1, jnp.int32),
            ]
        )
        ends = jnp.pad(
            jnp.concatenate([from_left[None], right_rows]).astype(jnp.float32), ((0, 5), (0, 0))
        )
        table_rows = -(-(shifted_rows + 1) // 128) * 128
        labels = jnp.pad(
            jnp.stack([row_of.astype(jnp.float32), used.astype(jnp.float32)]), ((0, 6), (0, 0))
        )

        def prepare(embedding, ends, *others):
            shifted = table_shard(embedding)
            return *call_table(lone_shift, shifted, ends, table_rows, embed_here), *others

        gathered, (table, owned, labels, vec_rows) = gather_relative(
            mats_low[:, None], orders, names, (embedding, ends, labels, vec_rows), prepare
        )
        *heads, saved = call_forward(
            lone, span_lengths, places[None], tok_rows, vec_rows, gathered, devices, seq_here
        )
        heads_all, _ = gather_relative(heads, orders, names)
        picked, expo, stats = call_logits(
            lone, lone_shift, table, heads_all, picks_here, embed_here, devices
        )
        stats = lax.all_to_all(stats, names, 0, 0, tiled=True)
        mix, hot_rows, own = call_mix(expo, labels, owned)
        plan = tuple(tuple(device_mask(name, names) for name in order) for order in back_orders)
        scale, *sinks = call_terms(lone, stats, mix, hot_rows, own, labels, plan, picks_here)
        d_cls = span_terms(picked[:, picks_here : picks_here + seq_here].reshape(-1, width))
        d_parts, _ = reduce_relative(
            sinks[0::3], list(zip(sinks[1::3], sinks[2::3])), back_orders
        )
        d_parts = [add_terms([term[0] for term in terms]) for terms in d_parts]
        top = jnp.concatenate(
            [jnp.concatenate(d_parts, axis=1), jnp.pad(d_cls, ((0, 16 - seq_here), (0, 0)))]
        )
        grad_input, d_vecs, *sinks = call_backward(
            span_lengths, spots, places[None], tok_rows, vec_rows, top, saved, third, seq_here
        )
        grad_input = grad_input.reshape(seq_here, length, width)
        def table_grad(state):
            expo, picked, d_vecs = state
            grad_embed = call_embed(
                lone_shift, expo, scale, labels, picked, picks_here, shifted_rows
            )
            grad_embed, d_vecs = lax.optimization_barrier((grad_embed, d_vecs))
            return grad_embed, vector_terms(d_vecs)

        def table_step(state):
            grad_embed, terms = state
            return *embed_step(grad_embed), jnp.sum(terms, axis=(0, 1))

        terms, (grad_embed, step_embed, grad_vecs) = reduce_relative(
            sinks[0::3],
            list(zip(sinks[1::3], sinks[2::3])),
            back_orders,
            (expo, picked, d_vecs),
            {0: table_grad, len(names) - 2: table_step},
            1,
        )
        grad_mats, step_mats = call_step(layer_mats, mom1_mats, mom2_mats, terms)
    else:
        same_row = (jnp.arange(width) < width - shift)[None, :]
        tall = jnp.concatenate(
            [from_left[None], table_shard(embedding), jnp.zeros((1, width), low)]
        )
        tall = tall.at[shifted_rows : shifted_rows + 2].add(right_rows)
        lanes = jnp.arange(width)
        turn = ((lanes[:, None] + shift) % width == lanes[None, :]).astype(low)
        rolled = jnp.where(same_row, tall[1:], tall[:-1])
        table = jnp.dot(rolled, turn, preferred_element_type=jnp.float32).astype(low)
        row_start = jnp.arange(shifted_rows + 1) * width - shift
        owned = (row_start >= 0) & (row_start < embed_here)
        touched = (row_start + width > 0) & (row_start < embed_here)
        gathered = [gather_bits(mats_low[k], orders[k], names) for k in range(3)]
        mats_all = jnp.stack(gathered, axis=1).reshape(-1)
        output, plain_backward = plain_forward(
            mats_all, vec_rows.reshape(-1), block_input, span_lengths
        )
        output_seq = output.reshape(seq_here, length, width)
        picked_here = jnp.take_along_axis(output_seq, mlm_positions[:, :, None], axis=1)
        heads = jnp.concatenate([picked_here.reshape(-1, width), output_seq[:, 0, :]]).astype(low)
        heads_all = jnp.concatenate(
            [gather_bits(heads[:, c], order, names) for c, order in zip(columns, orders)], axis=2
        )
        picked = heads_all[:, :picks_here, :].reshape(-1, width)
        logits = contract_cols(picked, table)
        masked = jnp.where(owned[None, :], logits, -jnp.inf)
        part_max = jnp.max(masked, axis=-1)
        part_sum = jnp.sum(jnp.exp(masked - part_max[:, None]), axis=-1)
        full_max = lax.pmax(part_max, names)
        full_sum = lax.psum(part_sum * jnp.exp(part_max - full_max), names)
        hot = row_of[:, None] == jnp.arange(shifted_rows + 1)[None, :]
        probs = jnp.exp(logits - full_max[:, None]) / full_sum[:, None]
        d_logits = jnp.where(
            used[:, None] & touched[None, :], probs - hot.astype(jnp.float32), 0.0
        ).astype(low)
        d_picked = jnp.dot(
            d_logits, jnp.where(owned[:, None], table, 0), preferred_element_type=jnp.float32
        )
        blocks = d_picked.astype(low).reshape(devices, picks_here, width)
        d_picked = jnp.concatenate(
            [
                reduce_bits(blocks[:, :, c], order, names)
                for c, order in zip(columns, back_orders)
            ],
            axis=1,
        ).astype(jnp.float32)
        select = (mlm_positions[:, :, None] == jnp.arange(length)[None, None, :]).astype(
            jnp.float32
        )
        d_output_seq = jnp.einsum(
            "gor,gon->grn",
            select,
            d_picked.reshape(seq_here, slots, width),
            precision=lax.Precision.HIGHEST,
        )
        d_cls = span_terms(heads_all[:, picks_here:, :].reshape(-1, width))
        d_output_seq = d_output_seq.at[:, 0, :].add(d_cls)
        valid = jnp.arange(length)[None, :] < span_lengths[:, None]
        d_output = d_output_seq.reshape(rows_here, width) * valid.reshape(rows_here, 1)
        grad_input, d_mats, d_vecs = plain_backward(d_output)
        d_mats = d_mats.reshape(devices, 3, third, width)
        summed = [
            reduce_bits(d_mats[:, k], back_orders[k], names).astype(jnp.float32) for k in range(3)
        ]
        picked_turned = jnp.dot(picked, turn.T, preferred_element_type=jnp.float32).astype(low)
        d_rolled = contract_rows(d_logits, picked_turned)
        grad_embed, step_embed = embed_step(jnp.where(same_row, d_rolled[:-1], d_rolled[1:]))
        grad_vecs = jnp.sum(vector_terms(d_vecs), axis=(0, 1))
        grad_mats = jnp.concatenate(summed).reshape(-1)
        step_mats = adam_step(layer_mats, grad_mats, mom1_mats, mom2_mats, step_float, decay_rate)
    step_vecs = adam_step(vectors, grad_vecs, mom1_vecs, mom2_vecs, step_float, 0.0)
    return (grad_input, grad_mats, grad_vecs, grad_embed, step_mats, step_vecs, step_embed)


def solution(mesh):
    fsdp_bits = mesh.shape["fsdp"].bit_length() - 1
    rep_bits = mesh.shape["rep"].bit_length() - 1
    names = tuple(f"f{k}" for k in reversed(range(fsdp_bits)))
    core = names[-1]
    names = names + tuple(f"r{k}" for k in reversed(range(rep_bits)))
    bits = Mesh(mesh.devices.reshape((2,) * len(names)), names)
    seqs = P(names, None, None)
    pairs = P(names, None)
    flat = P(names)
    return jax.shard_map(
        functools.partial(on_device, names, core),
        mesh=bits,
        in_specs=(seqs, flat, pairs, pairs) + (flat,) * 10,
        out_specs=(seqs,) + (flat,) * 6,
        check_vma=False,
    )
```

```python
import functools
import math

import jax
import jax.numpy as jnp
from jax import lax
from jax.experimental import pallas as pl
from jax.experimental.pallas import tpu as pltpu
from jax.sharding import Mesh, PartitionSpec as P

D = 768
FF = 3072
HEAD_DIM = 64
VOCAB = 30522
ADAM_STEP = 10


norm_eps = 1e-12
beta_one = 0.9
beta_two = 0.999
adam_eps = 1e-06
decay_rate = 0.01


def split_mats(flat):
    first = 3 * D * D
    second = first + D * D
    third = second + D * FF
    return (
        flat[:first].reshape(D, 3 * D),
        flat[first:second].reshape(D, D),
        flat[second:third].reshape(D, FF),
        flat[third:].reshape(FF, D),
    )


def split_vecs(flat):
    widths_list = [D, D, D, D, D, FF, D, D, D]
    pieces = []
    offset = 0
    for piece_width in widths_list:
        pieces.append(flat[offset : offset + piece_width].astype(jnp.float32))
        offset = offset + piece_width
    return pieces


def center_scale(resid):
    center = resid - jnp.mean(resid, axis=-1, keepdims=True)
    inverse = lax.rsqrt(jnp.mean(center * center, axis=-1, keepdims=True) + norm_eps)
    return (center * inverse, inverse)


def norm_back(d_normed, normed, inverse):
    return inverse * (
        d_normed
        - jnp.mean(d_normed, axis=-1, keepdims=True)
        - normed * jnp.mean(d_normed * normed, axis=-1, keepdims=True)
    )


def gelu_slope(value):
    return (
        0.5 * (1.0 + lax.erf(value * 0.7071067811865476))
        + value * jnp.exp(-0.5 * value * value) * 0.3989422804014327
    )


def contract_rows(left, right):
    return lax.dot_general(
        left, right, (((0,), (0,)), ((), ())), preferred_element_type=jnp.float32
    )


def contract_cols(left, right):
    return lax.dot_general(
        left, right, (((1,), (1,)), ((), ())), preferred_element_type=jnp.float32
    )


def adam_step(weight, grad, first, second, step_float, decay):
    first_new = beta_one * first + (1.0 - beta_one) * grad
    second_new = beta_two * second + (1.0 - beta_two) * grad * grad
    first_hat = first_new / (1.0 - beta_one**step_float)
    second_hat = second_new / (1.0 - beta_two**step_float)
    return first_hat / (jnp.sqrt(second_hat) + adam_eps) + decay * weight


def flip(value, name):
    return lax.ppermute(value, name, [(0, 1), (1, 0)])


def gather_bits(shard, order, names):
    grown = shard
    for name in order:
        other = flip(grown, name)
        first = lax.axis_index(name) == 0
        grown = jnp.stack([jnp.where(first, grown, other), jnp.where(first, other, grown)])
    axes = list(reversed(order))
    rank = len(axes)
    turn = [axes.index(name) for name in names] + list(range(rank, grown.ndim))
    return grown.transpose(turn).reshape((2**rank,) + shard.shape)


def reduce_bits(blocks, order, names):
    left = list(names)
    held = blocks.reshape((2,) * len(left) + blocks.shape[1:])
    for name in order:
        axis = left.index(name)
        here = lax.axis_index(name)
        send = lax.dynamic_index_in_dim(held, 1 - here, axis, keepdims=False)
        keep = lax.dynamic_index_in_dim(held, here, axis, keepdims=False)
        other = flip(send, name)
        held = (keep.astype(jnp.float32) + other.astype(jnp.float32)).astype(blocks.dtype)
        left.remove(name)
    return held


def bit_orders(names, core):
    outer = [name for name in names if name != core]
    count = len(outer)
    if count == 4:
        picks = ((0, 3, 2, 1), (0, 2, 1, 3), (0, 1, 3, 2))
        return [[outer[k] for k in pick] + [core] for pick in picks]
    step = max(1, count // 3)
    return [outer[step * k :] + outer[: step * k] + [core] for k in range(3)]


def device_mask(name, names):
    return 1 << (len(names) - 1 - names.index(name))


def gather_relative(shards, orders, names, early=(), exchange=None, work=None):
    held = []
    for number, (shard, order) in enumerate(zip(shards, orders)):
        grown, masks = shard, [0]
        for k, name in enumerate(order[:-2]):
            grown = lax.optimization_barrier(jnp.concatenate([grown, flip(grown, name)]))
            if exchange is not None and k == 0 and number == len(orders) - 1:
                grown, given = lax.optimization_barrier((grown, early[-1]))
                early = (*early[:-1], exchange(given))
            masks = masks + [mask | device_mask(name, names) for mask in masks]
        held.append((grown, masks))
    grown_all = [grown for grown, _ in held]
    others = [flip(grown, order[-2]) for grown, order in zip(grown_all, orders)]
    if work is not None:
        late, early = lax.optimization_barrier((grown_all, early))
        grown_all, early = lax.optimization_barrier((late, work(*early)))
    gathered = []
    for grown, other, (_, masks), order in zip(grown_all, others, held, orders):
        bit = device_mask(order[-2], names)
        pieces = [(grown, masks), (other, [mask | bit for mask in masks])]
        bit = device_mask(order[-1], names)
        pieces = pieces + [
            (flip(piece, order[-1]), [mask | bit for mask in own]) for piece, own in pieces
        ]
        gathered.append(pieces)
    return gathered, early


def add_terms(terms):
    total = terms[0].astype(jnp.float32)
    for term in terms[1:]:
        total = total + term.astype(jnp.float32)
    return total


def reduce_relative(keeps, sends, orders, state=None, works=(), early_sums=None):
    works = dict(works)
    sends = list(sends)
    terms_all = [[keep] for keep in keeps]
    whole_all = [[keep] for keep in keeps]
    for step in range(len(orders[0])):
        for k, order in enumerate(orders):
            half = terms_all[k][0].shape[0] // 2
            if step == 0:
                urgent, rest = (flip(send, order[step]) for send in sends[k])
                whole_all[k].append(rest)
            else:
                other = flip(sends[k], order[step])
                urgent, rest = other[half:], other[:half]
                whole_all[k].append(other)
            if half:
                upper = [term[half:] for term in terms_all[k]] + [urgent]
                sends[k] = add_terms(upper).astype(urgent.dtype)
                terms_all[k] = [term[:half] for term in terms_all[k]] + [rest]
            else:
                terms_all[k] = terms_all[k] + [urgent]
        if step == early_sums:
            left = terms_all[0][0].shape[0]
            for k in range(len(orders)):
                sends[k], terms = lax.optimization_barrier((sends[k], whole_all[k]))
                terms_all[k] = [add_terms([term[:left] for term in terms])]
                whole_all[k] = list(terms_all[k])
        if step in works:
            sends[-1], state = lax.optimization_barrier((sends[-1], state))
            state = works[step](state)
    return whole_all, state


def dot_nn(left, right):
    return lax.dot_general(
        left, right, (((1,), (0,)), ((), ())), preferred_element_type=jnp.float32
    )


def interleave(count, rows):
    span = rows // count
    to = lax.broadcasted_iota(jnp.int32, (rows, rows), 0)
    source = lax.broadcasted_iota(jnp.int32, (rows, rows), 1)
    return (source == count * lax.rem(to, span) + lax.div(to, span)).astype(jnp.bfloat16)


def deinterleave(count, rows):
    span = rows // count
    source = lax.broadcasted_iota(jnp.int32, (rows, rows), 1)
    to = lax.broadcasted_iota(jnp.int32, (rows, rows), 0)
    return (to == count * lax.rem(source, span) + lax.div(source, span)).astype(jnp.bfloat16)


def valid_rows(len_ref, rows, seq_here):
    length = rows // seq_here
    row = lax.broadcasted_iota(jnp.int32, (rows, 1), 0)
    valid = jnp.zeros((rows, 1), jnp.float32)
    for seq in range(seq_here):
        inside = (row >= seq * length) & (row < seq * length + len_ref[seq])
        valid = jnp.where(inside, 1.0, valid)
    return valid


def stack_pair(value):
    lane = lax.broadcasted_iota(jnp.int32, value.shape, 1)
    zero = jnp.zeros_like(value)
    left = lane < HEAD_DIM
    return jnp.concatenate([jnp.where(left, value, zero), jnp.where(left, zero, value)], axis=0)


def join_pair(stacked):
    half = stacked.shape[0] // 2
    lane = lax.broadcasted_iota(jnp.int32, (half, stacked.shape[1]), 1)
    return jnp.where(lane < HEAD_DIM, stacked[:half], stacked[half:])


def pair_scores(stacked, keys, limit):
    raw = contract_cols(stacked, keys) * HEAD_DIM ** (-0.5)
    column = lax.broadcasted_iota(jnp.int32, raw.shape, 1)
    return jnp.where(column < limit, raw, -1e30)


def center_rows(resid):
    center = resid - jnp.mean(resid, axis=-1, keepdims=True)
    inverse = lax.rsqrt(jnp.mean(center * center, axis=-1, keepdims=True) + norm_eps)
    return center * inverse, inverse


def gelu_phi(value):
    return 0.5 * (1.0 + lax.erf(value * 0.7071067811865476))


def forward_kernel(plan, planes, seq_here, *refs):
    me_ref, len_ref, place_ref, x_ref, vec_ref = refs[:5]
    blocks = refs[5 : 5 + len(plan)]
    heads_refs = refs[5 + len(plan) : 8 + len(plan)]
    wall_ref, qkv_ref, att_ref, n1_ref, pre_ref, n2_ref, stat_ref = refs[
        8 + len(plan) : 15 + len(plan)
    ]
    raw, turned, qkv, att, n1, pre_all, in_sem, out_sem = refs[15 + len(plan) :]
    rows, width = x_ref.shape
    length = rows // seq_here
    pairs = width // (2 * HEAD_DIM)
    up = 4 * width
    me = me_ref[0]
    for first in (True, False):
        for (part, unit, masks), block in zip(plan, blocks):
            for place, mask in enumerate(masks):
                device = me ^ mask
                early = device < planes

                @pl.when(early if first else jnp.logical_not(early))
                def _(device=device, part=part, unit=unit, block=block, place=place, first=first):
                    row = pl.multiple_of((3 * device + part) * unit, 16)
                    pltpu.make_async_copy(
                        block.at[place], raw.at[pl.ds(row, unit)], in_sem.at[0 if first else 1]
                    ).start()

    copies = []

    def save(source, target):
        copy = pltpu.make_async_copy(source, target, out_sem.at[len(copies)])
        copy.start()
        copies.append(copy)

    valid = valid_rows(len_ref, rows, seq_here)
    x = (x_ref[...].astype(jnp.float32) * valid).astype(jnp.bfloat16)
    split3, split4 = interleave(3, 384), interleave(4, 256)
    arrived = raw.at[0 : 3 * width]
    pltpu.make_async_copy(arrived, arrived, in_sem.at[0]).wait()

    for b in range(width // 128):
        block = dot_nn(split3, raw[384 * b : 384 * b + 384, :]).astype(jnp.bfloat16)
        for p in range(3):
            turned[width * p + 128 * b : width * p + 128 * b + 128, :] = block[
                128 * p : 128 * p + 128
            ]
    save(turned.at[0 : 3 * width], wall_ref.at[0 : 3 * width])
    for p, bias in ((0, 0), (1, None), (2, 1)):
        value = dot_nn(x, turned[width * p : width * (p + 1), :])
        if bias is not None:
            value = value + vec_ref[bias : bias + 1, :]
        qkv[:, width * p : width * (p + 1)] = value.astype(jnp.bfloat16)
    save(qkv, qkv_ref)

    stats = jnp.zeros((2 * length, 128), jnp.float32)
    lane = lax.broadcasted_iota(jnp.int32, stats.shape, 1)
    for seq in range(seq_here):
        here = slice(seq * length, (seq + 1) * length)
        for g in range(pairs):
            cols = [slice(width * p + 128 * g, width * p + 128 * g + 128) for p in range(3)]
            query, key, value = (qkv[here, c] for c in cols)
            scores = pair_scores(stack_pair(query), key, len_ref[seq])
            top = jnp.max(scores, axis=-1, keepdims=True)
            expo = jnp.exp(scores - top)
            total = jnp.sum(expo, axis=-1, keepdims=True)
            stats = jnp.where(lane == seq * pairs + g, top + jnp.log(total), stats)
            probs = (expo / total).astype(jnp.bfloat16)
            att[here, 128 * g : 128 * g + 128] = join_pair(dot_nn(probs, value)).astype(
                jnp.bfloat16
            )
    save(att, att_ref)
    arrived = raw.at[3 * width : 3 * up]
    pltpu.make_async_copy(arrived, arrived, in_sem.at[1]).wait()
    save(raw.at[3 * width : up], wall_ref.at[3 * width : up])
    save(raw.at[2 * up : 3 * up], wall_ref.at[2 * up : 3 * up])

    branch = dot_nn(att[...], raw[3 * width : up, :]) + vec_ref[2:3, :]
    for b in range(width // 64):
        block = dot_nn(split4, raw[up + 256 * b : up + 256 * b + 256, :]).astype(jnp.bfloat16)
        for p in range(4):
            row = width * (3 + p) + 64 * b
            turned[row : row + 64, :] = block[64 * p : 64 * p + 64]
    save(turned.at[3 * width : 7 * width], wall_ref.at[up : 2 * up])
    normed, inverse = center_rows(x.astype(jnp.float32) + branch)
    n1[...] = normed
    save(n1, n1_ref)
    stat_one = seq_here * pairs
    hidden = normed * vec_ref[3:4, :] + vec_ref[4:5, :]
    hidden_low = hidden.astype(jnp.bfloat16)
    total = hidden + vec_ref[9:10, :]
    for p in range(4):
        pre = dot_nn(hidden_low, turned[width * (3 + p) : width * (4 + p), :])
        pre = pre + vec_ref[5 + p : 6 + p, :]
        pre_all[p] = pre
        save(pre_all.at[p], pre_ref.at[p])
        act = (pre * gelu_phi(pre)).astype(jnp.bfloat16)
        total = total + dot_nn(act, raw[2 * up + width * p : 2 * up + width * (p + 1), :])
    normed, inverse_two = center_rows(total)
    n2_ref[...] = normed
    wide = lax.broadcasted_iota(jnp.int32, (rows, 128), 1)
    ends = jnp.where(
        wide == stat_one, inverse, jnp.where(wide == stat_one + 1, inverse_two, 0.0)
    )
    stat_ref[0] = stats
    stat_ref[1] = ends
    output = ((normed * vec_ref[10:11, :] + vec_ref[11:12, :]) * valid).astype(jnp.bfloat16)
    spot = lax.broadcasted_iota(jnp.int32, (rows, place_ref.shape[1]), 0)
    choose = (spot == place_ref[...]).astype(jnp.bfloat16)
    heads = contract_rows(choose, output).astype(jnp.bfloat16)
    cut = width // 3
    for k, heads_ref in enumerate(heads_refs):
        heads_ref[0] = heads[:, k * cut : (k + 1) * cut]
    for copy in copies:
        copy.wait()


def send_block(source, sinks, spots, device, part, out_sem):
    spot = spots[3 * device + part]
    half = sinks[0].shape[0]

    def copy(sink, place):
        pltpu.make_async_copy(source, sink.at[place], out_sem).start()

    keep, urgent, rest = sinks[3 * part : 3 * part + 3]
    pl.when(spot < half)(functools.partial(copy, keep, spot))
    pl.when((spot >= half) & (spot < half + half // 2))(
        functools.partial(copy, rest, spot - half)
    )
    pl.when(spot >= half + half // 2)(functools.partial(copy, urgent, spot - half - half // 2))


def sink_shapes(devices, block, dtype):
    half = devices // 2
    return [
        jax.ShapeDtypeStruct((count,) + block, dtype)
        for _ in range(3)
        for count in (half, half // 2, half // 2)
    ]


def wait_sinks(sinks, out_sem):
    for sink in sinks:
        pltpu.make_async_copy(sink, sink, out_sem).wait()


def backward_kernel(unit, seq_here, *refs):
    len_ref, spots, place_ref, x_ref, vec_ref, top_ref = refs[:6]
    wall_ref, qkv_ref, att_ref, n1_ref, pre_ref, n2_ref, stat_ref = refs[6:13]
    gin_ref, dvec_ref = refs[13:15]
    sinks = refs[15:24]
    wall, grads, parts, dqkv, qkv, att, n1, pre_all, in_sem, out_sem = refs[24:]
    rows, width = x_ref.shape
    length = rows // seq_here
    pairs = width // (2 * HEAD_DIM)
    low = jnp.bfloat16
    up = 4 * width
    ranges = [(n1_ref, n1)]
    for p in range(4):
        for first in (2 * up, up):
            rows_p = slice(first + width * p, first + width * (p + 1))
            ranges.append((wall_ref.at[rows_p], wall.at[rows_p]))
        ranges.append((pre_ref.at[p], pre_all.at[p]))
    out = slice(3 * width, up)
    ranges += [(att_ref, att), (wall_ref.at[out], wall.at[out]), (qkv_ref, qkv)]
    ranges += [(wall_ref.at[0 : 3 * width], wall.at[0 : 3 * width])]
    loads = [
        pltpu.make_async_copy(source, target, in_sem.at[k])
        for k, (source, target) in enumerate(ranges)
    ]
    for load in loads:
        load.start()

    def emit(first, last):
        for u in range(first // unit, last // unit):
            block = grads.at[u * unit : (u + 1) * unit]
            send_block(block, sinks, spots, u // 3, u % 3, out_sem)

    valid = valid_rows(len_ref, rows, seq_here)
    x = (x_ref[...].astype(jnp.float32) * valid).astype(low)
    stat_one = seq_here * pairs
    wide = lax.broadcasted_iota(jnp.int32, (rows, 128), 1)
    ends = stat_ref[1]
    inverse_one = jnp.sum(jnp.where(wide == stat_one, ends, 0.0), axis=-1, keepdims=True)
    inverse_two = jnp.sum(jnp.where(wide == stat_one + 1, ends, 0.0), axis=-1, keepdims=True)

    spot = lax.broadcasted_iota(jnp.int32, (rows, place_ref.shape[1]), 0)
    choose = (spot == place_ref[...]).astype(jnp.float32)
    d_output = valid * lax.dot_general(
        choose,
        top_ref[...],
        (((1,), (0,)), ((), ())),
        precision=lax.Precision.HIGHEST,
        preferred_element_type=jnp.float32,
    )
    normed = n2_ref[...]

    def sums(row, value):
        dvec_ref[row : row + 1, :] = jnp.sum(value, axis=0, keepdims=True)

    sums(10, d_output * normed)
    sums(11, d_output)
    d_resid = norm_back(d_output * vec_ref[10:11, :], normed, inverse_two)
    d_ffn = d_resid.astype(low)
    sums(9, d_ffn.astype(jnp.float32))
    d_hidden = d_resid
    loads[0].wait()
    normed = n1[...]
    hidden_low = (normed * vec_ref[3:4, :] + vec_ref[4:5, :]).astype(low)
    for p in range(4):
        for load in loads[1 + 3 * p : 4 + 3 * p]:
            load.wait()
        pre = pre_all[p]
        phi = gelu_phi(pre)
        act = (pre * phi).astype(low)
        down = slice(2 * up + width * p, 2 * up + width * (p + 1))
        grads[down, :] = contract_rows(act, d_ffn).astype(low)
        emit(down.start, down.stop)
        slope = phi + pre * jnp.exp(-0.5 * pre * pre) * 0.3989422804014327
        d_pre = (contract_cols(d_ffn, wall[down, :]) * slope).astype(low)
        sums(5 + p, d_pre.astype(jnp.float32))
        parts[width * p : width * (p + 1), :] = contract_rows(hidden_low, d_pre).astype(low)
        d_hidden = d_hidden + contract_cols(d_pre, wall[up + width * p : up + width * (p + 1), :])
    merge4 = deinterleave(4, 256)
    for b in range(width // 64):
        block = jnp.concatenate(
            [parts[width * p + 64 * b : width * p + 64 * b + 64, :] for p in range(4)], axis=0
        )
        grads[up + 256 * b : up + 256 * b + 256, :] = dot_nn(merge4, block).astype(low)
        if b % 3 == 2:
            emit(up + 256 * (b - 2), up + 256 * (b + 1))

    sums(3, d_hidden * normed)
    sums(4, d_hidden)
    d_resid = norm_back(d_hidden * vec_ref[3:4, :], normed, inverse_one)
    d_branch = d_resid.astype(low)
    sums(2, d_branch.astype(jnp.float32))
    for load in loads[13:]:
        load.wait()
    grads[3 * width : up, :] = contract_rows(att[...], d_branch).astype(low)
    emit(3 * width, up)
    d_att = contract_cols(d_branch, wall[3 * width : up, :]).astype(low)
    lane = lax.broadcasted_iota(jnp.int32, (2 * length, 128), 1)
    stats = stat_ref[0]
    for seq in range(seq_here):
        here = slice(seq * length, (seq + 1) * length)
        for g in range(pairs):
            cols = [slice(width * p + 128 * g, width * p + 128 * g + 128) for p in range(3)]
            query, key, value = (qkv[here, c] for c in cols)
            query = stack_pair(query)
            log_sum = jnp.sum(
                jnp.where(lane == seq * pairs + g, stats, 0.0), axis=-1, keepdims=True
            )
            probs = jnp.exp(pair_scores(query, key, len_ref[seq]) - log_sum)
            d_heads = stack_pair(d_att[here, 128 * g : 128 * g + 128])
            d_probs = contract_cols(d_heads, value)
            dqkv[here, cols[2]] = contract_rows(probs.astype(low), d_heads).astype(low)
            delta = jnp.sum(d_probs * probs, axis=-1, keepdims=True)
            d_scores = (probs * (d_probs - delta)).astype(low)
            scale = HEAD_DIM ** (-0.5)
            dqkv[here, cols[0]] = (join_pair(dot_nn(d_scores, key)) * scale).astype(low)
            dqkv[here, cols[1]] = (contract_rows(d_scores, query) * scale).astype(low)
    sums(0, dqkv[:, :width].astype(jnp.float32))
    sums(1, dqkv[:, 2 * width :].astype(jnp.float32))
    for p in range(3):
        d_part = dqkv[:, width * p : width * (p + 1)]
        parts[width * p : width * (p + 1), :] = contract_rows(x, d_part).astype(low)
    merge3 = deinterleave(3, 384)
    for b in range(width // 128):
        block = jnp.concatenate(
            [parts[width * p + 128 * b : width * p + 128 * b + 128, :] for p in range(3)], axis=0
        )
        grads[384 * b : 384 * b + 384, :] = dot_nn(merge3, block).astype(low)
        if b % 2 == 1:
            emit(384 * (b - 1), 384 * (b + 1))
    total = d_resid
    for p in range(3):
        d_part = dqkv[:, width * p : width * (p + 1)]
        total = total + contract_cols(d_part, wall[width * p : width * (p + 1), :])
    gin_ref[...] = total * valid
    wait_sinks(sinks, out_sem)


def call_forward(me, lengths, places, rows, vecs, gathered, devices, seq_here):
    count, width = rows.shape
    pieces = [(part, piece, masks) for part, own in enumerate(gathered) for piece, masks in own]
    plan = tuple((part, piece.shape[1], tuple(masks)) for part, piece, masks in pieces)
    total = 12 * width
    vmem = pl.BlockSpec(memory_space=pltpu.VMEM)
    smem = pl.BlockSpec(memory_space=pltpu.SMEM)
    hbm = pl.BlockSpec(memory_space=pl.ANY)
    low, full = jnp.bfloat16, jnp.float32
    outs = pl.pallas_call(
        functools.partial(forward_kernel, plan, devices // 4, seq_here),
        out_shape=[
            *[jax.ShapeDtypeStruct((1, places.shape[1], width // 3), low)] * 3,
            jax.ShapeDtypeStruct((total, width), low),
            jax.ShapeDtypeStruct((count, 3 * width), low),
            jax.ShapeDtypeStruct((count, width), low),
            jax.ShapeDtypeStruct((count, width), full),
            jax.ShapeDtypeStruct((4, count, width), full),
            jax.ShapeDtypeStruct((count, width), full),
            jax.ShapeDtypeStruct((2, count, 128), full),
        ],
        in_specs=[smem, smem, vmem, vmem, vmem] + [hbm] * len(pieces),
        out_specs=[vmem] * 3 + [hbm] * 5 + [vmem] * 2,
        scratch_shapes=[
            pltpu.VMEM((total, width), low),
            pltpu.VMEM((7 * width, width), low),
            pltpu.VMEM((count, 3 * width), low),
            pltpu.VMEM((count, width), low),
            pltpu.VMEM((count, width), full),
            pltpu.VMEM((4, count, width), full),
            pltpu.SemaphoreType.DMA((2,)),
            pltpu.SemaphoreType.DMA((11,)),
        ],
        compiler_params=pltpu.CompilerParams(vmem_limit_bytes=58 * 2**20),
        cost_estimate=pl.CostEstimate(
            flops=2 * count * total * width, bytes_accessed=48 * 2**20, transcendentals=0
        ),
    )(me, lengths, places, rows, vecs, *[piece for _, piece, _ in pieces])
    return *outs[:3], outs[3:]


def call_backward(lengths, spots, places, rows, vecs, top, saved, unit, seq_here):
    count, width = rows.shape
    total = 12 * width
    vmem = pl.BlockSpec(memory_space=pltpu.VMEM)
    smem = pl.BlockSpec(memory_space=pltpu.SMEM)
    hbm = pl.BlockSpec(memory_space=pl.ANY)
    low, full = jnp.bfloat16, jnp.float32
    return pl.pallas_call(
        functools.partial(backward_kernel, unit, seq_here),
        out_shape=[
            jax.ShapeDtypeStruct((count, width), full),
            jax.ShapeDtypeStruct((12, width), full),
        ]
        + sink_shapes(total // unit // 3, (unit, width), low),
        in_specs=[smem, smem, vmem, vmem, vmem, vmem] + [hbm] * 5 + [vmem] * 2,
        out_specs=[vmem, vmem] + [hbm] * 9,
        scratch_shapes=[
            pltpu.VMEM((total, width), low),
            pltpu.VMEM((total, width), low),
            pltpu.VMEM((4 * width, width), low),
            pltpu.VMEM((count, 3 * width), low),
            pltpu.VMEM((count, 3 * width), low),
            pltpu.VMEM((count, width), low),
            pltpu.VMEM((count, width), full),
            pltpu.VMEM((4, count, width), full),
            pltpu.SemaphoreType.DMA((17,)),
            pltpu.SemaphoreType.DMA,
        ],
        compiler_params=pltpu.CompilerParams(vmem_limit_bytes=58 * 2**20),
        cost_estimate=pl.CostEstimate(
            flops=4 * count * total * width, bytes_accessed=48 * 2**20, transcendentals=0
        ),
    )(lengths, spots, places, rows, vecs, top, *saved)


def turn_lanes(shift, width):
    source = lax.broadcasted_iota(jnp.int32, (width, width), 0) + shift
    source = jnp.where(source >= width, source - width, source)
    return (source == lax.broadcasted_iota(jnp.int32, (width, width), 1)).astype(jnp.bfloat16)


def table_kernel(embed_here, shift_ref, rows_ref, ends_ref, table_ref, owned_ref, tall):
    count, width = table_ref.shape
    here = rows_ref.shape[0]
    shift = shift_ref[0]
    tall[here:, :] = jnp.zeros((tall.shape[0] - here, width), jnp.float32)
    tall[8 : 8 + here, :] = rows_ref[...].astype(jnp.float32)
    tall[7:8, :] = ends_ref[0:1, :]
    tall[7 + here : 8 + here, :] = tall[7 + here : 8 + here, :] + ends_ref[1:2, :]
    tall[8 + here : 9 + here, :] = ends_ref[2:3, :]
    lane = lax.broadcasted_iota(jnp.int32, (count, width), 1)
    rolled = jnp.where(lane < width - shift, tall[8 : 8 + count, :], tall[7 : 7 + count, :])
    table = dot_nn(rolled.astype(jnp.bfloat16), turn_lanes(shift, width))
    start = lax.broadcasted_iota(jnp.int32, (count, 1), 0) * width - shift
    owned = (start >= 0) & (start < embed_here)
    table_ref[...] = table.astype(jnp.bfloat16)
    owned_ref[...] = jnp.where(owned, table, 0.0).astype(jnp.bfloat16)


def call_table(shift, rows, ends, count, embed_here):
    width = rows.shape[1]
    vmem = pl.BlockSpec(memory_space=pltpu.VMEM)
    smem = pl.BlockSpec(memory_space=pltpu.SMEM)
    return pl.pallas_call(
        functools.partial(table_kernel, embed_here),
        out_shape=[jax.ShapeDtypeStruct((count, width), jnp.bfloat16)] * 2,
        in_specs=[smem, vmem, vmem],
        out_specs=[vmem] * 2,
        scratch_shapes=[pltpu.VMEM((count + 16, width), jnp.float32)],
        compiler_params=pltpu.CompilerParams(vmem_limit_bytes=22 * 2**20),
        cost_estimate=pl.CostEstimate(
            flops=32 * count * width * width, bytes_accessed=40 * 2**20, transcendentals=0
        ),
    )(shift, rows, ends)


def eye_mask():
    return lax.broadcasted_iota(jnp.int32, (128, 128), 0) == lax.broadcasted_iota(
        jnp.int32, (128, 128), 1
    )


def to_row(column, eye):
    return jnp.concatenate(
        [
            jnp.sum(jnp.where(eye, column[k : k + 128], 0.0), axis=0, keepdims=True)
            for k in range(0, column.shape[0], 128)
        ],
        axis=1,
    )


def to_column(row, eye):
    return jnp.concatenate(
        [
            jnp.sum(jnp.where(eye, row[:, k : k + 128], 0.0), axis=1, keepdims=True)
            for k in range(0, row.shape[1], 128)
        ],
        axis=0,
    )


def logits_kernel(plan, embed_here, picks, span, *refs):
    me_ref, shift_ref, table_ref = refs[:3]
    blocks = refs[3 : 3 + len(plan)]
    picked_ref, expo_ref, stat_ref, top_ref, picked, expo_all, in_sem, out_sem = refs[
        3 + len(plan) :
    ]
    count, width = table_ref.shape
    me, shift = me_ref[0], shift_ref[0]
    group = 4
    for (part, masks), block in zip(plan, blocks):
        cols = pl.ds(part * block.shape[2], block.shape[2])
        for place, mask in enumerate(masks):
            device = me ^ mask
            pltpu.make_async_copy(
                block.at[place], picked.at[device, :, cols], in_sem
            ).start()
    whole = embed_here // width // 128 * 128
    eye = eye_mask()
    row_start = lax.broadcasted_iota(jnp.int32, (1, count), 1) * width - shift
    touched = (row_start < embed_here)[:, whole:]
    owned = (row_start >= 0)[:, :128]
    tops, sums, copies = [], [], []

    def save(source, target):
        copies.append(pltpu.make_async_copy(source, target, out_sem.at[len(copies)]))
        copies[-1].start()

    step = group * picks
    pltpu.make_async_copy(picked, picked, in_sem).wait()
    save(picked, picked_ref)
    for k in range(picked.shape[0] // group):
        here = slice(k * step, (k + 1) * step)
        rows = jnp.concatenate([picked[group * k + d, :picks, :] for d in range(group)], axis=0)
        logits = contract_cols(rows, table_ref[...])
        logits = jnp.concatenate(
            [logits[:, :whole], jnp.where(touched, logits[:, whole:], -1e30)], axis=1
        )
        top = jnp.max(logits, axis=1, keepdims=True)
        expo = jnp.exp(logits - top)
        expo_all[here, :] = expo
        save(expo_all.at[here], expo_ref.at[here])
        ends = jnp.where(owned, expo[:, :128], 0.0)
        total = jnp.sum(jnp.concatenate([ends, expo[:, 128:]], axis=1), axis=1, keepdims=True)
        tops.append(to_row(top, eye))
        sums.append(to_row(top + jnp.log(total), eye))
    join = span // step

    def blocks_of(own):
        return jnp.concatenate(
            [jnp.concatenate(own[k : k + join], axis=1) for k in range(0, len(own), join)], axis=0
        )

    top_ref[...] = blocks_of(tops)
    stats = blocks_of(sums)
    for device in range(stat_ref.shape[0]):
        stat_ref[device] = stats
    for copy in copies:
        copy.wait()


def call_logits(me, shift, table, gathered, picks, embed_here, devices):
    count, width = table.shape
    pieces = [(part, piece, masks) for part, own in enumerate(gathered) for piece, masks in own]
    plan = tuple((part, tuple(masks)) for part, _, masks in pieces)
    block = pieces[0][1].shape[1]
    rows = devices * picks
    span = rows // 8
    vmem = pl.BlockSpec(memory_space=pltpu.VMEM)
    smem = pl.BlockSpec(memory_space=pltpu.SMEM)
    hbm = pl.BlockSpec(memory_space=pl.ANY)
    low, full = jnp.bfloat16, jnp.float32
    return pl.pallas_call(
        functools.partial(logits_kernel, plan, embed_here, picks, span),
        out_shape=[
            jax.ShapeDtypeStruct((devices, block, width), low),
            jax.ShapeDtypeStruct((rows, count), full),
            jax.ShapeDtypeStruct((devices, 8, span), full),
            jax.ShapeDtypeStruct((8, span), full),
        ],
        in_specs=[smem, smem, vmem] + [hbm] * len(pieces),
        out_specs=[hbm, hbm, vmem, vmem],
        scratch_shapes=[
            pltpu.VMEM((devices, block, width), low),
            pltpu.VMEM((rows, count), full),
            pltpu.SemaphoreType.DMA,
            pltpu.SemaphoreType.DMA((devices // 4 + 1,)),
        ],
        compiler_params=pltpu.CompilerParams(vmem_limit_bytes=58 * 2**20),
        cost_estimate=pl.CostEstimate(
            flops=2 * rows * count * width, bytes_accessed=16 * 2**20, transcendentals=0
        ),
    )(me, shift, table, *[piece for _, piece, _ in pieces])


def terms_kernel(plan, picks, me_ref, *refs):
    stat_ref, top_ref, expo_ref, owned_ref, label_ref, scale_ref = refs[:6]
    sinks = refs[6:15]
    terms, out_sem = refs[15:]
    span, count = expo_ref.shape
    width = owned_ref.shape[1]
    chunks = terms.shape[0]
    group = span // picks
    me = me_ref[0]
    step = pl.program_id(0)
    chunk = step ^ lax.div(me, group)
    scales = []
    for half in range(2):
        row = 2 * chunk + half
        sums = stat_ref[:, pl.ds(row, 1), :]
        top = jnp.max(sums, axis=0)
        whole = top + jnp.log(jnp.sum(jnp.exp(sums - top[None]), axis=0))
        scales.append(jnp.exp(top_ref[pl.ds(row, 1), :] - whole))
    scale = jnp.concatenate(scales, axis=1)
    used = label_ref[1:2, :]
    scale = scale * used
    scale_ref[...] = jnp.broadcast_to(scale, scale_ref.shape)
    label = jnp.where(used > 0, label_ref[0:1, :], -1.0)
    eye = eye_mask()
    part = span // 2
    lane = lax.broadcasted_iota(jnp.int32, (part, count), 1)
    for k in range(0, span, part):
        here = slice(k, k + part)
        probs = expo_ref[here, :] * to_column(scale[:, here], eye)
        hot = lane == to_column(label[:, here], eye).astype(jnp.int32)
        d_logits = jnp.where(hot, probs - 1.0, probs).astype(jnp.bfloat16)
        terms[step, here, :] = dot_nn(d_logits, owned_ref[...]).astype(jnp.bfloat16)
    cut = width // 3
    half = sinks[0].shape[0]

    def send(now):
        for b in range(group):
            row = pl.multiple_of((b ^ lax.rem(me, group)) * picks, 16)
            for part, bits in enumerate(plan):
                relative = now * group + b
                spot = sum(
                    1 << (len(bits) - 1 - k) for k, bit in enumerate(bits) if relative & bit
                )
                kind = 0 if spot < half else (2 if spot < half + half // 2 else 1)
                spot = spot - (0, half + half // 2, half)[kind]
                pltpu.make_async_copy(
                    terms.at[now, pl.ds(row, picks), part * cut : (part + 1) * cut],
                    sinks[3 * part + kind].at[spot],
                    out_sem,
                ).start()

    for now in range(chunks):
        pl.when(step == now)(functools.partial(send, now))

    @pl.when(step == chunks - 1)
    def _():
        wait_sinks(sinks, out_sem)


def call_terms(me, stats, tops, expo, owned, labels, plan, picks):
    rows, count = expo.shape
    width = owned.shape[1]
    devices = stats.shape[0]
    span = 2 * stats.shape[2]
    hbm = pl.BlockSpec(memory_space=pl.ANY)
    low = jnp.bfloat16
    group = span // picks

    def tile(lanes):
        return pl.BlockSpec((span, lanes), lambda k, me: (k ^ lax.div(me[0], group), 0))

    row_tile = pl.BlockSpec((8, span), lambda k, me: (0, k ^ lax.div(me[0], group)))
    return pl.pallas_call(
        functools.partial(terms_kernel, plan, picks),
        grid_spec=pltpu.PrefetchScalarGridSpec(
            num_scalar_prefetch=1,
            grid=(rows // span,),
            in_specs=[
                pl.BlockSpec(stats.shape, lambda k, me: (0, 0, 0)),
                pl.BlockSpec(tops.shape, lambda k, me: (0, 0)),
                tile(count),
                pl.BlockSpec(owned.shape, lambda k, me: (0, 0)),
                row_tile,
            ],
            out_specs=[row_tile] + [hbm] * 9,
            scratch_shapes=[
                pltpu.VMEM((rows // span, span, width), low),
                pltpu.SemaphoreType.DMA,
            ],
        ),
        out_shape=[jax.ShapeDtypeStruct((8, rows), jnp.float32)]
        + sink_shapes(devices, (picks, width // 3), low),
        compiler_params=pltpu.CompilerParams(vmem_limit_bytes=48 * 2**20),
        cost_estimate=pl.CostEstimate(
            flops=2 * rows * count * width, bytes_accessed=12 * 2**20, transcendentals=0
        ),
    )(me, stats, tops, expo, owned, labels)


def embed_kernel(picks, shift_ref, expo_ref, scale_ref, label_ref, picked_ref, out_ref, wide, turn):
    here, width = out_ref.shape
    rows, count = expo_ref.shape
    shift = shift_ref[0]
    chunk = pl.program_id(0)

    @pl.when(chunk == 0)
    def _():
        turn[...] = turn_lanes(shift, width)

    eye = eye_mask()
    probs = expo_ref[...] * to_column(scale_ref[0:1, :], eye)
    lane = lax.broadcasted_iota(jnp.int32, (rows, count), 1)
    used = label_ref[1:2, :]
    label = jnp.where(used > 0, label_ref[0:1, :], -1.0)
    hot = lane == to_column(label, eye).astype(jnp.int32)
    terms = jnp.where(hot, probs - 1.0, probs).astype(jnp.bfloat16)
    picked = jnp.concatenate([picked_ref[d, :picks, :] for d in range(rows // picks)], axis=0)
    turned = contract_cols(picked, turn[...]).astype(jnp.bfloat16)
    total = contract_rows(terms, turned)

    @pl.when(chunk == 0)
    def _():
        wide[...] = total

    @pl.when(chunk > 0)
    def _():
        wide[...] = wide[...] + total

    @pl.when(chunk == pl.num_programs(0) - 1)
    def _():
        lane = lax.broadcasted_iota(jnp.int32, (here, width), 1)
        out_ref[...] = jnp.where(lane < width - shift, wide[:here, :], wide[1 : here + 1, :])


def call_embed(shift, expo, scale, labels, picked, picks, here):
    rows, count = expo.shape
    devices, block, width = picked.shape
    smem = pl.BlockSpec(memory_space=pltpu.SMEM)
    step = rows // 8
    row_tile = pl.BlockSpec((8, step), lambda k: (0, k))
    return pl.pallas_call(
        functools.partial(embed_kernel, picks),
        grid=(8,),
        out_shape=jax.ShapeDtypeStruct((here, width), jnp.float32),
        in_specs=[
            smem,
            pl.BlockSpec((step, count), lambda k: (k, 0)),
            row_tile,
            row_tile,
            pl.BlockSpec((devices // 8, block, width), lambda k: (k, 0, 0)),
        ],
        out_specs=pl.BlockSpec((here, width), lambda k: (0, 0)),
        scratch_shapes=[
            pltpu.VMEM((count, width), jnp.float32),
            pltpu.VMEM((width, width), jnp.bfloat16),
        ],
        compiler_params=pltpu.CompilerParams(vmem_limit_bytes=58 * 2**20),
        cost_estimate=pl.CostEstimate(
            flops=16 * rows * count * width, bytes_accessed=64 * 2**20, transcendentals=0
        ),
    )(shift, expo, scale, labels, picked)


def step_kernel(counts, *refs):
    weight_ref, first_ref, second_ref = refs[:3]
    grad_ref, step_ref = refs[-2:]
    start, row = 3, 0
    width = refs[3].shape[2]
    share = width // 128
    for count in counts:
        total = add_terms([ref[0] for ref in refs[start : start + count]])
        rows = total.shape[0]
        for q in range(share):
            grad_ref[pl.ds(share * row + q, rows, stride=share), :] = total[
                :, 128 * q : 128 * q + 128
            ]
        start, row = start + count, row + rows
    step_ref[...] = adam_step(
        weight_ref[...], grad_ref[...], first_ref[...], second_ref[...], float(ADAM_STEP), decay_rate
    )


def call_step(weight, first, second, terms):
    shape = jax.ShapeDtypeStruct((weight.shape[0] // 128, 128), jnp.float32)
    vmem = pl.BlockSpec(memory_space=pltpu.VMEM)
    given = [value.reshape(shape.shape) for value in (weight, first, second)]
    blocks = [term for own in terms for term in own]
    first_block = pl.BlockSpec((1,) + blocks[0].shape[1:], lambda k: (0, 0, 0))
    grad, step = pl.pallas_call(
        functools.partial(step_kernel, [len(own) for own in terms]),
        grid=(1,),
        out_shape=[shape] * 2,
        in_specs=[vmem] * 3 + [first_block] * len(blocks),
        out_specs=[vmem] * 2,
        compiler_params=pltpu.CompilerParams(vmem_limit_bytes=24 * 2**20),
    )(*given, *blocks)
    return grad.reshape(-1), step.reshape(-1)


def plain_forward(mats_all, vecs_all, block_input, span_lengths):
    seq_here, length, width = block_input.shape
    rows_here = seq_here * length
    heads_count = width // HEAD_DIM
    head_scale = HEAD_DIM ** (-0.5)
    low = jnp.bfloat16
    w_qkv, w_out, w_up, w_down = split_mats(mats_all)
    bias_q, bias_v, bias_out, gain_one, shift_one, bias_up, bias_down, gain_two, shift_two = (
        split_vecs(vecs_all)
    )
    valid = jnp.arange(length)[None, :] < span_lengths[:, None]
    valid_col = valid.reshape(rows_here, 1).astype(jnp.float32)
    tok_rows = (block_input * valid[:, :, None].astype(low)).reshape(rows_here, width)
    qkv_bias = jnp.concatenate([bias_q, jnp.zeros((width,), jnp.float32), bias_v])
    projected = (jnp.dot(tok_rows, w_qkv, preferred_element_type=jnp.float32) + qkv_bias).astype(
        low
    )
    shaped = projected.reshape(seq_here, length, 3, heads_count, HEAD_DIM)
    queries = shaped[:, :, 0]
    key_rows = shaped[:, :, 1]
    value_rows = shaped[:, :, 2]
    key_valid = valid[:, None, None, :]

    def make_scores():
        raw = (
            jnp.einsum("sqhd,skhd->shqk", queries, key_rows, preferred_element_type=jnp.float32)
            * head_scale
        )
        return jnp.where(key_valid, raw, -1e30)

    scores = make_scores()
    row_max = jnp.max(scores, axis=-1, keepdims=True)
    expo_vals = jnp.exp(scores - row_max)
    row_sum = jnp.sum(expo_vals, axis=-1, keepdims=True)
    row_lse = row_max + jnp.log(row_sum)
    attn_probs = (expo_vals / row_sum).astype(low)
    attended = (
        jnp.einsum("shqk,skhd->sqhd", attn_probs, value_rows, preferred_element_type=jnp.float32)
        .reshape(rows_here, width)
        .astype(low)
    )
    branch = jnp.dot(attended, w_out, preferred_element_type=jnp.float32) + bias_out
    normed_one, inverse_one = center_scale(tok_rows.astype(jnp.float32) + branch)
    hidden_one = normed_one * gain_one + shift_one
    hidden_low = hidden_one.astype(low)
    pre_act = jnp.dot(hidden_low, w_up, preferred_element_type=jnp.float32) + bias_up
    act_low = jax.nn.gelu(pre_act, approximate=False).astype(low)
    ffn_out = jnp.dot(act_low, w_down, preferred_element_type=jnp.float32) + bias_down
    normed_two, inverse_two = center_scale(hidden_one + ffn_out)
    output = (normed_two * gain_two + shift_two) * valid_col

    def plain_backward(d_output):
        d_gain_two = jnp.sum(d_output * normed_two, axis=0)
        d_shift_two = jnp.sum(d_output, axis=0)
        d_resid_two = norm_back(d_output * gain_two, normed_two, inverse_two)
        d_ffn = d_resid_two.astype(low)
        d_bias_down = jnp.sum(d_ffn.astype(jnp.float32), axis=0)
        d_w_down = contract_rows(act_low, d_ffn)
        d_act = contract_cols(d_ffn, w_down)
        d_pre = (d_act * gelu_slope(pre_act)).astype(low)
        d_bias_up = jnp.sum(d_pre.astype(jnp.float32), axis=0)
        d_w_up = contract_rows(hidden_low, d_pre)
        d_hidden = contract_cols(d_pre, w_up) + d_resid_two
        d_gain_one = jnp.sum(d_hidden * normed_one, axis=0)
        d_shift_one = jnp.sum(d_hidden, axis=0)
        d_resid_one = norm_back(d_hidden * gain_one, normed_one, inverse_one)
        d_branch = d_resid_one.astype(low)
        d_bias_out = jnp.sum(d_branch.astype(jnp.float32), axis=0)
        d_w_out = contract_rows(attended, d_branch)
        d_attended = (
            contract_cols(d_branch, w_out).astype(low).reshape(seq_here, length, heads_count, HEAD_DIM)
        )
        probs_again = jnp.exp(make_scores() - row_lse)
        probs_low = probs_again.astype(low)
        d_probs = jnp.einsum(
            "sqhd,skhd->shqk", d_attended, value_rows, preferred_element_type=jnp.float32
        )
        d_values = jnp.einsum(
            "shqk,sqhd->skhd", probs_low, d_attended, preferred_element_type=jnp.float32
        )
        row_delta = jnp.sum(d_probs * probs_again, axis=-1, keepdims=True)
        d_scores = (probs_again * (d_probs - row_delta)).astype(low)
        d_queries = (
            jnp.einsum("shqk,skhd->sqhd", d_scores, key_rows, preferred_element_type=jnp.float32)
            * head_scale
        )
        d_keys = (
            jnp.einsum("shqk,sqhd->skhd", d_scores, queries, preferred_element_type=jnp.float32)
            * head_scale
        )
        d_qkv = jnp.concatenate(
            [
                d_queries.reshape(rows_here, width),
                d_keys.reshape(rows_here, width),
                d_values.reshape(rows_here, width),
            ],
            axis=1,
        ).astype(low)
        d_qkv_float = d_qkv.astype(jnp.float32)
        d_bias_q = jnp.sum(d_qkv_float[:, :width], axis=0)
        d_bias_v = jnp.sum(d_qkv_float[:, 2 * width :], axis=0)
        d_w_qkv = contract_rows(tok_rows, d_qkv)
        grad_input = ((contract_cols(d_qkv, w_qkv) + d_resid_one) * valid_col).reshape(
            seq_here, length, width
        )
        d_mats = jnp.concatenate(
            [
                piece.astype(low).reshape(-1, width)
                for piece in (d_w_qkv, d_w_out, d_w_up, d_w_down)
            ]
        )
        d_vecs = jnp.concatenate(
            [
                d_bias_q,
                d_bias_v,
                d_bias_out,
                d_gain_one,
                d_shift_one,
                d_bias_up,
                d_bias_down,
                d_gain_two,
                d_shift_two,
            ]
        )
        return grad_input, d_mats, d_vecs

    return output, plain_backward


def on_device(
    names,
    core,
    block_input,
    span_lengths,
    mlm_positions,
    mlm_labels,
    span_pairs,
    layer_mats,
    vectors,
    embedding,
    mom1_mats,
    mom2_mats,
    mom1_vecs,
    mom2_vecs,
    mom1_embed,
    mom2_embed,
):
    seq_here, length, width = block_input.shape
    rows_here = seq_here * length
    devices = 2 ** len(names)
    me = lax.axis_index(names)
    orders = bit_orders(names, core)
    slots = mlm_positions.shape[1]
    picks_here = seq_here * slots
    low = jnp.bfloat16

    third = layer_mats.shape[0] // width // 3
    by_kernel = third % 16 == 0
    vec_here = vectors.shape[0]
    mats_low = layer_mats.astype(low).reshape(3, third, width)

    labels_flat = mlm_labels.reshape(-1)
    common = jnp.concatenate(
        [
            value.astype(low)
            for value in (
                vectors,
                labels_flat // 256,
                labels_flat % 256,
                span_pairs // 256,
                span_pairs % 256,
                span_lengths // 4,
            )
        ]
    )
    sizes = [vec_here, picks_here, picks_here, seq_here, seq_here, seq_here]
    common = jnp.pad(common, (0, width - common.shape[0]))
    others = jnp.arange(devices)[:, None]
    right, left = (me + 1) % devices, (me + devices - 1) % devices
    border = jnp.where(
        others == right,
        embedding[-width:].astype(low),
        jnp.where(others == left, embedding[:width].astype(low), jnp.zeros((), low)),
    )
    small = jnp.stack([jnp.broadcast_to(common, border.shape), border], axis=1)

    def share(small):
        return lax.all_to_all(small, names, 0, 0, tiled=True)

    embed_here = embedding.shape[0]
    shifted_rows = -(-embed_here // width)
    over = shifted_rows * width - embed_here
    shift = (me * (embed_here % width)) % width
    first_row = me * (embed_here // width) + (me * (embed_here % width)) // width

    def table_shard(embedding):
        return jnp.pad(embedding.astype(low), (0, over)).reshape(shifted_rows, width)


    def unpack(small_all):
        starts = [sum(sizes[:k]) for k in range(len(sizes))]
        vecs_all, labels_high, labels_low, pairs_high, pairs_low, quarter_all = (
            small_all[:, 0, start : start + size] for start, size in zip(starts, sizes)
        )
        vec_rows = vecs_all.reshape(-1).astype(jnp.float32).reshape(-1, width)

        def whole(high, small):
            return (high.astype(jnp.int32) * 256 + small.astype(jnp.int32)).reshape(-1)

        quarter_all = quarter_all.astype(jnp.int32).reshape(-1)
        used = (jnp.arange(slots)[None, :] < quarter_all[:, None]).reshape(-1)
        row_of = whole(labels_high, labels_low) - first_row
        from_left = lax.dynamic_index_in_dim(small_all[:, 1], left, 0, False)
        from_right = lax.dynamic_index_in_dim(small_all[:, 1], right, 0, False)
        right_rows = jnp.pad(from_right, (width - over, over)).reshape(2, width)
        return vec_rows, row_of, used, whole(pairs_high, pairs_low), from_left, right_rows

    seq_start = jnp.arange(seq_here, dtype=jnp.int32) * length

    def span_terms(cls_all, pairs_all):
        span_scale = 2.0 / math.sqrt(width)
        columns = jnp.arange(cls_all.shape[0])
        sims = contract_cols(cls_all, cls_all) * span_scale
        sims = jnp.where(columns[None, :] == columns[:, None], -1e30, sims)
        partner_hot = (columns[None, :] == pairs_all[:, None]).astype(jnp.float32)
        d_sims = (jax.nn.softmax(sims, axis=-1) - partner_hot).astype(low)
        mine = me * seq_here
        d_sims_rows = lax.dynamic_slice_in_dim(d_sims, mine, seq_here, 0)
        d_sims_cols = lax.dynamic_slice_in_dim(d_sims, mine, seq_here, 1)
        return (
            jnp.dot(d_sims_rows, cls_all, preferred_element_type=jnp.float32)
            + contract_rows(d_sims_cols, cls_all)
        ) * span_scale

    step_float = float(ADAM_STEP)

    def embed_step(grad_rows):
        grad = grad_rows.reshape(-1)[:embed_here]
        return grad, adam_step(embedding, grad, mom1_embed, mom2_embed, step_float, decay_rate)

    def vector_terms(d_vecs):
        return lax.all_to_all(d_vecs.reshape(devices, 1, vec_here), names, 0, 0, tiled=True)

    cut = width // 3
    columns = [slice(k * cut, (k + 1) * cut) for k in range(3)]
    back_orders = [order[::-1] for order in orders]
    if by_kernel:
        lone = me.astype(jnp.int32).reshape(1)
        lone_shift = shift.astype(jnp.int32).reshape(1)
        tok_rows = block_input.reshape(rows_here, width)
        relative = jnp.arange(devices, dtype=jnp.int32) ^ me.astype(jnp.int32)
        spots = jnp.stack(
            [
                sum(
                    ((relative & device_mask(name, names)) != 0).astype(jnp.int32)
                    << (len(names) - 1 - k)
                    for k, name in enumerate(order)
                )
                for order in back_orders
            ],
            axis=1,
        ).reshape(-1)
        places = jnp.concatenate(
            [
                (mlm_positions + seq_start[:, None]).reshape(-1),
                seq_start,
                jnp.full((16 - seq_here,), -1, jnp.int32),
            ]
        )
        table_rows = -(-(shifted_rows + 1) // 128) * 128

        def prepare(embedding, small_all):
            vec_rows, row_of, used, pairs_all, from_left, right_rows = unpack(small_all)
            ends = jnp.pad(
                jnp.concatenate([from_left[None], right_rows]).astype(jnp.float32),
                ((0, 5), (0, 0)),
            )
            labels = jnp.pad(
                jnp.stack([row_of.astype(jnp.float32), used.astype(jnp.float32)]),
                ((0, 6), (0, 0)),
            )
            shifted = table_shard(embedding)
            table, owned = call_table(lone_shift, shifted, ends, table_rows, embed_here)
            return table, owned, labels, vec_rows, pairs_all

        gathered, (table, owned, labels, vec_rows, pairs_all) = gather_relative(
            mats_low[:, None], orders, names, (embedding, small), share, prepare
        )
        *heads, saved = call_forward(
            lone, span_lengths, places[None], tok_rows, vec_rows, gathered, devices, seq_here
        )
        heads_all, _ = gather_relative(heads, orders, names)
        picked, expo, stats, tops = call_logits(
            lone, lone_shift, table, heads_all, picks_here, embed_here, devices
        )
        stats = lax.all_to_all(stats, names, 0, 0, tiled=True)
        plan = tuple(tuple(device_mask(name, names) for name in order) for order in back_orders)
        scale, *sinks = call_terms(
            lone, stats, tops, expo, owned, labels, plan, picks_here
        )
        d_cls = span_terms(
            picked[:, picks_here : picks_here + seq_here].reshape(-1, width), pairs_all
        )
        d_parts, _ = reduce_relative(
            sinks[0::3], list(zip(sinks[1::3], sinks[2::3])), back_orders
        )
        d_parts = [add_terms([term[0] for term in terms]) for terms in d_parts]
        top = jnp.concatenate(
            [jnp.concatenate(d_parts, axis=1), jnp.pad(d_cls, ((0, 16 - seq_here), (0, 0)))]
        )
        grad_input, d_vecs, *sinks = call_backward(
            span_lengths, spots, places[None], tok_rows, vec_rows, top, saved, third, seq_here
        )
        grad_input = grad_input.reshape(seq_here, length, width)
        def table_grad(state):
            expo, picked, d_vecs = state
            grad_embed = call_embed(
                lone_shift, expo, scale, labels, picked, picks_here, shifted_rows
            )
            grad_embed, d_vecs = lax.optimization_barrier((grad_embed, d_vecs))
            return grad_embed, vector_terms(d_vecs)

        def table_step(state):
            grad_embed, terms = state
            return *embed_step(grad_embed), jnp.sum(terms, axis=(0, 1))

        terms, (grad_embed, step_embed, grad_vecs) = reduce_relative(
            sinks[0::3],
            list(zip(sinks[1::3], sinks[2::3])),
            back_orders,
            (expo, picked, d_vecs),
            {0: table_grad, len(names) - 2: table_step},
            1,
        )
        grad_mats, step_mats = call_step(layer_mats, mom1_mats, mom2_mats, terms)
    else:
        vec_rows, row_of, used, pairs_all, from_left, right_rows = unpack(share(small))
        same_row = (jnp.arange(width) < width - shift)[None, :]
        tall = jnp.concatenate(
            [from_left[None], table_shard(embedding), jnp.zeros((1, width), low)]
        )
        tall = tall.at[shifted_rows : shifted_rows + 2].add(right_rows)
        lanes = jnp.arange(width)
        turn = ((lanes[:, None] + shift) % width == lanes[None, :]).astype(low)
        rolled = jnp.where(same_row, tall[1:], tall[:-1])
        table = jnp.dot(rolled, turn, preferred_element_type=jnp.float32).astype(low)
        row_start = jnp.arange(shifted_rows + 1) * width - shift
        owned = (row_start >= 0) & (row_start < embed_here)
        touched = (row_start + width > 0) & (row_start < embed_here)
        gathered = [gather_bits(mats_low[k], orders[k], names) for k in range(3)]
        mats_all = jnp.stack(gathered, axis=1).reshape(-1)
        output, plain_backward = plain_forward(
            mats_all, vec_rows.reshape(-1), block_input, span_lengths
        )
        output_seq = output.reshape(seq_here, length, width)
        picked_here = jnp.take_along_axis(output_seq, mlm_positions[:, :, None], axis=1)
        heads = jnp.concatenate([picked_here.reshape(-1, width), output_seq[:, 0, :]]).astype(low)
        heads_all = jnp.concatenate(
            [gather_bits(heads[:, c], order, names) for c, order in zip(columns, orders)], axis=2
        )
        picked = heads_all[:, :picks_here, :].reshape(-1, width)
        logits = contract_cols(picked, table)
        masked = jnp.where(owned[None, :], logits, -jnp.inf)
        part_max = jnp.max(masked, axis=-1)
        part_sum = jnp.sum(jnp.exp(masked - part_max[:, None]), axis=-1)
        full_max = lax.pmax(part_max, names)
        full_sum = lax.psum(part_sum * jnp.exp(part_max - full_max), names)
        hot = row_of[:, None] == jnp.arange(shifted_rows + 1)[None, :]
        probs = jnp.exp(logits - full_max[:, None]) / full_sum[:, None]
        d_logits = jnp.where(
            used[:, None] & touched[None, :], probs - hot.astype(jnp.float32), 0.0
        ).astype(low)
        d_picked = jnp.dot(
            d_logits, jnp.where(owned[:, None], table, 0), preferred_element_type=jnp.float32
        )
        blocks = d_picked.astype(low).reshape(devices, picks_here, width)
        d_picked = jnp.concatenate(
            [
                reduce_bits(blocks[:, :, c], order, names)
                for c, order in zip(columns, back_orders)
            ],
            axis=1,
        ).astype(jnp.float32)
        select = (mlm_positions[:, :, None] == jnp.arange(length)[None, None, :]).astype(
            jnp.float32
        )
        d_output_seq = jnp.einsum(
            "gor,gon->grn",
            select,
            d_picked.reshape(seq_here, slots, width),
            precision=lax.Precision.HIGHEST,
        )
        d_cls = span_terms(heads_all[:, picks_here:, :].reshape(-1, width), pairs_all)
        d_output_seq = d_output_seq.at[:, 0, :].add(d_cls)
        valid = jnp.arange(length)[None, :] < span_lengths[:, None]
        d_output = d_output_seq.reshape(rows_here, width) * valid.reshape(rows_here, 1)
        grad_input, d_mats, d_vecs = plain_backward(d_output)
        d_mats = d_mats.reshape(devices, 3, third, width)
        summed = [
            reduce_bits(d_mats[:, k], back_orders[k], names).astype(jnp.float32) for k in range(3)
        ]
        picked_turned = jnp.dot(picked, turn.T, preferred_element_type=jnp.float32).astype(low)
        d_rolled = contract_rows(d_logits, picked_turned)
        grad_embed, step_embed = embed_step(jnp.where(same_row, d_rolled[:-1], d_rolled[1:]))
        grad_vecs = jnp.sum(vector_terms(d_vecs), axis=(0, 1))
        grad_mats = jnp.concatenate(summed).reshape(-1)
        step_mats = adam_step(layer_mats, grad_mats, mom1_mats, mom2_mats, step_float, decay_rate)
    step_vecs = adam_step(vectors, grad_vecs, mom1_vecs, mom2_vecs, step_float, 0.0)
    return (grad_input, grad_mats, grad_vecs, grad_embed, step_mats, step_vecs, step_embed)


def solution(mesh):
    fsdp_bits = mesh.shape["fsdp"].bit_length() - 1
    rep_bits = mesh.shape["rep"].bit_length() - 1
    names = tuple(f"f{k}" for k in reversed(range(fsdp_bits)))
    core = names[-1]
    names = names + tuple(f"r{k}" for k in reversed(range(rep_bits)))
    bits = Mesh(mesh.devices.reshape((2,) * len(names)), names)
    seqs = P(names, None, None)
    pairs = P(names, None)
    flat = P(names)
    return jax.shard_map(
        functools.partial(on_device, names, core),
        mesh=bits,
        in_specs=(seqs, flat, pairs, pairs) + (flat,) * 10,
        out_specs=(seqs,) + (flat,) * 6,
        check_vma=False,
    )
```

```python
import functools
import math

import jax
import jax.numpy as jnp
from jax import lax
from jax.experimental import pallas as pl
from jax.experimental.pallas import tpu as pltpu
from jax.sharding import Mesh, PartitionSpec as P

D = 768
FF = 3072
HEAD_DIM = 64
VOCAB = 30522
ADAM_STEP = 10


norm_eps = 1e-12
beta_one = 0.9
beta_two = 0.999
adam_eps = 1e-06
decay_rate = 0.01


def split_mats(flat):
    first = 3 * D * D
    second = first + D * D
    third = second + D * FF
    return (
        flat[:first].reshape(D, 3 * D),
        flat[first:second].reshape(D, D),
        flat[second:third].reshape(D, FF),
        flat[third:].reshape(FF, D),
    )


def split_vecs(flat):
    widths_list = [D, D, D, D, D, FF, D, D, D]
    pieces = []
    offset = 0
    for piece_width in widths_list:
        pieces.append(flat[offset : offset + piece_width].astype(jnp.float32))
        offset = offset + piece_width
    return pieces


def center_scale(resid):
    center = resid - jnp.mean(resid, axis=-1, keepdims=True)
    inverse = lax.rsqrt(jnp.mean(center * center, axis=-1, keepdims=True) + norm_eps)
    return (center * inverse, inverse)


def norm_back(d_normed, normed, inverse):
    return inverse * (
        d_normed
        - jnp.mean(d_normed, axis=-1, keepdims=True)
        - normed * jnp.mean(d_normed * normed, axis=-1, keepdims=True)
    )


def gelu_slope(value):
    return (
        0.5 * (1.0 + lax.erf(value * 0.7071067811865476))
        + value * jnp.exp(-0.5 * value * value) * 0.3989422804014327
    )


def contract_rows(left, right):
    return lax.dot_general(
        left, right, (((0,), (0,)), ((), ())), preferred_element_type=jnp.float32
    )


def contract_cols(left, right):
    return lax.dot_general(
        left, right, (((1,), (1,)), ((), ())), preferred_element_type=jnp.float32
    )


def adam_step(weight, grad, first, second, step_float, decay):
    first_new = beta_one * first + (1.0 - beta_one) * grad
    second_new = beta_two * second + (1.0 - beta_two) * grad * grad
    first_hat = first_new / (1.0 - beta_one**step_float)
    second_hat = second_new / (1.0 - beta_two**step_float)
    return first_hat / (jnp.sqrt(second_hat) + adam_eps) + decay * weight


def flip(value, name):
    return lax.ppermute(value, name, [(0, 1), (1, 0)])


def gather_bits(shard, order, names):
    grown = shard
    for name in order:
        other = flip(grown, name)
        first = lax.axis_index(name) == 0
        grown = jnp.stack([jnp.where(first, grown, other), jnp.where(first, other, grown)])
    axes = list(reversed(order))
    rank = len(axes)
    turn = [axes.index(name) for name in names] + list(range(rank, grown.ndim))
    return grown.transpose(turn).reshape((2**rank,) + shard.shape)


def reduce_bits(blocks, order, names):
    left = list(names)
    held = blocks.reshape((2,) * len(left) + blocks.shape[1:])
    for name in order:
        axis = left.index(name)
        here = lax.axis_index(name)
        send = lax.dynamic_index_in_dim(held, 1 - here, axis, keepdims=False)
        keep = lax.dynamic_index_in_dim(held, here, axis, keepdims=False)
        other = flip(send, name)
        held = (keep.astype(jnp.float32) + other.astype(jnp.float32)).astype(blocks.dtype)
        left.remove(name)
    return held


def bit_orders(names, core, picks):
    outer = [name for name in names if name != core]
    count = len(outer)
    if count == 4:
        return [[outer[k] for k in pick] + [core] for pick in picks]
    step = max(1, count // 3)
    return [outer[step * k :] + outer[: step * k] + [core] for k in range(3)]


def device_mask(name, names):
    return 1 << (len(names) - 1 - names.index(name))


def gather_relative(shards, orders, names, early=(), exchange=None, work=None, split=False):
    held = []
    for number, (shard, order) in enumerate(zip(shards, orders)):
        grown, masks = shard, [0]
        for k, name in enumerate(order[:-2]):
            other, bit = flip(grown, name), device_mask(name, names)
            pieces = [grown, other]
            masks_all = [masks, [mask | bit for mask in masks]]
            if split and k == len(order) - 3:
                pieces = list(lax.optimization_barrier(pieces))
                break
            grown = lax.optimization_barrier(jnp.concatenate(pieces))
            masks = sum(masks_all, [])
            pieces, masks_all = [grown], [masks]
            if exchange is not None and k == 0 and number == len(orders) - 1:
                grown, given = lax.optimization_barrier((grown, early[-1]))
                early = (*early[:-1], exchange(given))
                pieces = [grown]
        held.append((pieces, masks_all))
    grown_all = [pieces for pieces, _ in held]
    others_all = [
        [flip(piece, order[-2]) for piece in pieces] for pieces, order in zip(grown_all, orders)
    ]
    if work is not None:
        late, early = lax.optimization_barrier((grown_all, early))
        grown_all, early = lax.optimization_barrier((late, work(*early)))
    gathered = []
    for pieces, others, (_, masks_all), order in zip(grown_all, others_all, held, orders):
        bit = device_mask(order[-2], names)
        pairs = list(zip(pieces, masks_all)) + [
            (other, [mask | bit for mask in masks]) for other, masks in zip(others, masks_all)
        ]
        bit = device_mask(order[-1], names)
        pairs = pairs + [
            (flip(piece, order[-1]), [mask | bit for mask in masks]) for piece, masks in pairs
        ]
        gathered.append(pairs)
    return gathered, early


def add_terms(terms):
    total = terms[0].astype(jnp.float32)
    for term in terms[1:]:
        total = total + term.astype(jnp.float32)
    return total


def reduce_relative(keeps, sends, orders, state=None, works=(), early_sums=None):
    works = dict(works)
    sends = list(sends)
    terms_all = [[keep] for keep in keeps]
    whole_all = [[keep] for keep in keeps]
    for step in range(len(orders[0])):
        for k, order in enumerate(orders):
            half = terms_all[k][0].shape[0] // 2
            if step == 0:
                urgent, rest = (flip(send, order[step]) for send in sends[k])
                whole_all[k].append(rest)
            else:
                other = flip(sends[k], order[step])
                urgent, rest = other[half:], other[:half]
                whole_all[k].append(other)
            if half:
                upper = [term[half:] for term in terms_all[k]] + [urgent]
                sends[k] = add_terms(upper).astype(urgent.dtype)
                terms_all[k] = [term[:half] for term in terms_all[k]] + [rest]
            else:
                terms_all[k] = terms_all[k] + [urgent]
        if step == early_sums:
            left = terms_all[0][0].shape[0]
            for k in range(len(orders)):
                sends[k], terms = lax.optimization_barrier((sends[k], whole_all[k]))
                terms_all[k] = [add_terms([term[:left] for term in terms])]
                whole_all[k] = list(terms_all[k])
        if step in works:
            sends[-1], state = lax.optimization_barrier((sends[-1], state))
            state = works[step](state)
    return whole_all, state


def dot_nn(left, right):
    return lax.dot_general(
        left, right, (((1,), (0,)), ((), ())), preferred_element_type=jnp.float32
    )


def interleave(count, rows):
    span = rows // count
    to = lax.broadcasted_iota(jnp.int32, (rows, rows), 0)
    source = lax.broadcasted_iota(jnp.int32, (rows, rows), 1)
    return (source == count * lax.rem(to, span) + lax.div(to, span)).astype(jnp.bfloat16)


def deinterleave(count, rows):
    span = rows // count
    source = lax.broadcasted_iota(jnp.int32, (rows, rows), 1)
    to = lax.broadcasted_iota(jnp.int32, (rows, rows), 0)
    return (to == count * lax.rem(source, span) + lax.div(source, span)).astype(jnp.bfloat16)


def valid_rows(len_ref, rows, seq_here):
    length = rows // seq_here
    row = lax.broadcasted_iota(jnp.int32, (rows, 1), 0)
    valid = jnp.zeros((rows, 1), jnp.float32)
    for seq in range(seq_here):
        inside = (row >= seq * length) & (row < seq * length + len_ref[seq])
        valid = jnp.where(inside, 1.0, valid)
    return valid


def stack_pair(value):
    lane = lax.broadcasted_iota(jnp.int32, value.shape, 1)
    zero = jnp.zeros_like(value)
    left = lane < HEAD_DIM
    return jnp.concatenate([jnp.where(left, value, zero), jnp.where(left, zero, value)], axis=0)


def join_pair(stacked):
    half = stacked.shape[0] // 2
    lane = lax.broadcasted_iota(jnp.int32, (half, stacked.shape[1]), 1)
    return jnp.where(lane < HEAD_DIM, stacked[:half], stacked[half:])


def pair_scores(stacked, keys, limit):
    raw = contract_cols(stacked, keys) * HEAD_DIM ** (-0.5)
    column = lax.broadcasted_iota(jnp.int32, raw.shape, 1)
    return jnp.where(column < limit, raw, -1e30)


def center_rows(resid):
    center = resid - jnp.mean(resid, axis=-1, keepdims=True)
    inverse = lax.rsqrt(jnp.mean(center * center, axis=-1, keepdims=True) + norm_eps)
    return center * inverse, inverse


def gelu_phi(value):
    return 0.5 * (1.0 + lax.erf(value * 0.7071067811865476))


def forward_kernel(plan, planes, seq_here, *refs):
    me_ref, len_ref, place_ref, x_ref, vec_ref = refs[:5]
    blocks = refs[5 : 5 + len(plan)]
    heads_refs = refs[5 + len(plan) : 8 + len(plan)]
    wall_ref, qkv_ref, att_ref, n1_ref, pre_ref, n2_ref, stat_ref = refs[
        8 + len(plan) : 15 + len(plan)
    ]
    raw, turned, qkv, att, n1, pre_all, in_sem, out_sem = refs[15 + len(plan) :]
    rows, width = x_ref.shape
    length = rows // seq_here
    pairs = width // (2 * HEAD_DIM)
    up = 4 * width
    me = me_ref[0]
    for first in (True, False):
        for (part, unit, masks), block in zip(plan, blocks):
            for place, mask in enumerate(masks):
                device = me ^ mask
                early = device < planes

                @pl.when(early if first else jnp.logical_not(early))
                def _(device=device, part=part, unit=unit, block=block, place=place, first=first):
                    row = pl.multiple_of((3 * device + part) * unit, 16)
                    pltpu.make_async_copy(
                        block.at[place], raw.at[pl.ds(row, unit)], in_sem.at[0 if first else 1]
                    ).start()

    copies = []

    def save(source, target):
        copy = pltpu.make_async_copy(source, target, out_sem.at[len(copies)])
        copy.start()
        copies.append(copy)

    valid = valid_rows(len_ref, rows, seq_here)
    x = (x_ref[...].astype(jnp.float32) * valid).astype(jnp.bfloat16)
    split3, split4 = interleave(3, 384), interleave(4, 256)
    arrived = raw.at[0 : 3 * width]
    pltpu.make_async_copy(arrived, arrived, in_sem.at[0]).wait()

    for b in range(width // 128):
        block = dot_nn(split3, raw[384 * b : 384 * b + 384, :]).astype(jnp.bfloat16)
        for p in range(3):
            turned[width * p + 128 * b : width * p + 128 * b + 128, :] = block[
                128 * p : 128 * p + 128
            ]
    save(turned.at[0 : 3 * width], wall_ref.at[0 : 3 * width])
    for p, bias in ((0, 0), (1, None), (2, 1)):
        value = dot_nn(x, turned[width * p : width * (p + 1), :])
        if bias is not None:
            value = value + vec_ref[bias : bias + 1, :]
        qkv[:, width * p : width * (p + 1)] = value.astype(jnp.bfloat16)
    save(qkv, qkv_ref)

    stats = jnp.zeros((2 * length, 128), jnp.float32)
    lane = lax.broadcasted_iota(jnp.int32, stats.shape, 1)
    for seq in range(seq_here):
        here = slice(seq * length, (seq + 1) * length)
        for g in range(pairs):
            cols = [slice(width * p + 128 * g, width * p + 128 * g + 128) for p in range(3)]
            query, key, value = (qkv[here, c] for c in cols)
            scores = pair_scores(stack_pair(query), key, len_ref[seq])
            top = jnp.max(scores, axis=-1, keepdims=True)
            expo = jnp.exp(scores - top)
            total = jnp.sum(expo, axis=-1, keepdims=True)
            stats = jnp.where(lane == seq * pairs + g, top + jnp.log(total), stats)
            probs = (expo / total).astype(jnp.bfloat16)
            att[here, 128 * g : 128 * g + 128] = join_pair(dot_nn(probs, value)).astype(
                jnp.bfloat16
            )
    save(att, att_ref)
    arrived = raw.at[3 * width : 3 * up]
    pltpu.make_async_copy(arrived, arrived, in_sem.at[1]).wait()
    save(raw.at[3 * width : up], wall_ref.at[3 * width : up])
    save(raw.at[2 * up : 3 * up], wall_ref.at[2 * up : 3 * up])

    branch = dot_nn(att[...], raw[3 * width : up, :]) + vec_ref[2:3, :]
    for b in range(width // 64):
        block = dot_nn(split4, raw[up + 256 * b : up + 256 * b + 256, :]).astype(jnp.bfloat16)
        for p in range(4):
            row = width * (3 + p) + 64 * b
            turned[row : row + 64, :] = block[64 * p : 64 * p + 64]
    save(turned.at[3 * width : 7 * width], wall_ref.at[up : 2 * up])
    normed, inverse = center_rows(x.astype(jnp.float32) + branch)
    n1[...] = normed
    save(n1, n1_ref)
    stat_one = seq_here * pairs
    hidden = normed * vec_ref[3:4, :] + vec_ref[4:5, :]
    hidden_low = hidden.astype(jnp.bfloat16)
    total = hidden + vec_ref[9:10, :]
    for p in range(4):
        pre = dot_nn(hidden_low, turned[width * (3 + p) : width * (4 + p), :])
        pre = pre + vec_ref[5 + p : 6 + p, :]
        pre_all[p] = pre
        save(pre_all.at[p], pre_ref.at[p])
        act = (pre * gelu_phi(pre)).astype(jnp.bfloat16)
        total = total + dot_nn(act, raw[2 * up + width * p : 2 * up + width * (p + 1), :])
    normed, inverse_two = center_rows(total)
    n2_ref[...] = normed
    wide = lax.broadcasted_iota(jnp.int32, (rows, 128), 1)
    ends = jnp.where(
        wide == stat_one, inverse, jnp.where(wide == stat_one + 1, inverse_two, 0.0)
    )
    stat_ref[0] = stats
    stat_ref[1] = ends
    output = ((normed * vec_ref[10:11, :] + vec_ref[11:12, :]) * valid).astype(jnp.bfloat16)
    spot = lax.broadcasted_iota(jnp.int32, (rows, place_ref.shape[1]), 0)
    choose = (spot == place_ref[...]).astype(jnp.bfloat16)
    heads = contract_rows(choose, output).astype(jnp.bfloat16)
    cut = width // 3
    for k, heads_ref in enumerate(heads_refs):
        heads_ref[0] = heads[:, k * cut : (k + 1) * cut]
    for copy in copies:
        copy.wait()


def send_block(source, sinks, spots, device, part, out_sem):
    spot = spots[3 * device + part]
    half = sinks[0].shape[0]

    def copy(sink, place):
        pltpu.make_async_copy(source, sink.at[place], out_sem).start()

    keep, urgent, rest = sinks[3 * part : 3 * part + 3]
    pl.when(spot < half)(functools.partial(copy, keep, spot))
    pl.when((spot >= half) & (spot < half + half // 2))(
        functools.partial(copy, rest, spot - half)
    )
    pl.when(spot >= half + half // 2)(functools.partial(copy, urgent, spot - half - half // 2))


def sink_shapes(devices, block, dtype):
    half = devices // 2
    return [
        jax.ShapeDtypeStruct((count,) + block, dtype)
        for _ in range(3)
        for count in (half, half // 2, half // 2)
    ]


def wait_sinks(sinks, out_sem):
    for sink in sinks:
        pltpu.make_async_copy(sink, sink, out_sem).wait()


def backward_kernel(unit, seq_here, *refs):
    len_ref, spots, place_ref, x_ref, vec_ref, top_ref = refs[:6]
    wall_ref, qkv_ref, att_ref, n1_ref, pre_ref, n2_ref, stat_ref = refs[6:13]
    gin_ref, dvec_ref = refs[13:15]
    sinks = refs[15:24]
    wall, grads, parts, dqkv, qkv, att, n1, pre_all, in_sem, out_sem = refs[24:]
    rows, width = x_ref.shape
    length = rows // seq_here
    pairs = width // (2 * HEAD_DIM)
    low = jnp.bfloat16
    up = 4 * width
    ranges = [(n1_ref, n1)]
    for p in range(4):
        for first in (2 * up, up):
            rows_p = slice(first + width * p, first + width * (p + 1))
            ranges.append((wall_ref.at[rows_p], wall.at[rows_p]))
        ranges.append((pre_ref.at[p], pre_all.at[p]))
    out = slice(3 * width, up)
    ranges += [(att_ref, att), (wall_ref.at[out], wall.at[out]), (qkv_ref, qkv)]
    ranges += [(wall_ref.at[0 : 3 * width], wall.at[0 : 3 * width])]
    loads = [
        pltpu.make_async_copy(source, target, in_sem.at[k])
        for k, (source, target) in enumerate(ranges)
    ]
    for load in loads:
        load.start()

    def emit(first, last):
        for u in range(first // unit, last // unit):
            block = grads.at[u * unit : (u + 1) * unit]
            send_block(block, sinks, spots, u // 3, u % 3, out_sem)

    valid = valid_rows(len_ref, rows, seq_here)
    x = (x_ref[...].astype(jnp.float32) * valid).astype(low)
    stat_one = seq_here * pairs
    wide = lax.broadcasted_iota(jnp.int32, (rows, 128), 1)
    ends = stat_ref[1]
    inverse_one = jnp.sum(jnp.where(wide == stat_one, ends, 0.0), axis=-1, keepdims=True)
    inverse_two = jnp.sum(jnp.where(wide == stat_one + 1, ends, 0.0), axis=-1, keepdims=True)

    spot = lax.broadcasted_iota(jnp.int32, (rows, place_ref.shape[1]), 0)
    choose = (spot == place_ref[...]).astype(jnp.float32)
    d_output = valid * lax.dot_general(
        choose,
        top_ref[...],
        (((1,), (0,)), ((), ())),
        precision=lax.Precision.HIGHEST,
        preferred_element_type=jnp.float32,
    )
    normed = n2_ref[...]

    def sums(row, value):
        dvec_ref[row : row + 1, :] = jnp.sum(value, axis=0, keepdims=True)

    sums(10, d_output * normed)
    sums(11, d_output)
    d_resid = norm_back(d_output * vec_ref[10:11, :], normed, inverse_two)
    d_ffn = d_resid.astype(low)
    sums(9, d_ffn.astype(jnp.float32))
    d_hidden = d_resid
    loads[0].wait()
    normed = n1[...]
    hidden_low = (normed * vec_ref[3:4, :] + vec_ref[4:5, :]).astype(low)
    for p in range(4):
        for load in loads[1 + 3 * p : 4 + 3 * p]:
            load.wait()
        pre = pre_all[p]
        phi = gelu_phi(pre)
        act = (pre * phi).astype(low)
        down = slice(2 * up + width * p, 2 * up + width * (p + 1))
        grads[down, :] = contract_rows(act, d_ffn).astype(low)
        emit(down.start, down.stop)
        slope = phi + pre * jnp.exp(-0.5 * pre * pre) * 0.3989422804014327
        d_pre = (contract_cols(d_ffn, wall[down, :]) * slope).astype(low)
        sums(5 + p, d_pre.astype(jnp.float32))
        parts[width * p : width * (p + 1), :] = contract_rows(hidden_low, d_pre).astype(low)
        d_hidden = d_hidden + contract_cols(d_pre, wall[up + width * p : up + width * (p + 1), :])
    merge4 = deinterleave(4, 256)
    for b in range(width // 64):
        block = jnp.concatenate(
            [parts[width * p + 64 * b : width * p + 64 * b + 64, :] for p in range(4)], axis=0
        )
        grads[up + 256 * b : up + 256 * b + 256, :] = dot_nn(merge4, block).astype(low)
        if b % 3 == 2:
            emit(up + 256 * (b - 2), up + 256 * (b + 1))

    sums(3, d_hidden * normed)
    sums(4, d_hidden)
    d_resid = norm_back(d_hidden * vec_ref[3:4, :], normed, inverse_one)
    d_branch = d_resid.astype(low)
    sums(2, d_branch.astype(jnp.float32))
    for load in loads[13:]:
        load.wait()
    grads[3 * width : up, :] = contract_rows(att[...], d_branch).astype(low)
    emit(3 * width, up)
    d_att = contract_cols(d_branch, wall[3 * width : up, :]).astype(low)
    lane = lax.broadcasted_iota(jnp.int32, (2 * length, 128), 1)
    stats = stat_ref[0]
    for seq in range(seq_here):
        here = slice(seq * length, (seq + 1) * length)
        for g in range(pairs):
            cols = [slice(width * p + 128 * g, width * p + 128 * g + 128) for p in range(3)]
            query, key, value = (qkv[here, c] for c in cols)
            query = stack_pair(query)
            log_sum = jnp.sum(
                jnp.where(lane == seq * pairs + g, stats, 0.0), axis=-1, keepdims=True
            )
            probs = jnp.exp(pair_scores(query, key, len_ref[seq]) - log_sum)
            d_heads = stack_pair(d_att[here, 128 * g : 128 * g + 128])
            d_probs = contract_cols(d_heads, value)
            dqkv[here, cols[2]] = contract_rows(probs.astype(low), d_heads).astype(low)
            delta = jnp.sum(d_probs * probs, axis=-1, keepdims=True)
            d_scores = (probs * (d_probs - delta)).astype(low)
            scale = HEAD_DIM ** (-0.5)
            dqkv[here, cols[0]] = (join_pair(dot_nn(d_scores, key)) * scale).astype(low)
            dqkv[here, cols[1]] = (contract_rows(d_scores, query) * scale).astype(low)
    sums(0, dqkv[:, :width].astype(jnp.float32))
    sums(1, dqkv[:, 2 * width :].astype(jnp.float32))
    for p in range(3):
        d_part = dqkv[:, width * p : width * (p + 1)]
        parts[width * p : width * (p + 1), :] = contract_rows(x, d_part).astype(low)
    merge3 = deinterleave(3, 384)
    for b in range(width // 128):
        block = jnp.concatenate(
            [parts[width * p + 128 * b : width * p + 128 * b + 128, :] for p in range(3)], axis=0
        )
        grads[384 * b : 384 * b + 384, :] = dot_nn(merge3, block).astype(low)
        if b % 2 == 1:
            emit(384 * (b - 1), 384 * (b + 1))
    total = d_resid
    for p in range(3):
        d_part = dqkv[:, width * p : width * (p + 1)]
        total = total + contract_cols(d_part, wall[width * p : width * (p + 1), :])
    gin_ref[...] = total * valid
    wait_sinks(sinks, out_sem)


def call_forward(me, lengths, places, rows, vecs, gathered, devices, seq_here):
    count, width = rows.shape
    pieces = [(part, piece, masks) for part, own in enumerate(gathered) for piece, masks in own]
    plan = tuple((part, piece.shape[1], tuple(masks)) for part, piece, masks in pieces)
    total = 12 * width
    vmem = pl.BlockSpec(memory_space=pltpu.VMEM)
    smem = pl.BlockSpec(memory_space=pltpu.SMEM)
    hbm = pl.BlockSpec(memory_space=pl.ANY)
    low, full = jnp.bfloat16, jnp.float32
    outs = pl.pallas_call(
        functools.partial(forward_kernel, plan, devices // 4, seq_here),
        out_shape=[
            *[jax.ShapeDtypeStruct((1, places.shape[1], width // 3), low)] * 3,
            jax.ShapeDtypeStruct((total, width), low),
            jax.ShapeDtypeStruct((count, 3 * width), low),
            jax.ShapeDtypeStruct((count, width), low),
            jax.ShapeDtypeStruct((count, width), full),
            jax.ShapeDtypeStruct((4, count, width), full),
            jax.ShapeDtypeStruct((count, width), full),
            jax.ShapeDtypeStruct((2, count, 128), full),
        ],
        in_specs=[smem, smem, vmem, vmem, vmem] + [hbm] * len(pieces),
        out_specs=[vmem] * 3 + [hbm] * 5 + [vmem] * 2,
        scratch_shapes=[
            pltpu.VMEM((total, width), low),
            pltpu.VMEM((7 * width, width), low),
            pltpu.VMEM((count, 3 * width), low),
            pltpu.VMEM((count, width), low),
            pltpu.VMEM((count, width), full),
            pltpu.VMEM((4, count, width), full),
            pltpu.SemaphoreType.DMA((2,)),
            pltpu.SemaphoreType.DMA((11,)),
        ],
        compiler_params=pltpu.CompilerParams(vmem_limit_bytes=58 * 2**20),
        cost_estimate=pl.CostEstimate(
            flops=2 * count * total * width, bytes_accessed=48 * 2**20, transcendentals=0
        ),
    )(me, lengths, places, rows, vecs, *[piece for _, piece, _ in pieces])
    return *outs[:3], outs[3:]


def call_backward(lengths, spots, places, rows, vecs, top, saved, unit, seq_here):
    count, width = rows.shape
    total = 12 * width
    vmem = pl.BlockSpec(memory_space=pltpu.VMEM)
    smem = pl.BlockSpec(memory_space=pltpu.SMEM)
    hbm = pl.BlockSpec(memory_space=pl.ANY)
    low, full = jnp.bfloat16, jnp.float32
    return pl.pallas_call(
        functools.partial(backward_kernel, unit, seq_here),
        out_shape=[
            jax.ShapeDtypeStruct((count, width), full),
            jax.ShapeDtypeStruct((12, width), full),
        ]
        + sink_shapes(total // unit // 3, (unit, width), low),
        in_specs=[smem, smem, vmem, vmem, vmem, vmem] + [hbm] * 5 + [vmem] * 2,
        out_specs=[vmem, vmem] + [hbm] * 9,
        scratch_shapes=[
            pltpu.VMEM((total, width), low),
            pltpu.VMEM((total, width), low),
            pltpu.VMEM((4 * width, width), low),
            pltpu.VMEM((count, 3 * width), low),
            pltpu.VMEM((count, 3 * width), low),
            pltpu.VMEM((count, width), low),
            pltpu.VMEM((count, width), full),
            pltpu.VMEM((4, count, width), full),
            pltpu.SemaphoreType.DMA((17,)),
            pltpu.SemaphoreType.DMA,
        ],
        compiler_params=pltpu.CompilerParams(vmem_limit_bytes=58 * 2**20),
        cost_estimate=pl.CostEstimate(
            flops=4 * count * total * width, bytes_accessed=48 * 2**20, transcendentals=0
        ),
    )(lengths, spots, places, rows, vecs, top, *saved)


def turn_lanes(shift, width):
    source = lax.broadcasted_iota(jnp.int32, (width, width), 0) + shift
    source = jnp.where(source >= width, source - width, source)
    return (source == lax.broadcasted_iota(jnp.int32, (width, width), 1)).astype(jnp.bfloat16)


def table_kernel(embed_here, shift_ref, rows_ref, ends_ref, table_ref, owned_ref, tall):
    count, width = table_ref.shape
    here = rows_ref.shape[0]
    shift = shift_ref[0]
    tall[here:, :] = jnp.zeros((tall.shape[0] - here, width), jnp.float32)
    tall[8 : 8 + here, :] = rows_ref[...].astype(jnp.float32)
    tall[7:8, :] = ends_ref[0:1, :]
    tall[7 + here : 8 + here, :] = tall[7 + here : 8 + here, :] + ends_ref[1:2, :]
    tall[8 + here : 9 + here, :] = ends_ref[2:3, :]
    lane = lax.broadcasted_iota(jnp.int32, (count, width), 1)
    rolled = jnp.where(lane < width - shift, tall[8 : 8 + count, :], tall[7 : 7 + count, :])
    table = dot_nn(rolled.astype(jnp.bfloat16), turn_lanes(shift, width))
    start = lax.broadcasted_iota(jnp.int32, (count, 1), 0) * width - shift
    owned = (start >= 0) & (start < embed_here)
    table_ref[...] = table.astype(jnp.bfloat16)
    owned_ref[...] = jnp.where(owned, table, 0.0).astype(jnp.bfloat16)


def call_table(shift, rows, ends, count, embed_here):
    width = rows.shape[1]
    vmem = pl.BlockSpec(memory_space=pltpu.VMEM)
    smem = pl.BlockSpec(memory_space=pltpu.SMEM)
    return pl.pallas_call(
        functools.partial(table_kernel, embed_here),
        out_shape=[jax.ShapeDtypeStruct((count, width), jnp.bfloat16)] * 2,
        in_specs=[smem, vmem, vmem],
        out_specs=[vmem] * 2,
        scratch_shapes=[pltpu.VMEM((count + 16, width), jnp.float32)],
        compiler_params=pltpu.CompilerParams(vmem_limit_bytes=22 * 2**20),
        cost_estimate=pl.CostEstimate(
            flops=32 * count * width * width, bytes_accessed=40 * 2**20, transcendentals=0
        ),
    )(shift, rows, ends)


def eye_mask():
    return lax.broadcasted_iota(jnp.int32, (128, 128), 0) == lax.broadcasted_iota(
        jnp.int32, (128, 128), 1
    )


def to_row(column, eye):
    return jnp.concatenate(
        [
            jnp.sum(jnp.where(eye, column[k : k + 128], 0.0), axis=0, keepdims=True)
            for k in range(0, column.shape[0], 128)
        ],
        axis=1,
    )


def to_column(row, eye):
    return jnp.concatenate(
        [
            jnp.sum(jnp.where(eye, row[:, k : k + 128], 0.0), axis=1, keepdims=True)
            for k in range(0, row.shape[1], 128)
        ],
        axis=0,
    )


def logits_kernel(plan, embed_here, picks, span, *refs):
    me_ref, shift_ref, table_ref = refs[:3]
    blocks = refs[3 : 3 + len(plan)]
    picked_ref, expo_ref, stat_ref, top_ref, picked, expo_all, in_sem, out_sem = refs[
        3 + len(plan) :
    ]
    count, width = table_ref.shape
    me, shift = me_ref[0], shift_ref[0]
    group = 4
    for (part, masks), block in zip(plan, blocks):
        cols = pl.ds(part * block.shape[2], block.shape[2])
        for place, mask in enumerate(masks):
            device = me ^ mask
            pltpu.make_async_copy(
                block.at[place], picked.at[device, :, cols], in_sem
            ).start()
    whole = embed_here // width // 128 * 128
    eye = eye_mask()
    row_start = lax.broadcasted_iota(jnp.int32, (1, count), 1) * width - shift
    touched = (row_start < embed_here)[:, whole:]
    owned = (row_start >= 0)[:, :128]
    tops, sums, copies = [], [], []

    def save(source, target):
        copies.append(pltpu.make_async_copy(source, target, out_sem.at[len(copies)]))
        copies[-1].start()

    step = group * picks
    pltpu.make_async_copy(picked, picked, in_sem).wait()
    save(picked, picked_ref)
    for k in range(picked.shape[0] // group):
        here = slice(k * step, (k + 1) * step)
        rows = jnp.concatenate([picked[group * k + d, :picks, :] for d in range(group)], axis=0)
        logits = contract_cols(rows, table_ref[...])
        logits = jnp.concatenate(
            [logits[:, :whole], jnp.where(touched, logits[:, whole:], -1e30)], axis=1
        )
        top = jnp.max(logits, axis=1, keepdims=True)
        expo = jnp.exp(logits - top)
        expo_all[here, :] = expo
        save(expo_all.at[here], expo_ref.at[here])
        ends = jnp.where(owned, expo[:, :128], 0.0)
        total = jnp.sum(jnp.concatenate([ends, expo[:, 128:]], axis=1), axis=1, keepdims=True)
        tops.append(to_row(top, eye))
        sums.append(to_row(top + jnp.log(total), eye))
    join = span // step

    def blocks_of(own):
        return jnp.concatenate(
            [jnp.concatenate(own[k : k + join], axis=1) for k in range(0, len(own), join)], axis=0
        )

    top_ref[...] = blocks_of(tops)
    stats = blocks_of(sums)
    for device in range(stat_ref.shape[0]):
        stat_ref[device] = stats
    for copy in copies:
        copy.wait()


def call_logits(me, shift, table, gathered, picks, embed_here, devices):
    count, width = table.shape
    pieces = [(part, piece, masks) for part, own in enumerate(gathered) for piece, masks in own]
    plan = tuple((part, tuple(masks)) for part, _, masks in pieces)
    block = pieces[0][1].shape[1]
    rows = devices * picks
    span = rows // 8
    vmem = pl.BlockSpec(memory_space=pltpu.VMEM)
    smem = pl.BlockSpec(memory_space=pltpu.SMEM)
    hbm = pl.BlockSpec(memory_space=pl.ANY)
    low, full = jnp.bfloat16, jnp.float32
    return pl.pallas_call(
        functools.partial(logits_kernel, plan, embed_here, picks, span),
        out_shape=[
            jax.ShapeDtypeStruct((devices, block, width), low),
            jax.ShapeDtypeStruct((rows, count), full),
            jax.ShapeDtypeStruct((devices, 8, span), full),
            jax.ShapeDtypeStruct((8, span), full),
        ],
        in_specs=[smem, smem, vmem] + [hbm] * len(pieces),
        out_specs=[hbm, hbm, vmem, vmem],
        scratch_shapes=[
            pltpu.VMEM((devices, block, width), low),
            pltpu.VMEM((rows, count), full),
            pltpu.SemaphoreType.DMA,
            pltpu.SemaphoreType.DMA((devices // 4 + 1,)),
        ],
        compiler_params=pltpu.CompilerParams(vmem_limit_bytes=58 * 2**20),
        cost_estimate=pl.CostEstimate(
            flops=2 * rows * count * width, bytes_accessed=16 * 2**20, transcendentals=0
        ),
    )(me, shift, table, *[piece for _, piece, _ in pieces])


def terms_kernel(plan, picks, me_ref, *refs):
    stat_ref, top_ref, expo_ref, owned_ref, label_ref, scale_ref = refs[:6]
    sinks = refs[6:15]
    terms, out_sem = refs[15:]
    span, count = expo_ref.shape
    width = owned_ref.shape[1]
    chunks = terms.shape[0]
    group = span // picks
    me = me_ref[0]
    step = pl.program_id(0)
    chunk = step ^ lax.div(me, group)
    scales = []
    for half in range(2):
        row = 2 * chunk + half
        sums = stat_ref[:, pl.ds(row, 1), :]
        top = jnp.max(sums, axis=0)
        whole = top + jnp.log(jnp.sum(jnp.exp(sums - top[None]), axis=0))
        scales.append(jnp.exp(top_ref[pl.ds(row, 1), :] - whole))
    scale = jnp.concatenate(scales, axis=1)
    used = label_ref[1:2, :]
    scale = scale * used
    scale_ref[...] = jnp.broadcast_to(scale, scale_ref.shape)
    label = jnp.where(used > 0, label_ref[0:1, :], -1.0)
    eye = eye_mask()
    part = span // 2
    lane = lax.broadcasted_iota(jnp.int32, (part, count), 1)
    for k in range(0, span, part):
        here = slice(k, k + part)
        probs = expo_ref[here, :] * to_column(scale[:, here], eye)
        hot = lane == to_column(label[:, here], eye).astype(jnp.int32)
        d_logits = jnp.where(hot, probs - 1.0, probs).astype(jnp.bfloat16)
        terms[step, here, :] = dot_nn(d_logits, owned_ref[...]).astype(jnp.bfloat16)
    cut = width // 3
    half = sinks[0].shape[0]

    def send(now):
        for b in range(group):
            row = pl.multiple_of((b ^ lax.rem(me, group)) * picks, 16)
            for part, bits in enumerate(plan):
                relative = now * group + b
                spot = sum(
                    1 << (len(bits) - 1 - k) for k, bit in enumerate(bits) if relative & bit
                )
                kind = 0 if spot < half else (2 if spot < half + half // 2 else 1)
                spot = spot - (0, half + half // 2, half)[kind]
                pltpu.make_async_copy(
                    terms.at[now, pl.ds(row, picks), part * cut : (part + 1) * cut],
                    sinks[3 * part + kind].at[spot],
                    out_sem,
                ).start()

    for now in range(chunks):
        pl.when(step == now)(functools.partial(send, now))

    @pl.when(step == chunks - 1)
    def _():
        wait_sinks(sinks, out_sem)


def call_terms(me, stats, tops, expo, owned, labels, plan, picks):
    rows, count = expo.shape
    width = owned.shape[1]
    devices = stats.shape[0]
    span = 2 * stats.shape[2]
    hbm = pl.BlockSpec(memory_space=pl.ANY)
    low = jnp.bfloat16
    group = span // picks

    def tile(lanes):
        return pl.BlockSpec((span, lanes), lambda k, me: (k ^ lax.div(me[0], group), 0))

    row_tile = pl.BlockSpec((8, span), lambda k, me: (0, k ^ lax.div(me[0], group)))
    return pl.pallas_call(
        functools.partial(terms_kernel, plan, picks),
        grid_spec=pltpu.PrefetchScalarGridSpec(
            num_scalar_prefetch=1,
            grid=(rows // span,),
            in_specs=[
                pl.BlockSpec(stats.shape, lambda k, me: (0, 0, 0)),
                pl.BlockSpec(tops.shape, lambda k, me: (0, 0)),
                tile(count),
                pl.BlockSpec(owned.shape, lambda k, me: (0, 0)),
                row_tile,
            ],
            out_specs=[row_tile] + [hbm] * 9,
            scratch_shapes=[
                pltpu.VMEM((rows // span, span, width), low),
                pltpu.SemaphoreType.DMA,
            ],
        ),
        out_shape=[jax.ShapeDtypeStruct((8, rows), jnp.float32)]
        + sink_shapes(devices, (picks, width // 3), low),
        compiler_params=pltpu.CompilerParams(vmem_limit_bytes=48 * 2**20),
        cost_estimate=pl.CostEstimate(
            flops=2 * rows * count * width, bytes_accessed=12 * 2**20, transcendentals=0
        ),
    )(me, stats, tops, expo, owned, labels)


def embed_kernel(picks, shift_ref, expo_ref, scale_ref, label_ref, picked_ref, out_ref, wide, turn):
    here, width = out_ref.shape
    rows, count = expo_ref.shape
    shift = shift_ref[0]
    chunk = pl.program_id(0)

    @pl.when(chunk == 0)
    def _():
        turn[...] = turn_lanes(shift, width)

    eye = eye_mask()
    probs = expo_ref[...] * to_column(scale_ref[0:1, :], eye)
    lane = lax.broadcasted_iota(jnp.int32, (rows, count), 1)
    used = label_ref[1:2, :]
    label = jnp.where(used > 0, label_ref[0:1, :], -1.0)
    hot = lane == to_column(label, eye).astype(jnp.int32)
    terms = jnp.where(hot, probs - 1.0, probs).astype(jnp.bfloat16)
    picked = jnp.concatenate([picked_ref[d, :picks, :] for d in range(rows // picks)], axis=0)
    turned = contract_cols(picked, turn[...]).astype(jnp.bfloat16)
    total = contract_rows(terms, turned)

    @pl.when(chunk == 0)
    def _():
        wide[...] = total

    @pl.when(chunk > 0)
    def _():
        wide[...] = wide[...] + total

    @pl.when(chunk == pl.num_programs(0) - 1)
    def _():
        lane = lax.broadcasted_iota(jnp.int32, (here, width), 1)
        out_ref[...] = jnp.where(lane < width - shift, wide[:here, :], wide[1 : here + 1, :])


def call_embed(shift, expo, scale, labels, picked, picks, here):
    rows, count = expo.shape
    devices, block, width = picked.shape
    smem = pl.BlockSpec(memory_space=pltpu.SMEM)
    step = rows // 8
    row_tile = pl.BlockSpec((8, step), lambda k: (0, k))
    return pl.pallas_call(
        functools.partial(embed_kernel, picks),
        grid=(8,),
        out_shape=jax.ShapeDtypeStruct((here, width), jnp.float32),
        in_specs=[
            smem,
            pl.BlockSpec((step, count), lambda k: (k, 0)),
            row_tile,
            row_tile,
            pl.BlockSpec((devices // 8, block, width), lambda k: (k, 0, 0)),
        ],
        out_specs=pl.BlockSpec((here, width), lambda k: (0, 0)),
        scratch_shapes=[
            pltpu.VMEM((count, width), jnp.float32),
            pltpu.VMEM((width, width), jnp.bfloat16),
        ],
        compiler_params=pltpu.CompilerParams(vmem_limit_bytes=58 * 2**20),
        cost_estimate=pl.CostEstimate(
            flops=16 * rows * count * width, bytes_accessed=64 * 2**20, transcendentals=0
        ),
    )(shift, expo, scale, labels, picked)


def step_kernel(counts, *refs):
    weight_ref, first_ref, second_ref = refs[:3]
    grad_ref, step_ref = refs[-2:]
    start, row = 3, 0
    width = refs[3].shape[2]
    share = width // 128
    for count in counts:
        total = add_terms([ref[0] for ref in refs[start : start + count]])
        rows = total.shape[0]
        for q in range(share):
            grad_ref[pl.ds(share * row + q, rows, stride=share), :] = total[
                :, 128 * q : 128 * q + 128
            ]
        start, row = start + count, row + rows
    step_ref[...] = adam_step(
        weight_ref[...], grad_ref[...], first_ref[...], second_ref[...], float(ADAM_STEP), decay_rate
    )


def call_step(weight, first, second, terms):
    shape = jax.ShapeDtypeStruct((weight.shape[0] // 128, 128), jnp.float32)
    vmem = pl.BlockSpec(memory_space=pltpu.VMEM)
    given = [value.reshape(shape.shape) for value in (weight, first, second)]
    blocks = [term for own in terms for term in own]
    first_block = pl.BlockSpec((1,) + blocks[0].shape[1:], lambda k: (0, 0, 0))
    grad, step = pl.pallas_call(
        functools.partial(step_kernel, [len(own) for own in terms]),
        grid=(1,),
        out_shape=[shape] * 2,
        in_specs=[vmem] * 3 + [first_block] * len(blocks),
        out_specs=[vmem] * 2,
        compiler_params=pltpu.CompilerParams(vmem_limit_bytes=24 * 2**20),
    )(*given, *blocks)
    return grad.reshape(-1), step.reshape(-1)


def plain_forward(mats_all, vecs_all, block_input, span_lengths):
    seq_here, length, width = block_input.shape
    rows_here = seq_here * length
    heads_count = width // HEAD_DIM
    head_scale = HEAD_DIM ** (-0.5)
    low = jnp.bfloat16
    w_qkv, w_out, w_up, w_down = split_mats(mats_all)
    bias_q, bias_v, bias_out, gain_one, shift_one, bias_up, bias_down, gain_two, shift_two = (
        split_vecs(vecs_all)
    )
    valid = jnp.arange(length)[None, :] < span_lengths[:, None]
    valid_col = valid.reshape(rows_here, 1).astype(jnp.float32)
    tok_rows = (block_input * valid[:, :, None].astype(low)).reshape(rows_here, width)
    qkv_bias = jnp.concatenate([bias_q, jnp.zeros((width,), jnp.float32), bias_v])
    projected = (jnp.dot(tok_rows, w_qkv, preferred_element_type=jnp.float32) + qkv_bias).astype(
        low
    )
    shaped = projected.reshape(seq_here, length, 3, heads_count, HEAD_DIM)
    queries = shaped[:, :, 0]
    key_rows = shaped[:, :, 1]
    value_rows = shaped[:, :, 2]
    key_valid = valid[:, None, None, :]

    def make_scores():
        raw = (
            jnp.einsum("sqhd,skhd->shqk", queries, key_rows, preferred_element_type=jnp.float32)
            * head_scale
        )
        return jnp.where(key_valid, raw, -1e30)

    scores = make_scores()
    row_max = jnp.max(scores, axis=-1, keepdims=True)
    expo_vals = jnp.exp(scores - row_max)
    row_sum = jnp.sum(expo_vals, axis=-1, keepdims=True)
    row_lse = row_max + jnp.log(row_sum)
    attn_probs = (expo_vals / row_sum).astype(low)
    attended = (
        jnp.einsum("shqk,skhd->sqhd", attn_probs, value_rows, preferred_element_type=jnp.float32)
        .reshape(rows_here, width)
        .astype(low)
    )
    branch = jnp.dot(attended, w_out, preferred_element_type=jnp.float32) + bias_out
    normed_one, inverse_one = center_scale(tok_rows.astype(jnp.float32) + branch)
    hidden_one = normed_one * gain_one + shift_one
    hidden_low = hidden_one.astype(low)
    pre_act = jnp.dot(hidden_low, w_up, preferred_element_type=jnp.float32) + bias_up
    act_low = jax.nn.gelu(pre_act, approximate=False).astype(low)
    ffn_out = jnp.dot(act_low, w_down, preferred_element_type=jnp.float32) + bias_down
    normed_two, inverse_two = center_scale(hidden_one + ffn_out)
    output = (normed_two * gain_two + shift_two) * valid_col

    def plain_backward(d_output):
        d_gain_two = jnp.sum(d_output * normed_two, axis=0)
        d_shift_two = jnp.sum(d_output, axis=0)
        d_resid_two = norm_back(d_output * gain_two, normed_two, inverse_two)
        d_ffn = d_resid_two.astype(low)
        d_bias_down = jnp.sum(d_ffn.astype(jnp.float32), axis=0)
        d_w_down = contract_rows(act_low, d_ffn)
        d_act = contract_cols(d_ffn, w_down)
        d_pre = (d_act * gelu_slope(pre_act)).astype(low)
        d_bias_up = jnp.sum(d_pre.astype(jnp.float32), axis=0)
        d_w_up = contract_rows(hidden_low, d_pre)
        d_hidden = contract_cols(d_pre, w_up) + d_resid_two
        d_gain_one = jnp.sum(d_hidden * normed_one, axis=0)
        d_shift_one = jnp.sum(d_hidden, axis=0)
        d_resid_one = norm_back(d_hidden * gain_one, normed_one, inverse_one)
        d_branch = d_resid_one.astype(low)
        d_bias_out = jnp.sum(d_branch.astype(jnp.float32), axis=0)
        d_w_out = contract_rows(attended, d_branch)
        d_attended = (
            contract_cols(d_branch, w_out).astype(low).reshape(seq_here, length, heads_count, HEAD_DIM)
        )
        probs_again = jnp.exp(make_scores() - row_lse)
        probs_low = probs_again.astype(low)
        d_probs = jnp.einsum(
            "sqhd,skhd->shqk", d_attended, value_rows, preferred_element_type=jnp.float32
        )
        d_values = jnp.einsum(
            "shqk,sqhd->skhd", probs_low, d_attended, preferred_element_type=jnp.float32
        )
        row_delta = jnp.sum(d_probs * probs_again, axis=-1, keepdims=True)
        d_scores = (probs_again * (d_probs - row_delta)).astype(low)
        d_queries = (
            jnp.einsum("shqk,skhd->sqhd", d_scores, key_rows, preferred_element_type=jnp.float32)
            * head_scale
        )
        d_keys = (
            jnp.einsum("shqk,sqhd->skhd", d_scores, queries, preferred_element_type=jnp.float32)
            * head_scale
        )
        d_qkv = jnp.concatenate(
            [
                d_queries.reshape(rows_here, width),
                d_keys.reshape(rows_here, width),
                d_values.reshape(rows_here, width),
            ],
            axis=1,
        ).astype(low)
        d_qkv_float = d_qkv.astype(jnp.float32)
        d_bias_q = jnp.sum(d_qkv_float[:, :width], axis=0)
        d_bias_v = jnp.sum(d_qkv_float[:, 2 * width :], axis=0)
        d_w_qkv = contract_rows(tok_rows, d_qkv)
        grad_input = ((contract_cols(d_qkv, w_qkv) + d_resid_one) * valid_col).reshape(
            seq_here, length, width
        )
        d_mats = jnp.concatenate(
            [
                piece.astype(low).reshape(-1, width)
                for piece in (d_w_qkv, d_w_out, d_w_up, d_w_down)
            ]
        )
        d_vecs = jnp.concatenate(
            [
                d_bias_q,
                d_bias_v,
                d_bias_out,
                d_gain_one,
                d_shift_one,
                d_bias_up,
                d_bias_down,
                d_gain_two,
                d_shift_two,
            ]
        )
        return grad_input, d_mats, d_vecs

    return output, plain_backward


def on_device(
    names,
    core,
    block_input,
    span_lengths,
    mlm_positions,
    mlm_labels,
    span_pairs,
    layer_mats,
    vectors,
    embedding,
    mom1_mats,
    mom2_mats,
    mom1_vecs,
    mom2_vecs,
    mom1_embed,
    mom2_embed,
):
    seq_here, length, width = block_input.shape
    rows_here = seq_here * length
    devices = 2 ** len(names)
    me = lax.axis_index(names)
    orders = bit_orders(names, core, ((0, 3, 2, 1), (0, 2, 1, 3), (0, 1, 3, 2)))
    head_orders = bit_orders(names, core, ((3, 0, 1, 2), (0, 2, 3, 1), (0, 1, 2, 3)))
    slots = mlm_positions.shape[1]
    picks_here = seq_here * slots
    low = jnp.bfloat16

    third = layer_mats.shape[0] // width // 3
    by_kernel = third % 16 == 0
    vec_here = vectors.shape[0]
    mats_low = layer_mats.astype(low).reshape(3, third, width)

    labels_flat = mlm_labels.reshape(-1)
    common = jnp.concatenate(
        [
            value.astype(low)
            for value in (
                vectors,
                labels_flat // 256,
                labels_flat % 256,
                span_pairs // 256,
                span_pairs % 256,
                span_lengths // 4,
            )
        ]
    )
    sizes = [vec_here, picks_here, picks_here, seq_here, seq_here, seq_here]
    common = jnp.pad(common, (0, width - common.shape[0]))
    others = jnp.arange(devices)[:, None]
    right, left = (me + 1) % devices, (me + devices - 1) % devices
    border = jnp.where(
        others == right,
        embedding[-width:].astype(low),
        jnp.where(others == left, embedding[:width].astype(low), jnp.zeros((), low)),
    )
    small = jnp.stack([jnp.broadcast_to(common, border.shape), border], axis=1)

    def share(small):
        return lax.all_to_all(small, names, 0, 0, tiled=True)

    embed_here = embedding.shape[0]
    shifted_rows = -(-embed_here // width)
    over = shifted_rows * width - embed_here
    shift = (me * (embed_here % width)) % width
    first_row = me * (embed_here // width) + (me * (embed_here % width)) // width

    def table_shard(embedding):
        return jnp.pad(embedding.astype(low), (0, over)).reshape(shifted_rows, width)


    def unpack(small_all, first, last):
        starts = [sum(sizes[:k]) for k in range(len(sizes))]
        return [
            small_all[:, 0, starts[k] : starts[k] + sizes[k]].reshape(-1)
            for k in range(first, last)
        ]

    def unpack_layer(small_all):
        (vecs_all,) = unpack(small_all, 0, 1)
        from_left = lax.dynamic_index_in_dim(small_all[:, 1], left, 0, False)
        from_right = lax.dynamic_index_in_dim(small_all[:, 1], right, 0, False)
        right_rows = jnp.pad(from_right, (width - over, over)).reshape(2, width)
        return vecs_all.astype(jnp.float32).reshape(-1, width), from_left, right_rows

    def unpack_heads(small_all):
        labels_high, labels_low, pairs_high, pairs_low, quarter_all = (
            value.astype(jnp.int32) for value in unpack(small_all, 1, 6)
        )
        used = (jnp.arange(slots)[None, :] < quarter_all[:, None]).reshape(-1)
        row_of = labels_high * 256 + labels_low - first_row
        return row_of, used, pairs_high * 256 + pairs_low

    seq_start = jnp.arange(seq_here, dtype=jnp.int32) * length

    def span_terms(cls_all, pairs_all):
        span_scale = 2.0 / math.sqrt(width)
        columns = jnp.arange(cls_all.shape[0])
        sims = contract_cols(cls_all, cls_all) * span_scale
        sims = jnp.where(columns[None, :] == columns[:, None], -1e30, sims)
        partner_hot = (columns[None, :] == pairs_all[:, None]).astype(jnp.float32)
        d_sims = (jax.nn.softmax(sims, axis=-1) - partner_hot).astype(low)
        mine = me * seq_here
        d_sims_rows = lax.dynamic_slice_in_dim(d_sims, mine, seq_here, 0)
        d_sims_cols = lax.dynamic_slice_in_dim(d_sims, mine, seq_here, 1)
        return (
            jnp.dot(d_sims_rows, cls_all, preferred_element_type=jnp.float32)
            + contract_rows(d_sims_cols, cls_all)
        ) * span_scale

    step_float = float(ADAM_STEP)

    def embed_step(grad_rows):
        grad = grad_rows.reshape(-1)[:embed_here]
        return grad, adam_step(embedding, grad, mom1_embed, mom2_embed, step_float, decay_rate)

    def vector_terms(d_vecs):
        return lax.all_to_all(d_vecs.reshape(devices, 1, vec_here), names, 0, 0, tiled=True)

    cut = width // 3
    columns = [slice(k * cut, (k + 1) * cut) for k in range(3)]
    back_orders = [order[::-1] for order in orders]
    if by_kernel:
        lone = me.astype(jnp.int32).reshape(1)
        lone_shift = shift.astype(jnp.int32).reshape(1)
        tok_rows = block_input.reshape(rows_here, width)
        relative = jnp.arange(devices, dtype=jnp.int32) ^ me.astype(jnp.int32)
        spots = jnp.stack(
            [
                sum(
                    ((relative & device_mask(name, names)) != 0).astype(jnp.int32)
                    << (len(names) - 1 - k)
                    for k, name in enumerate(order)
                )
                for order in back_orders
            ],
            axis=1,
        ).reshape(-1)
        places = jnp.concatenate(
            [
                (mlm_positions + seq_start[:, None]).reshape(-1),
                seq_start,
                jnp.full((16 - seq_here,), -1, jnp.int32),
            ]
        )
        table_rows = -(-(shifted_rows + 1) // 128) * 128

        def prepare(embedding, small_all):
            vec_rows, from_left, right_rows = unpack_layer(small_all)
            ends = jnp.pad(
                jnp.concatenate([from_left[None], right_rows]).astype(jnp.float32),
                ((0, 5), (0, 0)),
            )
            shifted = table_shard(embedding)
            table, owned = call_table(lone_shift, shifted, ends, table_rows, embed_here)
            return table, owned, vec_rows, small_all

        gathered, (table, owned, vec_rows, small_all) = gather_relative(
            mats_low[:, None], orders, names, (embedding, small), share, prepare, True
        )
        *heads, saved = call_forward(
            lone, span_lengths, places[None], tok_rows, vec_rows, gathered, devices, seq_here
        )
        heads_all, _ = gather_relative(heads, head_orders, names)
        picked, expo, stats, tops = call_logits(
            lone, lone_shift, table, heads_all, picks_here, embed_here, devices
        )
        stats, small_all = lax.optimization_barrier((stats, small_all))
        row_of, used, pairs_all = unpack_heads(small_all)
        labels = jnp.pad(
            jnp.stack([row_of.astype(jnp.float32), used.astype(jnp.float32)]), ((0, 6), (0, 0))
        )
        stats = lax.all_to_all(stats, names, 0, 0, tiled=True)
        head_back = [order[::-1] for order in head_orders]
        plan = tuple(tuple(device_mask(name, names) for name in order) for order in head_back)
        scale, *sinks = call_terms(
            lone, stats, tops, expo, owned, labels, plan, picks_here
        )
        d_cls = span_terms(
            picked[:, picks_here : picks_here + seq_here].reshape(-1, width), pairs_all
        )
        d_parts, _ = reduce_relative(
            sinks[0::3], list(zip(sinks[1::3], sinks[2::3])), head_back
        )
        d_parts = [add_terms([term[0] for term in terms]) for terms in d_parts]
        top = jnp.concatenate(
            [jnp.concatenate(d_parts, axis=1), jnp.pad(d_cls, ((0, 16 - seq_here), (0, 0)))]
        )
        grad_input, d_vecs, *sinks = call_backward(
            span_lengths, spots, places[None], tok_rows, vec_rows, top, saved, third, seq_here
        )
        grad_input = grad_input.reshape(seq_here, length, width)
        def table_grad(state):
            expo, picked, d_vecs = state
            grad_embed = call_embed(
                lone_shift, expo, scale, labels, picked, picks_here, shifted_rows
            )
            grad_embed, d_vecs = lax.optimization_barrier((grad_embed, d_vecs))
            return grad_embed, vector_terms(d_vecs)

        def table_step(state):
            grad_embed, terms = state
            return *embed_step(grad_embed), jnp.sum(terms, axis=(0, 1))

        terms, (grad_embed, step_embed, grad_vecs) = reduce_relative(
            sinks[0::3],
            list(zip(sinks[1::3], sinks[2::3])),
            back_orders,
            (expo, picked, d_vecs),
            {0: table_grad, len(names) - 2: table_step},
            1,
        )
        grad_mats, step_mats = call_step(layer_mats, mom1_mats, mom2_mats, terms)
    else:
        small_all = share(small)
        vec_rows, from_left, right_rows = unpack_layer(small_all)
        row_of, used, pairs_all = unpack_heads(small_all)
        same_row = (jnp.arange(width) < width - shift)[None, :]
        tall = jnp.concatenate(
            [from_left[None], table_shard(embedding), jnp.zeros((1, width), low)]
        )
        tall = tall.at[shifted_rows : shifted_rows + 2].add(right_rows)
        lanes = jnp.arange(width)
        turn = ((lanes[:, None] + shift) % width == lanes[None, :]).astype(low)
        rolled = jnp.where(same_row, tall[1:], tall[:-1])
        table = jnp.dot(rolled, turn, preferred_element_type=jnp.float32).astype(low)
        row_start = jnp.arange(shifted_rows + 1) * width - shift
        owned = (row_start >= 0) & (row_start < embed_here)
        touched = (row_start + width > 0) & (row_start < embed_here)
        gathered = [gather_bits(mats_low[k], orders[k], names) for k in range(3)]
        mats_all = jnp.stack(gathered, axis=1).reshape(-1)
        output, plain_backward = plain_forward(
            mats_all, vec_rows.reshape(-1), block_input, span_lengths
        )
        output_seq = output.reshape(seq_here, length, width)
        picked_here = jnp.take_along_axis(output_seq, mlm_positions[:, :, None], axis=1)
        heads = jnp.concatenate([picked_here.reshape(-1, width), output_seq[:, 0, :]]).astype(low)
        heads_all = jnp.concatenate(
            [gather_bits(heads[:, c], order, names) for c, order in zip(columns, orders)], axis=2
        )
        picked = heads_all[:, :picks_here, :].reshape(-1, width)
        logits = contract_cols(picked, table)
        masked = jnp.where(owned[None, :], logits, -jnp.inf)
        part_max = jnp.max(masked, axis=-1)
        part_sum = jnp.sum(jnp.exp(masked - part_max[:, None]), axis=-1)
        full_max = lax.pmax(part_max, names)
        full_sum = lax.psum(part_sum * jnp.exp(part_max - full_max), names)
        hot = row_of[:, None] == jnp.arange(shifted_rows + 1)[None, :]
        probs = jnp.exp(logits - full_max[:, None]) / full_sum[:, None]
        d_logits = jnp.where(
            used[:, None] & touched[None, :], probs - hot.astype(jnp.float32), 0.0
        ).astype(low)
        d_picked = jnp.dot(
            d_logits, jnp.where(owned[:, None], table, 0), preferred_element_type=jnp.float32
        )
        blocks = d_picked.astype(low).reshape(devices, picks_here, width)
        d_picked = jnp.concatenate(
            [
                reduce_bits(blocks[:, :, c], order, names)
                for c, order in zip(columns, back_orders)
            ],
            axis=1,
        ).astype(jnp.float32)
        select = (mlm_positions[:, :, None] == jnp.arange(length)[None, None, :]).astype(
            jnp.float32
        )
        d_output_seq = jnp.einsum(
            "gor,gon->grn",
            select,
            d_picked.reshape(seq_here, slots, width),
            precision=lax.Precision.HIGHEST,
        )
        d_cls = span_terms(heads_all[:, picks_here:, :].reshape(-1, width), pairs_all)
        d_output_seq = d_output_seq.at[:, 0, :].add(d_cls)
        valid = jnp.arange(length)[None, :] < span_lengths[:, None]
        d_output = d_output_seq.reshape(rows_here, width) * valid.reshape(rows_here, 1)
        grad_input, d_mats, d_vecs = plain_backward(d_output)
        d_mats = d_mats.reshape(devices, 3, third, width)
        summed = [
            reduce_bits(d_mats[:, k], back_orders[k], names).astype(jnp.float32) for k in range(3)
        ]
        picked_turned = jnp.dot(picked, turn.T, preferred_element_type=jnp.float32).astype(low)
        d_rolled = contract_rows(d_logits, picked_turned)
        grad_embed, step_embed = embed_step(jnp.where(same_row, d_rolled[:-1], d_rolled[1:]))
        grad_vecs = jnp.sum(vector_terms(d_vecs), axis=(0, 1))
        grad_mats = jnp.concatenate(summed).reshape(-1)
        step_mats = adam_step(layer_mats, grad_mats, mom1_mats, mom2_mats, step_float, decay_rate)
    step_vecs = adam_step(vectors, grad_vecs, mom1_vecs, mom2_vecs, step_float, 0.0)
    return (grad_input, grad_mats, grad_vecs, grad_embed, step_mats, step_vecs, step_embed)


def solution(mesh):
    fsdp_bits = mesh.shape["fsdp"].bit_length() - 1
    rep_bits = mesh.shape["rep"].bit_length() - 1
    names = tuple(f"f{k}" for k in reversed(range(fsdp_bits)))
    core = names[-1]
    names = names + tuple(f"r{k}" for k in reversed(range(rep_bits)))
    bits = Mesh(mesh.devices.reshape((2,) * len(names)), names)
    seqs = P(names, None, None)
    pairs = P(names, None)
    flat = P(names)
    return jax.shard_map(
        functools.partial(on_device, names, core),
        mesh=bits,
        in_specs=(seqs, flat, pairs, pairs) + (flat,) * 10,
        out_specs=(seqs,) + (flat,) * 6,
        check_vma=False,
    )
```
